32 devices in a mesh: grp: 2 (over x), ep: 16 (over z, y, core), dp: 1.
Axes of the slice: x: 2, y: 2, z: 4, core: 2. Of those that a mesh axis runs over, the one named last changes fastest.
Arguments:
- rows_in: bfloat16 [2, 256, 4096], P('grp', ('ep', 'dp')), may hold values from -6 to 6
- cotangent: bfloat16 [256, 4096], P(('ep', 'dp')), may hold values from -6 to 6
- lengths: int32 [4], replicated, may hold values from 1 to 128, 256 in all
- train_experts: int32 [256, 8], P(('ep', 'dp')), may hold values from 0 to 15, all different within a row; in each aligned block of 16 rows (0 to 15, 16 to 31, ...) at most 10 rows name the same one
- train_gates: float32 [256, 8], P(('ep', 'dp')), may hold values from 0.02 to 0.3
- decode_experts: int32 [2, 256, 8], P(None, ('ep', 'dp')), may hold values from 0 to 15, all different within a row; in each aligned block of 16 rows (0 to 15, 16 to 31, ..., all dimensions but the last counted through in order) at most 10 rows name the same one
- decode_gates: float32 [2, 256, 8], P(None, ('ep', 'dp')), may hold values from 0.02 to 0.3
- gate_up: bfloat16 [2, 16, 4096, 2, 768], P('grp', 'ep', None, None, 'dp'), may hold values from -0.09375 to 0.09375
- down: bfloat16 [2, 16, 768, 4096], P('grp', 'ep', 'dp'), may hold values from -0.21875 to 0.21875
Outputs:
- result: bfloat16 [2, 256, 4096], P('grp', ('ep', 'dp'))
The draws below stay inside these ranges and needn't reach their ends.
Inputs may be any that keep to these rules, and one draw needn't show every extreme that they name: `train_experts`: in every aligned block of 16 rows (the rows of one device), the 8 ids of a row differ and no id is named by more than 10 rows of the block; some block reaches 10. `decode_experts`: for each step, in every aligned block of 16 rows (the rows of one device), the 8 ids of a row differ and no id is named by more than 10 rows of the block; some block reaches 10. The lengths sum to 256 and the longest is exactly 128.
All inputs are finite; a program needn't handle non-finite values.
Results may differ from the reference program's by a relative error of at most 0.008.
Values may be sent and summed in bfloat16 or wider, within the bound.
No kernel may reach another device: no remote copies, remote signals or barrier semaphores. Data moves between devices by JAX's collectives and lax.ppermute only.
A program may use at most 192 MiB of HBM per device.

```python
import math
import jax
import jax.numpy as jnp
import numpy as np
from jax import lax

D = 4096
HID = 768
TOP = 8
DSTEPS = 2
ROWS_DEV = 16
EXPERTS = 16
NROWS = 256
CAP = 10
SEQS = 4
MAXLEN = 128
N_EP = 16
N_DP = 1


def levels(rng, shape, cuts, least, top_value):
    def one(axis_at, parts):
        heights = jax.random.uniform(jax.random.fold_in(jax.random.fold_in(rng, 6), axis_at), (parts,), jnp.float32, least / len(cuts), top_value / len(cuts))
        return jnp.repeat(jnp.exp(heights), shape[axis_at] // parts).reshape((-1,) + (1,) * (len(shape) - axis_at - 1))

    level = one(*cuts[0])
    for cut in cuts[1:]:
        level = level * one(*cut)
    return level


def length_profile(count, total, bound, slope):
    weights = [(1 << 20) // math.isqrt(grade ** slope) + 1 for grade in range(2, count + 1)]
    rest, counts = total - bound - (count - 1), [1] * (count - 1)
    while rest > 0:
        free = [i for i in range(count - 1) if counts[i] < bound]
        mass, left = sum([weights[i] for i in free]), rest
        for i in free:
            addition = min(bound - counts[i], max(1, left * weights[i] // mass), rest)
            counts[i] = counts[i] + addition
            rest = rest - addition
    return np.array([bound] + counts)


def ragged(stream_key, count, total, most, slope):
    if count == 2:
        one = jax.random.randint(stream_key, (), max(1, total - most), min(most, total - 1) + 1)
        return jnp.stack([one, total - one])
    tallies = jnp.asarray(length_profile(count, total, most, slope), jnp.int32)
    twos = (count - 1) // 2
    giver, receiver = tallies[1:1 + 2 * twos:2], tallies[2:2 + 2 * twos:2]
    room = jnp.minimum(giver - 1, most - receiver)
    shifted = jax.random.randint(jax.random.fold_in(stream_key, 1), (twos,), 0, 1 << 20) % (room + 1)
    tallies = tallies.at[1:1 + 2 * twos:2].set(giver - shifted).at[2:2 + 2 * twos:2].set(receiver + shifted)
    return tallies[jax.random.permutation(jax.random.fold_in(stream_key, 2), count)]


def assign_block(stream_key, own, number, rows, number_of, top, reach, skew):
    order = jax.random.permutation(stream_key, number_of)
    crowded, usual = shares(number_of, rows * top, reach, skew, True), shares(number_of, rows * top, reach, skew, False)
    places = jnp.arange(number_of)

    def named(tallies, offset_by):
        used = int((tallies > 0).sum())
        fixed = max(1, used // 4)
        moved = fixed + (places - fixed + offset_by * (used - fixed)) % max(1, number_of - fixed)
        return jnp.zeros((number_of,), jnp.int32).at[order[jnp.where(places < fixed, places, moved)]].set(jnp.asarray(tallies, jnp.int32))

    tallies = jnp.where(number % 4 == 0, named(crowded, number // 4), named(usual, number - number // 4 - 1))
    mixed = jax.random.permutation(jax.random.fold_in(own, 3), number_of)
    source_of, sink = mixed[0:number_of // 2 * 2:2], mixed[1:number_of // 2 * 2:2]
    slack = jnp.minimum(tallies[source_of] - 1, reach - tallies[sink]) // 2
    slack = jnp.where((source_of == order[0]) | (sink == order[0]) | (tallies[sink] == 0), 0, jnp.maximum(slack, 0))
    moved = jax.random.randint(jax.random.fold_in(own, 4), (number_of // 2,), 0, 1 << 20) % (slack + 1)
    tallies = tallies.at[source_of].add(-moved).at[sink].add(moved)
    items = jnp.searchsorted(jnp.cumsum(tallies), jnp.arange(rows * top), side="right").astype(jnp.int32)
    listing = items.reshape(top, rows).T
    listing = listing[jax.random.permutation(jax.random.fold_in(own, 1), rows)]
    offset_by = jax.random.randint(jax.random.fold_in(own, 2), (rows, 1), 0, top)
    return jnp.take_along_axis(listing, (jnp.arange(top)[None, :] + offset_by) % top, axis=1)


def shares(number_of, total, reach, skew, full):
    portions = [(1 << 20) // math.isqrt(standing ** skew) + 1 for standing in range(1, number_of + 1)]
    largest = reach if full else min(reach, max(-(-total // number_of), total * portions[0] // sum(portions)))
    least = 1 if total - largest >= number_of - 1 else 0
    counts, rest = [largest] + [least] * (number_of - 1), total - largest - least * (number_of - 1)
    while rest > 0:
        candidates = [i for i in range(1, number_of) if counts[i] < largest] or [i for i in range(1, number_of) if counts[i] < reach]
        whole, remaining = sum([portions[i] for i in candidates]), rest
        for i in candidates:
            extra = min(reach - counts[i], max(1, remaining * portions[i] // whole), rest)
            counts[i] = counts[i] + extra
            rest = rest - extra
    return np.array(counts)


def centred(stream_key, dims, scale, bound, shards=(), held_as=jnp.bfloat16):
    array = scale * jax.random.normal(stream_key, dims, jnp.float32)
    if shards:
        array = array * levels(stream_key, dims, shards, -0.22, 0.18)
    return jnp.clip(array, -bound, bound).astype(held_as)


def setup_inputs(seed: int = 0) -> dict:
    key_of = jax.random.split(jax.random.key(seed), 10)
    rows_in = centred(key_of[0], (2, NROWS, D), 1.0, 6.0, ((0, 2), (1, 16)))
    cotangent = centred(key_of[1], (NROWS, D), 1.0, 6.0, ((0, 16),))
    lengths = ragged(key_of[2], SEQS, NROWS, MAXLEN, 2).astype(jnp.int32)
    train_experts_keys = jax.random.split(jax.random.fold_in(key_of[3], 1), NROWS // ROWS_DEV)
    train_experts_turns = jax.random.permutation(jax.random.fold_in(key_of[3], 3), NROWS // ROWS_DEV)
    train_experts = jax.vmap(lambda own, number: assign_block(jax.random.fold_in(key_of[3], 2), own, number, ROWS_DEV, EXPERTS, TOP, CAP, 2))(train_experts_keys, train_experts_turns).reshape((NROWS, TOP))
    train_gates = jnp.clip(0.02 + 0.28 * jax.random.uniform(key_of[4], (NROWS, TOP), jnp.float32) ** levels(key_of[4], (NROWS, TOP), ((0, 16),), -0.2, 0.2), 0.02, 0.3)
    decode_experts_keys = jax.random.split(jax.random.fold_in(key_of[5], 1), DSTEPS * NROWS // ROWS_DEV)
    decode_experts_turns = jax.random.permutation(jax.random.fold_in(key_of[5], 3), DSTEPS * NROWS // ROWS_DEV)
    decode_experts = jax.vmap(lambda own, number: assign_block(jax.random.fold_in(key_of[5], 2), own, number, ROWS_DEV, EXPERTS, TOP, CAP, 2))(decode_experts_keys, decode_experts_turns).reshape((DSTEPS, NROWS, TOP))
    decode_gates = jnp.clip(0.02 + 0.28 * jax.random.uniform(key_of[6], (DSTEPS, NROWS, TOP), jnp.float32) ** levels(key_of[6], (DSTEPS, NROWS, TOP), ((1, 16),), -0.2, 0.2), 0.02, 0.3)
    gate_up = centred(key_of[7], (2, EXPERTS, D, 2, HID), D ** -0.5, 0.09375, ((0, 2), (1, 16)))
    down = centred(key_of[8], (2, EXPERTS, HID, D), HID ** -0.5, 0.21875, ((0, 2), (1, 16)))
    return {"rows_in": rows_in, "cotangent": cotangent, "lengths": lengths, "train_experts": train_experts, "train_gates": train_gates, "decode_experts": decode_experts, "decode_gates": decode_gates, "gate_up": gate_up, "down": down}


EPSILON = 1e-06

def round_keep(values):
    return lax.optimization_barrier(values.astype(jnp.bfloat16)).astype(jnp.float32)

def token_weights(lengths):
    ends = jnp.cumsum(lengths).astype(jnp.int32)
    starts = ends - lengths
    places = jnp.arange(NROWS, dtype=jnp.int32)
    inside = (places[:, None] >= starts[None, :]) & (places[:, None] < ends[None, :])
    seq_len = lax.optimization_barrier(jnp.sum(jnp.where(inside, lengths[None, :], 0), axis=1)).astype(jnp.float32)
    return 2.0 * MAXLEN / (seq_len + MAXLEN)

def slot_tables(expert_ids):
    blocks = expert_ids.reshape(N_EP * N_DP, ROWS_DEV * TOP)
    onehot = (blocks[:, :, None] == jnp.arange(EXPERTS, dtype=jnp.int32)[None, None, :]).astype(jnp.int32)
    ranks = lax.optimization_barrier(jnp.sum((jnp.cumsum(onehot, axis=1) - onehot) * onehot, axis=2))
    sources = jnp.arange(N_EP * N_DP, dtype=jnp.int32)[:, None]
    position = (sources * CAP + ranks).reshape(-1).astype(jnp.int32)
    expert = expert_ids.reshape(-1).astype(jnp.int32)
    pairs = jnp.arange(NROWS * TOP, dtype=jnp.int32)
    table = jnp.full((EXPERTS, N_EP * N_DP * CAP), NROWS * TOP, jnp.int32).at[expert, position].set(pairs)
    return (table, expert, position)

def expert_forward(slot_rows, weights_gu, weights_dn):
    both = jnp.dot(slot_rows, weights_gu.reshape(D, 2 * HID), preferred_element_type=jnp.float32).reshape(-1, 2, HID)
    active = both[:, 0]
    upward = both[:, 1]
    hidden = (active * jax.nn.sigmoid(active) * upward).astype(jnp.bfloat16)
    part_size = HID // N_DP
    total = jnp.zeros((slot_rows.shape[0], D), jnp.float32)
    for part_index in range(N_DP):
        lower = part_index * part_size
        piece = jnp.dot(hidden[:, lower:lower + part_size], weights_dn[lower:lower + part_size], preferred_element_type=jnp.float32)
        total = total + round_keep(piece)
    return total

def expert_learn(slot_rows, slot_grads, weights_gu, weights_dn):
    count = N_EP * N_DP * CAP
    both = jnp.dot(slot_rows, weights_gu.reshape(D, 2 * HID), preferred_element_type=jnp.float32).reshape(count, 2, HID)
    active = both[:, 0]
    upward = both[:, 1]
    sigma = jax.nn.sigmoid(active)
    swish = active * sigma
    hidden = (swish * upward).astype(jnp.bfloat16)
    back = lax.dot_general(slot_grads, weights_dn, (((1,), (1,)), ((), ())), preferred_element_type=jnp.float32)
    d_active = back * upward * sigma * (1.0 + active * (1.0 - sigma))
    d_upward = back * swish
    d_both = jnp.stack([d_active, d_upward], axis=1).astype(jnp.bfloat16)
    rows_four = slot_rows.reshape(N_EP, N_DP, CAP, D).astype(jnp.float32)
    grads_four = slot_grads.reshape(N_EP, N_DP, CAP, D).astype(jnp.float32)
    per_dn = jnp.einsum('epch,epcd->phd', hidden.reshape(N_EP, N_DP, CAP, HID).astype(jnp.float32), grads_four, precision=lax.Precision.HIGHEST)
    per_gu = jnp.einsum('epcd,epcgh->pdgh', rows_four, d_both.reshape(N_EP, N_DP, CAP, 2, HID).astype(jnp.float32), precision=lax.Precision.HIGHEST)
    grad_dn = jnp.zeros((HID, D), jnp.float32)
    grad_gu = jnp.zeros((D, 2, HID), jnp.float32)
    for replica in range(N_DP):
        grad_dn = grad_dn + round_keep(per_dn[replica])
        grad_gu = grad_gu + round_keep(per_gu[replica])
    part_size = HID // N_DP
    slot_dx = jnp.zeros((count, D), jnp.float32)
    for part_index in range(N_DP):
        lower = part_index * part_size
        piece = jnp.einsum('mgh,dgh->md', d_both[:, :, lower:lower + part_size].astype(jnp.float32), weights_gu[:, :, lower:lower + part_size].astype(jnp.float32), precision=lax.Precision.HIGHEST)
        slot_dx = slot_dx + round_keep(piece)
    scale_gu = jnp.sqrt(lax.optimization_barrier(jnp.mean(grad_gu * grad_gu, axis=0, keepdims=True)) + EPSILON)
    scale_dn = jnp.sqrt(lax.optimization_barrier(jnp.mean(grad_dn * grad_dn, axis=1, keepdims=True)) + EPSILON)
    fresh_gu = (weights_gu.astype(jnp.float32) - 0.5 / D ** 0.5 * grad_gu / scale_gu).astype(jnp.bfloat16)
    fresh_dn = (weights_dn.astype(jnp.float32) - 0.5 / HID ** 0.5 * grad_dn / scale_dn).astype(jnp.bfloat16)
    return (slot_dx, fresh_gu, fresh_dn)

def reference(rows_in, cotangent, lengths, train_experts, train_gates, decode_experts, decode_gates, gate_up, down):
    weight = token_weights(lengths)
    zero_row = jnp.zeros((1, D), jnp.bfloat16)
    tokens = jnp.concatenate([rows_in[0], zero_row], axis=0)
    cot_pad = jnp.concatenate([cotangent, zero_row], axis=0)
    scaled = (train_gates * weight[:, None]).reshape(-1)
    scale_pad = jnp.concatenate([scaled, jnp.zeros((1,), jnp.float32)], axis=0)
    learn_table, learn_expert, learn_position = slot_tables(train_experts)

    def stale_step(current, step_index):
        table, expert, position = slot_tables(decode_experts[step_index])
        padded = jnp.concatenate([current, zero_row], axis=0)

        def one_expert(expert_index):
            return expert_forward(padded[table[expert_index] // TOP], gate_up[1, expert_index], down[1, expert_index])
        outputs = lax.map(one_expert, jnp.arange(EXPERTS, dtype=jnp.int32))
        pair_out = outputs[expert, position].reshape(NROWS, TOP, D)
        added = lax.optimization_barrier(jnp.sum(decode_gates[step_index][:, :, None] * pair_out, axis=1))
        return (current.astype(jnp.float32) + added).astype(jnp.bfloat16)

    def fresh_step(current, step_index):
        table, expert, position = slot_tables(decode_experts[step_index])
        padded = jnp.concatenate([current, zero_row], axis=0)

        def one_expert(expert_index):
            slot_pairs = learn_table[expert_index]
            slot_rows = tokens[slot_pairs // TOP]
            slot_grads = (scale_pad[slot_pairs][:, None] * cot_pad[slot_pairs // TOP].astype(jnp.float32)).astype(jnp.bfloat16)
            slot_dx, fresh_gu, fresh_dn = expert_learn(slot_rows, slot_grads, gate_up[0, expert_index], down[0, expert_index])
            return (slot_dx, expert_forward(padded[table[expert_index] // TOP], fresh_gu, fresh_dn))
        dx_slots, outputs = lax.map(one_expert, jnp.arange(EXPERTS, dtype=jnp.int32))
        pair_out = outputs[expert, position].reshape(NROWS, TOP, D)
        added = lax.optimization_barrier(jnp.sum(decode_gates[step_index][:, :, None] * pair_out, axis=1))
        return ((current.astype(jnp.float32) + added).astype(jnp.bfloat16), dx_slots)
    current = stale_step(rows_in[1], 0)
    current, dx_slots = fresh_step(current, 1)
    for step_index in range(2, DSTEPS):
        current, ignored = fresh_step(current, step_index)
    pair_dx = dx_slots[learn_expert, learn_position].reshape(NROWS, TOP, D)
    grads = weight[:, None] * cotangent.astype(jnp.float32) + lax.optimization_barrier(jnp.sum(pair_dx, axis=1))
    return jnp.stack([grads.astype(jnp.bfloat16), current], axis=0)
```

```python
import jax
import jax.numpy as jnp
from jax import lax
from jax.sharding import PartitionSpec as P

EPSILON = 1e-06
AXES = ("ep", "dp")


def across(block, source, target):
    return lax.ppermute(block, "grp", [(source, target)])


def gate_table(expert_ids, gate_values, expert_count):
    named = expert_ids[:, :, None] == jnp.arange(expert_count, dtype=jnp.int32)[None, None, :]
    return jnp.sum(jnp.where(named, gate_values[:, :, None], 0.0), axis=1)


def renew(weights, grads, axis_number, rate):
    scale = jnp.sqrt(jnp.mean(grads * grads, axis=axis_number, keepdims=True) + EPSILON)
    return (weights.astype(jnp.float32) - rate * grads / scale).astype(jnp.bfloat16)


def wide(a, b, contract):
    return lax.dot_general(a, b, (contract, ((), ())), preferred_element_type=jnp.float32)


def expert_ffn(rows, gates, planes, weights_dn):
    active = wide(rows, planes[0], ((1,), (0,)))
    upward = wide(rows, planes[1], ((1,), (0,)))
    hidden = (active * jax.nn.sigmoid(active) * upward).astype(jnp.bfloat16)
    return gates[:, None] * wide(hidden, weights_dn, ((1,), (0,)))


def per_device(
    rows_in,
    cotangent,
    lengths,
    train_experts,
    train_gates,
    decode_experts,
    decode_gates,
    gate_up,
    down,
):
    ep_count = lax.axis_size("ep")
    dp_count = lax.axis_size("dp")
    row_count, model_width = cotangent.shape
    is_learner = lax.axis_index("grp") == 0
    hidden_all = gate_up.shape[4] * dp_count
    own_dn = down[0, 0]
    planes = lax.optimization_barrier(jnp.transpose(gate_up[0, 0], (1, 0, 2)))

    own_rows = rows_in[0]
    total_rows = row_count * ep_count * dp_count
    longest = 2 * total_rows // lengths.shape[0]
    first_row = (lax.axis_index("ep") * dp_count + lax.axis_index("dp")) * row_count
    places = first_row + jnp.arange(row_count, dtype=jnp.int32)
    ends = jnp.cumsum(lengths)
    starts = ends - lengths
    inside = (places[:, None] >= starts[None, :]) & (places[:, None] < ends[None, :])
    seq_len = jnp.sum(jnp.where(inside, lengths[None, :], 0), axis=1).astype(jnp.float32)
    weight = 2.0 * longest / (seq_len + longest)
    cot_wide = weight[:, None] * cotangent.astype(jnp.float32)

    train_table = weight[:, None] * gate_table(train_experts, train_gates, ep_count)
    stale_table = gate_table(decode_experts[0], decode_gates[0], ep_count)
    fresh_table = gate_table(decode_experts[1], decode_gates[1], ep_count)
    table = jnp.concatenate(
        [jnp.where(is_learner, train_table, stale_table), fresh_table], axis=1
    )
    every_table = lax.all_gather(table, AXES, tiled=True)
    mine = lax.axis_index("ep")
    first_gates = lax.dynamic_index_in_dim(every_table, mine, 1, keepdims=False)
    fresh_gates = lax.dynamic_index_in_dim(every_table, mine + ep_count, 1, keepdims=False)

    rows = lax.all_gather(own_rows, AXES, tiled=True)
    cots = lax.all_gather(cotangent, AXES, tiled=True)

    def learn(rows, cots):
        grads = (first_gates[:, None] * cots.astype(jnp.float32)).astype(jnp.bfloat16)
        active = wide(rows, planes[0], ((1,), (0,)))
        upward = wide(rows, planes[1], ((1,), (0,)))
        sigma = jax.nn.sigmoid(active)
        swish = active * sigma
        hidden = (swish * upward).astype(jnp.bfloat16)
        back = wide(grads, own_dn, ((1,), (1,)))
        d_active = (back * upward * sigma * (1.0 + active * (1.0 - sigma))).astype(jnp.bfloat16)
        d_upward = (back * swish).astype(jnp.bfloat16)
        slot_dx = wide(d_active, planes[0], ((1,), (1,))) + wide(d_upward, planes[1], ((1,), (1,)))
        return (slot_dx.astype(jnp.bfloat16), grads, hidden, d_active, d_upward)

    def decode(rows, cots):
        out = expert_ffn(rows, first_gates, planes, own_dn).astype(jnp.bfloat16)
        blank = jnp.zeros((total_rows, own_dn.shape[0]), jnp.bfloat16)
        return (out, cots, blank, blank, blank)

    part, grads, hidden, d_active, d_upward = lax.cond(is_learner, learn, decode, rows, cots)
    summed = lax.psum_scatter(part, AXES, scatter_dimension=0, tiled=True)
    base = jnp.where(is_learner, cot_wide, own_rows.astype(jnp.float32))
    carried = (base + summed.astype(jnp.float32)).astype(jnp.bfloat16)

    def update(rows, grads, hidden, d_active, d_upward):
        rate = 0.5 / model_width**0.5
        fresh_gate = renew(planes[0], wide(rows, d_active, ((0,), (0,))), 0, rate)
        fresh_up = renew(planes[1], wide(rows, d_upward, ((0,), (0,))), 0, rate)
        fresh_dn = renew(own_dn, wide(hidden, grads, ((0,), (0,))), 1, 0.5 / hidden_all**0.5)
        return (jnp.stack([fresh_gate, fresh_up], axis=0), fresh_dn)

    fresh_planes, fresh_dn = lax.cond(
        is_learner,
        update,
        lambda *unused: (planes, own_dn),
        rows,
        grads,
        hidden,
        d_active,
        d_upward,
    )
    arrived = lax.all_gather(across(carried, 1, 0), AXES, tiled=True)
    fresh_part = lax.cond(
        is_learner,
        lambda r: expert_ffn(r, fresh_gates, fresh_planes, fresh_dn).astype(jnp.bfloat16),
        lambda r: r,
        arrived,
    )
    fresh_sum = lax.psum_scatter(fresh_part, AXES, scatter_dimension=0, tiled=True)
    moved = across(fresh_sum, 0, 1)
    final_rows = jnp.where(
        is_learner,
        carried,
        (carried.astype(jnp.float32) + moved.astype(jnp.float32)).astype(jnp.bfloat16),
    )
    return final_rows[None]


def solution(mesh):
    placed = (
        P("grp", ("ep", "dp"), None),
        P(("ep", "dp"), None),
        P(),
        P(("ep", "dp"), None),
        P(("ep", "dp"), None),
        P(None, ("ep", "dp"), None),
        P(None, ("ep", "dp"), None),
        P("grp", "ep", None, None, "dp"),
        P("grp", "ep", "dp", None),
    )
    return jax.shard_map(
        per_device,
        mesh=mesh,
        in_specs=placed,
        out_specs=P("grp", ("ep", "dp"), None),
        check_vma=False,
    )
```

```python
import jax
import jax.numpy as jnp
from jax import lax
from jax.sharding import PartitionSpec as P

EPSILON = 1e-06
AXES = ("ep", "dp")


def across(block, source, target):
    return lax.ppermute(block, "grp", [(source, target)])


def radices(device_count):
    sizes = []
    rest = device_count
    for size in (2, 2):
        if rest % size == 0 and rest > 1:
            sizes.append(size)
            rest //= size
    while rest > 1:
        size = 4 if rest % 4 == 0 else 2
        sizes.append(size)
        rest //= size
    return sizes[::-1]


def stages(device_count):
    strides = []
    stride = device_count
    for size in radices(device_count):
        stride //= size
        strides.append((stride, size))
    return strides


def swap(block, device_count, flip, roles):
    pairs = [
        (role * device_count + i, role * device_count + (i ^ flip))
        for role in roles
        for i in range(device_count)
    ]
    return lax.ppermute(block, ("grp",) + AXES, pairs)


def gather(block, device_count, roles):
    pieces = {0: block}
    for stride, size in stages(device_count):
        fresh = {}
        for turn in range(1, size):
            for offset, piece in pieces.items():
                fresh[offset ^ (turn * stride)] = swap(piece, device_count, turn * stride, roles)
        pieces.update(fresh)
    return jnp.concatenate([pieces[i] for i in range(device_count)], axis=0)


def scatter_sum(part, device_count, roles):
    row_count = part.shape[0] // device_count
    width = part.shape[1]
    for stride, size in stages(device_count)[::-1]:
        cut = part.reshape(-1, size, row_count, width)
        total = cut[:, 0].reshape(-1, width).astype(jnp.float32)
        for turn in range(1, size):
            sent = cut[:, turn].reshape(-1, width)
            total = total + swap(sent, device_count, turn * stride, roles).astype(jnp.float32)
        part = total.astype(jnp.bfloat16)
    return total


def two_part(table):
    upper = lax.reduce_precision(table, 8, 7)
    return [upper.astype(jnp.bfloat16), (table - upper).astype(jnp.bfloat16)]


def gate_table(expert_ids, gate_values, expert_count):
    named = expert_ids[:, :, None] == jnp.arange(expert_count, dtype=jnp.int32)[None, None, :]
    return jnp.sum(jnp.where(named, gate_values[:, :, None], 0.0), axis=1)


def renew(weights, grads, axis_number, rate):
    scale = jnp.sqrt(jnp.mean(grads * grads, axis=axis_number, keepdims=True) + EPSILON)
    return (weights.astype(jnp.float32) - rate * grads / scale).astype(jnp.bfloat16)


def wide(a, b, contract):
    return lax.dot_general(a, b, (contract, ((), ())), preferred_element_type=jnp.float32)


def expert_ffn(rows, gates, planes, weights_dn):
    active = wide(rows, planes[0], ((1,), (0,)))
    upward = wide(rows, planes[1], ((1,), (0,)))
    hidden = (active * jax.nn.sigmoid(active) * upward).astype(jnp.bfloat16)
    return gates[:, None] * wide(hidden, weights_dn, ((1,), (0,)))


def per_device(
    rows_in,
    cotangent,
    lengths,
    train_experts,
    train_gates,
    decode_experts,
    decode_gates,
    gate_up,
    down,
):
    ep_count = lax.axis_size("ep")
    dp_count = lax.axis_size("dp")
    row_count, model_width = cotangent.shape
    is_learner = lax.axis_index("grp") == 0
    hidden_all = gate_up.shape[4] * dp_count
    own_dn = down[0, 0]
    planes = lax.optimization_barrier(jnp.transpose(gate_up[0, 0], (1, 0, 2)))

    own_rows = rows_in[0]
    total_rows = row_count * ep_count * dp_count
    longest = 2 * total_rows // lengths.shape[0]
    first_row = (lax.axis_index("ep") * dp_count + lax.axis_index("dp")) * row_count
    places = first_row + jnp.arange(row_count, dtype=jnp.int32)
    ends = jnp.cumsum(lengths)
    starts = ends - lengths
    inside = (places[:, None] >= starts[None, :]) & (places[:, None] < ends[None, :])
    seq_len = jnp.sum(jnp.where(inside, lengths[None, :], 0), axis=1).astype(jnp.float32)
    weight = 2.0 * longest / (seq_len + longest)
    cot_wide = weight[:, None] * cotangent.astype(jnp.float32)

    train_table = weight[:, None] * gate_table(train_experts, train_gates, ep_count)
    stale_table = gate_table(decode_experts[0], decode_gates[0], ep_count)
    fresh_table = gate_table(decode_experts[1], decode_gates[1], ep_count)
    device_count = ep_count * dp_count
    table = two_part(jnp.where(is_learner, train_table, stale_table)) + two_part(fresh_table)
    spare = -4 * ep_count % 128
    table.append(jnp.zeros((row_count, spare), jnp.bfloat16))
    every = gather(jnp.concatenate([own_rows] + table, axis=1), device_count, (0, 1))
    rows = every[:, :model_width]
    mine = lax.axis_index("ep")

    def gates_of(place):
        parts = [
            lax.dynamic_index_in_dim(every, model_width + mine + i * ep_count, 1, keepdims=False)
            for i in (place, place + 1)
        ]
        return parts[0].astype(jnp.float32) + parts[1].astype(jnp.float32)

    first_gates = gates_of(0)
    fresh_gates = gates_of(2)
    cots = gather(cotangent, device_count, (0,))

    def learn(rows, cots):
        grads = (first_gates[:, None] * cots.astype(jnp.float32)).astype(jnp.bfloat16)
        active = wide(rows, planes[0], ((1,), (0,)))
        upward = wide(rows, planes[1], ((1,), (0,)))
        sigma = jax.nn.sigmoid(active)
        swish = active * sigma
        hidden = (swish * upward).astype(jnp.bfloat16)
        back = wide(grads, own_dn, ((1,), (1,)))
        d_active = (back * upward * sigma * (1.0 + active * (1.0 - sigma))).astype(jnp.bfloat16)
        d_upward = (back * swish).astype(jnp.bfloat16)
        slot_dx = wide(d_active, planes[0], ((1,), (1,))) + wide(d_upward, planes[1], ((1,), (1,)))
        return (slot_dx.astype(jnp.bfloat16), grads, hidden, d_active, d_upward)

    def decode(rows, cots):
        out = expert_ffn(rows, first_gates, planes, own_dn).astype(jnp.bfloat16)
        blank = jnp.zeros((total_rows, own_dn.shape[0]), jnp.bfloat16)
        return (out, cots, blank, blank, blank)

    part, grads, hidden, d_active, d_upward = lax.cond(is_learner, learn, decode, rows, cots)
    summed = scatter_sum(part, device_count, (0, 1))
    base = jnp.where(is_learner, cot_wide, own_rows.astype(jnp.float32))
    carried = (base + summed).astype(jnp.bfloat16)

    def update(rows, grads, hidden, d_active, d_upward):
        rate = 0.5 / model_width**0.5
        fresh_gate = renew(planes[0], wide(rows, d_active, ((0,), (0,))), 0, rate)
        fresh_up = renew(planes[1], wide(rows, d_upward, ((0,), (0,))), 0, rate)
        fresh_dn = renew(own_dn, wide(hidden, grads, ((0,), (0,))), 1, 0.5 / hidden_all**0.5)
        return (jnp.stack([fresh_gate, fresh_up], axis=0), fresh_dn)

    fresh_planes, fresh_dn = lax.cond(
        is_learner,
        update,
        lambda *unused: (planes, own_dn),
        rows,
        grads,
        hidden,
        d_active,
        d_upward,
    )
    arrived = gather(across(carried, 1, 0), device_count, (0,))
    fresh_part = lax.cond(
        is_learner,
        lambda r: expert_ffn(r, fresh_gates, fresh_planes, fresh_dn).astype(jnp.bfloat16),
        lambda r: r,
        arrived,
    )
    fresh_sum = scatter_sum(fresh_part, device_count, (0,))
    moved = across(fresh_sum.astype(jnp.bfloat16), 0, 1)
    final_rows = jnp.where(
        is_learner,
        carried,
        (carried.astype(jnp.float32) + moved.astype(jnp.float32)).astype(jnp.bfloat16),
    )
    return final_rows[None]


def solution(mesh):
    placed = (
        P("grp", ("ep", "dp"), None),
        P(("ep", "dp"), None),
        P(),
        P(("ep", "dp"), None),
        P(("ep", "dp"), None),
        P(None, ("ep", "dp"), None),
        P(None, ("ep", "dp"), None),
        P("grp", "ep", None, None, "dp"),
        P("grp", "ep", "dp", None),
    )
    return jax.shard_map(
        per_device,
        mesh=mesh,
        in_specs=placed,
        out_specs=P("grp", ("ep", "dp"), None),
        check_vma=False,
    )
```

```python
import functools

import jax
import jax.numpy as jnp
from jax import lax
from jax.experimental import pallas as pl
from jax.experimental.pallas import tpu as pltpu
from jax.sharding import PartitionSpec as P

EPSILON = 1e-06
AXES = ("ep", "dp")


def across(block, source, target):
    return lax.ppermute(block, "grp", [(source, target)])


def radices(device_count):
    sizes = []
    rest = device_count
    for size in (2, 2):
        if rest % size == 0 and rest > 1:
            sizes.append(size)
            rest //= size
    while rest > 1:
        size = 4 if rest % 4 == 0 else 2
        sizes.append(size)
        rest //= size
    return sizes[::-1]


def stages(device_count):
    strides = []
    stride = device_count
    for size in radices(device_count):
        stride //= size
        strides.append((stride, size))
    return strides


def swap(block, device_count, flip, roles):
    pairs = [
        (role * device_count + i, role * device_count + (i ^ flip))
        for role in roles
        for i in range(device_count)
    ]
    return lax.ppermute(block, ("grp",) + AXES, pairs)


def gather(block, device_count, roles):
    for stride, size in stages(device_count):
        got = [swap(block, device_count, turn * stride, roles) for turn in range(1, size)]
        block = jnp.concatenate([block] + got, axis=0)
    return block


def scatter_sum(part, device_count, roles):
    for stride, size in stages(device_count)[::-1]:
        cuts = jnp.split(part, size, axis=0)
        total = cuts[0].astype(jnp.float32)
        for turn in range(1, size):
            total = total + swap(cuts[turn], device_count, turn * stride, roles).astype(jnp.float32)
        part = total.astype(jnp.bfloat16)
    return total


def two_part(table):
    upper = lax.reduce_precision(table, 8, 7)
    return [upper.astype(jnp.bfloat16), (table - upper).astype(jnp.bfloat16)]


def gate_table(expert_ids, gate_values, expert_count):
    named = expert_ids[:, :, None] == jnp.arange(expert_count, dtype=jnp.int32)[None, None, :]
    return jnp.sum(jnp.where(named, gate_values[:, :, None], 0.0), axis=1)


def renew(weights, grads, axis_number, rate):
    scale = jnp.sqrt(jnp.mean(grads * grads, axis=axis_number, keepdims=True) + EPSILON)
    return (weights.astype(jnp.float32) - rate * grads / scale).astype(jnp.bfloat16)


def wide(a, b, contract):
    return lax.dot_general(a, b, (contract, ((), ())), preferred_element_type=jnp.float32)


def nn(a, b):
    return wide(a, b, ((1,), (0,)))


def nt(a, b):
    return wide(a, b, ((1,), (1,)))


def pick_gates(table, column, step):
    places = lax.broadcasted_iota(jnp.int32, table.shape, 1)
    taken = (places == column) | (places == column + step)
    return jnp.sum(jnp.where(taken, table.astype(jnp.float32), 0.0), axis=1, keepdims=True)


def ffn_kernel(place, rows_ref, table_ref, gu_ref, dn_ref, out_ref, total, *, experts):
    step = pl.program_id(0)
    rows = rows_ref[...]
    active = nn(rows, gu_ref[0])
    upward = nn(rows, gu_ref[1])
    hidden = (active * jax.nn.sigmoid(active) * upward).astype(jnp.bfloat16)
    width = dn_ref.shape[1]
    tile = min(width, 1024)
    last = pl.num_programs(0) - 1
    gates = pick_gates(table_ref[...], place[0], experts)
    for lower in range(0, width, tile):
        cut = pl.ds(lower, tile)
        fresh = nn(hidden, dn_ref[:, cut])

        @pl.when(step == 0)
        def _():
            total[:, cut] = fresh

        @pl.when((step > 0) & (step < last))
        def _():
            total[:, cut] += fresh

        @pl.when((step > 0) & (step == last))
        def _():
            out_ref[:, cut] = (gates * (total[:, cut] + fresh)).astype(jnp.bfloat16)

    if pl.num_programs(0) == 1:
        out_ref[...] = (gates * total[...]).astype(jnp.bfloat16)


def hidden_block(hidden_count):
    return 256 if hidden_count % 256 == 0 else 128


def ffn_call(place, rows, table, planes, weights_dn, experts):
    row_count = rows.shape[0]
    hidden_count, width = weights_dn.shape
    spare = table.shape[1] - width
    size = hidden_block(hidden_count)
    steps = hidden_count // size
    return pl.pallas_call(
        functools.partial(ffn_kernel, experts=experts),
        grid_spec=pltpu.PrefetchScalarGridSpec(
            num_scalar_prefetch=1,
            grid=(steps,),
            in_specs=[
                pl.BlockSpec((row_count, width), lambda j, p: (0, 0)),
                pl.BlockSpec((row_count, spare), lambda j, p: (0, width // spare)),
                pl.BlockSpec((2, width, size), lambda j, p: (0, 0, j)),
                pl.BlockSpec((size, width), lambda j, p: (j, 0)),
            ],
            out_specs=pl.BlockSpec((row_count, width), lambda j, p: (0, 0)),
            scratch_shapes=[pltpu.VMEM((row_count, width), jnp.float32)],
        ),
        out_shape=jax.ShapeDtypeStruct((row_count, width), jnp.bfloat16),
        compiler_params=pltpu.CompilerParams(vmem_limit_bytes=40 << 20),
        cost_estimate=pl.CostEstimate(
            flops=6 * row_count * hidden_count * width,
            bytes_accessed=6 * hidden_count * width,
            transcendentals=row_count * hidden_count,
        ),
        name="ffn",
    )(place, rows, table, planes, weights_dn)


def learn_kernel(
    place, rows_ref, table_ref, cot_ref, gu_ref, dn_ref, dx_ref, new_gu_ref, new_dn_ref,
    turned, pulls, total, grads, grads_dn, *, experts, rates,
):
    step = pl.program_id(0)
    width = rows_ref.shape[1]
    tile = min(width, 512)
    tiles = width // tile

    @pl.when(step == 0)
    def _():
        gates = pick_gates(table_ref[...], place[0], experts)
        total[...] = jnp.zeros_like(total)

        @pl.loop(0, tiles)
        def _(i):
            cut = pl.ds(pl.multiple_of(i * tile, tile), tile)
            pulls[:, cut] = (gates * cot_ref[:, cut].astype(jnp.float32)).astype(jnp.bfloat16)
            turned[cut, :] = rows_ref[:, cut].T

    active = nn(rows_ref[...], gu_ref[0])
    upward = nn(rows_ref[...], gu_ref[1])
    back = nt(pulls[...], dn_ref[...])
    sigma = jax.nn.sigmoid(active)
    swish = active * sigma
    hidden = (swish * upward).astype(jnp.bfloat16)
    d_active = (back * upward * sigma * (1.0 + active * (1.0 - sigma))).astype(jnp.bfloat16)
    d_upward = (back * swish).astype(jnp.bfloat16)
    hidden_turned = hidden.T

    @pl.loop(0, tiles)
    def _(i):
        cut = pl.ds(pl.multiple_of(i * tile, tile), tile)
        total[:, cut] += nt(d_active, gu_ref[0, cut, :]) + nt(d_upward, gu_ref[1, cut, :])

    for half, sent in ((0, d_active), (1, d_upward)):
        def square(i, so_far):
            cut = pl.ds(pl.multiple_of(i * tile, tile), tile)
            fresh = nn(turned[cut, :], sent)
            grads[cut, :] = fresh
            return so_far + jnp.sum(fresh * fresh, axis=0, keepdims=True)

        squares = lax.fori_loop(0, tiles, square, jnp.zeros((1, sent.shape[1]), jnp.float32))
        scale = rates[0] / jnp.sqrt(squares / width + EPSILON)

        @pl.loop(0, tiles)
        def _(i):
            cut = pl.ds(pl.multiple_of(i * tile, tile), tile)
            old = gu_ref[half, cut, :].astype(jnp.float32)
            new_gu_ref[half, cut, :] = (old - grads[cut, :] * scale).astype(jnp.bfloat16)

    def square_dn(i, so_far):
        cut = pl.ds(pl.multiple_of(i * tile, tile), tile)
        fresh = nn(hidden_turned, pulls[:, cut])
        grads_dn[:, cut] = fresh
        return so_far + jnp.sum(fresh * fresh, axis=1, keepdims=True)

    squares = lax.fori_loop(0, tiles, square_dn, jnp.zeros((dn_ref.shape[0], 1), jnp.float32))
    scale = rates[1] / jnp.sqrt(squares / width + EPSILON)

    @pl.loop(0, tiles)
    def _(i):
        cut = pl.ds(pl.multiple_of(i * tile, tile), tile)
        old = dn_ref[:, cut].astype(jnp.float32)
        new_dn_ref[:, cut] = (old - grads_dn[:, cut] * scale).astype(jnp.bfloat16)

    @pl.when(step == pl.num_programs(0) - 1)
    def _():
        @pl.loop(0, tiles)
        def _(i):
            cut = pl.ds(pl.multiple_of(i * tile, tile), tile)
            dx_ref[:, cut] = total[:, cut].astype(jnp.bfloat16)


def learn_call(place, rows, table, cots, planes, weights_dn, experts, rates):
    row_count = rows.shape[0]
    hidden_count, width = weights_dn.shape
    spare = table.shape[1] - width
    size = hidden_block(hidden_count)
    once = pl.Buffered(1)
    return pl.pallas_call(
        functools.partial(learn_kernel, experts=experts, rates=rates),
        grid_spec=pltpu.PrefetchScalarGridSpec(
            num_scalar_prefetch=1,
            grid=(hidden_count // size,),
            in_specs=[
                pl.BlockSpec((row_count, width), lambda j, p: (0, 0), pipeline_mode=once),
                pl.BlockSpec((row_count, spare), lambda j, p: (0, width // spare)),
                pl.BlockSpec((row_count, width), lambda j, p: (0, 0), pipeline_mode=once),
                pl.BlockSpec((2, width, size), lambda j, p: (0, 0, j)),
                pl.BlockSpec((size, width), lambda j, p: (j, 0)),
            ],
            out_specs=[
                pl.BlockSpec((row_count, width), lambda j, p: (0, 0)),
                pl.BlockSpec((2, width, size), lambda j, p: (0, 0, j)),
                pl.BlockSpec((size, width), lambda j, p: (j, 0)),
            ],
            scratch_shapes=[
                pltpu.VMEM((width, row_count), jnp.bfloat16),
                pltpu.VMEM((row_count, width), jnp.bfloat16),
                pltpu.VMEM((row_count, width), jnp.float32),
                pltpu.VMEM((width, size), jnp.float32),
                pltpu.VMEM((size, width), jnp.float32),
            ],
        ),
        out_shape=[
            jax.ShapeDtypeStruct((row_count, width), jnp.bfloat16),
            jax.ShapeDtypeStruct(planes.shape, jnp.bfloat16),
            jax.ShapeDtypeStruct(weights_dn.shape, jnp.bfloat16),
        ],
        compiler_params=pltpu.CompilerParams(vmem_limit_bytes=58 << 20),
        cost_estimate=pl.CostEstimate(
            flops=16 * row_count * hidden_count * width,
            bytes_accessed=12 * hidden_count * width,
            transcendentals=row_count * hidden_count,
        ),
        name="learn",
    )(place, rows, table, cots, planes, weights_dn)


def unset(like):
    return pl.pallas_call(
        lambda out_ref: None,
        out_shape=jax.ShapeDtypeStruct(like.shape, like.dtype),
        out_specs=pl.BlockSpec(memory_space=pl.ANY),
        name="unset",
    )()


def ffn_plain(place, rows, table, planes, weights_dn, experts):
    width = weights_dn.shape[1]
    rows = rows[:, :width]
    gates = pick_gates(table[:, width:], place[0], experts)
    active = nn(rows, planes[0])
    upward = nn(rows, planes[1])
    hidden = (active * jax.nn.sigmoid(active) * upward).astype(jnp.bfloat16)
    return (gates * nn(hidden, weights_dn)).astype(jnp.bfloat16)


def learn_plain(place, rows, table, cots, planes, weights_dn, experts, rates):
    width = weights_dn.shape[1]
    rows = rows[:, :width]
    gates = pick_gates(table[:, width:], place[0], experts)
    pulls = (gates * cots.astype(jnp.float32)).astype(jnp.bfloat16)
    active = nn(rows, planes[0])
    upward = nn(rows, planes[1])
    back = nt(pulls, weights_dn)
    sigma = jax.nn.sigmoid(active)
    swish = active * sigma
    hidden = (swish * upward).astype(jnp.bfloat16)
    d_active = (back * upward * sigma * (1.0 + active * (1.0 - sigma))).astype(jnp.bfloat16)
    d_upward = (back * swish).astype(jnp.bfloat16)
    dx_part = (nt(d_active, planes[0]) + nt(d_upward, planes[1])).astype(jnp.bfloat16)
    new_planes = jnp.stack(
        [
            renew(planes[0], wide(rows, d_active, ((0,), (0,))), 0, rates[0]),
            renew(planes[1], wide(rows, d_upward, ((0,), (0,))), 0, rates[0]),
        ],
        axis=0,
    )
    new_dn = renew(weights_dn, wide(hidden, pulls, ((0,), (0,))), 1, rates[1])
    return (dx_part, new_planes, new_dn)


def per_device(
    rows_in,
    cotangent,
    lengths,
    train_experts,
    train_gates,
    decode_experts,
    decode_gates,
    gate_up,
    down,
):
    ep_count = lax.axis_size("ep")
    dp_count = lax.axis_size("dp")
    row_count, model_width = cotangent.shape
    is_learner = lax.axis_index("grp") == 0
    hidden_all = gate_up.shape[4] * dp_count
    own_dn = down[0, 0]
    planes = lax.optimization_barrier(jnp.transpose(gate_up[0, 0], (1, 0, 2)))

    own_rows = rows_in[0]
    total_rows = row_count * ep_count * dp_count
    longest = 2 * total_rows // lengths.shape[0]
    first_row = (lax.axis_index("ep") * dp_count + lax.axis_index("dp")) * row_count
    places = first_row + jnp.arange(row_count, dtype=jnp.int32)
    ends = jnp.cumsum(lengths)
    starts = ends - lengths
    inside = (places[:, None] >= starts[None, :]) & (places[:, None] < ends[None, :])
    seq_len = jnp.sum(jnp.where(inside, lengths[None, :], 0), axis=1).astype(jnp.float32)
    weight = 2.0 * longest / (seq_len + longest)
    cot_wide = weight[:, None] * cotangent.astype(jnp.float32)

    train_table = weight[:, None] * gate_table(train_experts, train_gates, ep_count)
    stale_table = gate_table(decode_experts[0], decode_gates[0], ep_count)
    fresh_table = gate_table(decode_experts[1], decode_gates[1], ep_count)
    device_count = ep_count * dp_count
    table = two_part(jnp.where(is_learner, train_table, stale_table)) + two_part(fresh_table)
    spare = -4 * ep_count % 128
    table.append(jnp.zeros((row_count, spare), jnp.bfloat16))
    every = gather(jnp.concatenate([own_rows] + table, axis=1), device_count, (0, 1))
    mine = lax.axis_index("ep").astype(jnp.int32)
    first_place = mine.reshape(1)
    fresh_place = first_place + 2 * ep_count
    rates = (0.5 / model_width**0.5, 0.5 / hidden_all**0.5)
    run_ffn, run_learn = (
        (ffn_call, learn_call) if total_rows <= 256 else (ffn_plain, learn_plain)
    )
    cots = gather(cotangent, device_count, (0,))

    def learn(every, cots, planes, own_dn):
        dx_part, new_planes, new_dn = run_learn(
            first_place, every, every, cots, planes, own_dn, ep_count, rates
        )
        return (unset(dx_part), dx_part, new_planes, new_dn)

    def decode(every, cots, planes, own_dn):
        part = run_ffn(first_place, every, every, planes, own_dn, ep_count)
        return (part, unset(part), unset(planes), unset(own_dn))

    part, dx_part, new_planes, new_dn = lax.cond(
        is_learner, learn, decode, every, cots, planes, own_dn
    )
    stale_sum = scatter_sum(part, device_count, (1,))
    current = (own_rows.astype(jnp.float32) + stale_sum).astype(jnp.bfloat16)
    dx_sum = scatter_sum(dx_part, device_count, (0,))
    arrived = gather(across(current, 1, 0), device_count, (0,))
    fresh_part = lax.cond(
        is_learner,
        lambda r, e, g, d: run_ffn(fresh_place, r, e, g, d, ep_count),
        lambda r, e, g, d: unset(r),
        arrived,
        every,
        new_planes,
        new_dn,
    )
    fresh_sum = scatter_sum(fresh_part, device_count, (0,))
    moved = across(fresh_sum.astype(jnp.bfloat16), 0, 1).astype(jnp.float32)
    final_rows = jnp.where(is_learner, cot_wide + dx_sum, current.astype(jnp.float32) + moved)
    return final_rows.astype(jnp.bfloat16)[None]


def solution(mesh):
    placed = (
        P("grp", ("ep", "dp"), None),
        P(("ep", "dp"), None),
        P(),
        P(("ep", "dp"), None),
        P(("ep", "dp"), None),
        P(None, ("ep", "dp"), None),
        P(None, ("ep", "dp"), None),
        P("grp", "ep", None, None, "dp"),
        P("grp", "ep", "dp", None),
    )
    return jax.shard_map(
        per_device,
        mesh=mesh,
        in_specs=placed,
        out_specs=P("grp", ("ep", "dp"), None),
        check_vma=False,
    )
```

```python
import functools

import jax
import jax.numpy as jnp
from jax import lax
from jax.experimental import pallas as pl
from jax.experimental.pallas import tpu as pltpu
from jax.sharding import PartitionSpec as P

EPSILON = 1e-06
AXES = ("ep", "dp")


def across(block, source, target):
    return lax.ppermute(block, "grp", [(source, target)])


def stages(device_count):
    sizes = []
    rest = device_count
    while rest > 1:
        size = 2 if len(sizes) < 2 or rest % 4 else 4
        sizes.append(size)
        rest //= size
    strides = []
    stride = device_count
    for size in sizes[::-1]:
        stride //= size
        strides.append((stride, size))
    return strides


def swap(block, device_count, flip, role):
    pairs = [
        (part * device_count + i, part * device_count + (i ^ flip))
        for part in role
        for i in range(device_count)
    ]
    return lax.ppermute(block, ("grp",) + AXES, pairs)


def tied(*values):
    return lax.optimization_barrier(values)


def gather(block, device_count, role, beside=None):
    if device_count != 16:
        for stride, size in stages(device_count):
            got = [swap(block, device_count, turn * stride, role) for turn in range(1, size)]
            block = jnp.concatenate([block] + got, axis=0)
        return [block], beside
    far = [swap(block, 16, turn * 4, role) for turn in (1, 2, 3)]
    near = jnp.concatenate([block, far[0]], axis=0)
    if beside is not None:
        near, beside = tied(near, beside)
    away = jnp.concatenate(far[1:], axis=0)
    near = jnp.concatenate([near, swap(near, 16, 2, role)], axis=0)
    away = jnp.concatenate([away, swap(away, 16, 2, role)], axis=0)
    return [near, swap(near, 16, 1, role), away, swap(away, 16, 1, role)], beside


def plus(kept, *sent):
    total = kept.astype(jnp.float32)
    for one in sent:
        total = total + one.astype(jnp.float32)
    return total


def halves(array):
    return jnp.split(array, 2, axis=0)


def scatter_sum_wide(part, device_count, role):
    for stride, size in stages(device_count)[::-1]:
        cuts = jnp.split(part, size, axis=0)
        got = [swap(cuts[turn], device_count, turn * stride, role) for turn in range(1, size)]
        total = plus(cuts[0], *got)
        part = total.astype(jnp.bfloat16)
    return total


def sum_core(pieces, role):
    away = plus(pieces[2], swap(pieces[3], 16, 1, role)).astype(jnp.bfloat16)
    near = plus(pieces[0], swap(pieces[1], 16, 1, role)).astype(jnp.bfloat16)
    return near, away


def sum_y(near, away, role):
    kept, sent = halves(away)
    away = plus(kept, swap(sent, 16, 2, role)).astype(jnp.bfloat16)
    kept, sent = halves(near)
    near = plus(kept, swap(sent, 16, 2, role)).astype(jnp.bfloat16)
    return near, away


def sum_z(near, away, role):
    second, third = [swap(h, 16, f, role) for h, f in zip(halves(away), (8, 12))]
    kept, sent = halves(near)
    return plus(kept, swap(sent, 16, 4, role), second, third)


def scatter_sum(pieces, device_count, role):
    if device_count != 16:
        return scatter_sum_wide(pieces[0], device_count, role)
    near, away = sum_core(pieces, role)
    near, away = sum_y(near, away, role)
    return sum_z(near, away, role)


def renew(weights, grads, axis_number, rate):
    scale = jnp.sqrt(jnp.mean(grads * grads, axis=axis_number, keepdims=True) + EPSILON)
    return (weights.astype(jnp.float32) - rate * grads / scale).astype(jnp.bfloat16)


def wide(a, b, contract):
    return lax.dot_general(a, b, (contract, ((), ())), preferred_element_type=jnp.float32)


def nn(a, b):
    return wide(a, b, ((1,), (0,)))


def nt(a, b):
    return wide(a, b, ((1,), (1,)))


def prep_kernel(
    place, lengths, rows_ref, cot_ref, ids_ref, gates_ref, dec_ids_ref, dec_gates_ref,
    out_ref, base_ref, *, experts, longest,
):
    width = rows_ref.shape[1]
    row_count = rows_ref.shape[0]
    learner = place[1] == 0
    places = place[0] * row_count + lax.broadcasted_iota(jnp.int32, (1, row_count), 1)
    start = jnp.int32(0)
    seq_len = jnp.zeros((1, row_count), jnp.int32)
    for i in range(lengths.shape[0]):
        end = start + lengths[i]
        seq_len = jnp.where((places >= start) & (places < end), lengths[i], seq_len)
        start = end
    weight = 2.0 * longest / (seq_len.astype(jnp.float32) + longest)
    names = lax.broadcasted_iota(jnp.int32, (experts, row_count), 0)

    def table(ids, gates):
        total = jnp.zeros((experts, row_count), jnp.float32)
        for k in range(ids.shape[0]):
            total = total + jnp.where(names == ids[k : k + 1], gates[k : k + 1], 0.0)
        return total

    train = table(ids_ref[...], gates_ref[...]) * weight
    stale = table(dec_ids_ref[0], dec_gates_ref[0])
    first = jnp.where(learner, train, stale)
    fresh = table(dec_ids_ref[1], dec_gates_ref[1])
    parts = []
    for one in (first, fresh):
        upper = one.astype(jnp.bfloat16).astype(jnp.float32)
        parts += [upper, one - upper]
    spare = out_ref.shape[1] - width
    if spare > 4 * experts:
        parts.append(jnp.zeros((spare - 4 * experts, row_count), jnp.float32))
    stacked = jnp.concatenate(parts, axis=0)
    weights = jnp.broadcast_to(weight, (128, row_count))
    square = jnp.concatenate([stacked, weights], axis=0)
    square = jnp.concatenate(
        [square, jnp.zeros((square.shape[0], 128 - row_count), jnp.float32)], axis=1
    )
    for i in range(spare // 128):
        turned = square[128 * i : 128 * (i + 1)].T
        out_ref[:, width + 128 * i : width + 128 * (i + 1)] = turned[:row_count].astype(
            jnp.bfloat16
        )
    column = square[spare:].T[:row_count, 0:1]
    out_ref[:, :width] = rows_ref[...]
    base_ref[...] = jnp.where(
        learner, column * cot_ref[...].astype(jnp.float32), rows_ref[...].astype(jnp.float32)
    )


def prep_call(place, lengths, rows, cot, ids, gates, dec_ids, dec_gates, experts, longest):
    row_count, width = rows.shape
    spare = -(-4 * experts // 128) * 128
    scalars = pl.BlockSpec(memory_space=pltpu.SMEM)
    whole = pl.BlockSpec(memory_space=pltpu.VMEM)
    return pl.pallas_call(
        functools.partial(prep_kernel, experts=experts, longest=longest),
        in_specs=[scalars, scalars] + [whole] * 6,
        out_specs=[whole, whole],
        out_shape=[
            jax.ShapeDtypeStruct((row_count, width + spare), jnp.bfloat16),
            jax.ShapeDtypeStruct((row_count, width), jnp.float32),
        ],
        name="prep",
    )(place, lengths, rows, cot, ids.T, gates.T, jnp.swapaxes(dec_ids, 1, 2), jnp.swapaxes(dec_gates, 1, 2))


def pick_gates(table, column, step):
    places = lax.broadcasted_iota(jnp.int32, table.shape, 1)
    taken = (places == column) | (places == column + step)
    return jnp.sum(jnp.where(taken, table.astype(jnp.float32), 0.0), axis=1, keepdims=True)


def hidden_block(hidden_count):
    return 256 if hidden_count % 256 == 0 else 128


def ffn_kernel(place, *refs, count, experts, steps, size):
    rows_refs, table_refs = refs[:count], refs[count : 2 * count]
    gu_ref, dn_ref = refs[2 * count : 2 * count + 2]
    out_refs = refs[2 * count + 2 : 3 * count + 2]
    rows, hidden = refs[3 * count + 2 :]
    step = pl.program_id(0)
    part = rows_refs[0].shape[0]

    @pl.when(step == 0)
    def _():
        for i in range(count):
            rows[part * i : part * (i + 1), :] = rows_refs[i][...]

    for j in range(steps):

        @pl.when(step == j)
        def _():
            active = nn(rows[...], gu_ref[0])
            upward = nn(rows[...], gu_ref[1])
            hidden[:, size * j : size * (j + 1)] = (
                active * jax.nn.sigmoid(active) * upward
            ).astype(jnp.bfloat16)

    @pl.when(step >= steps)
    def _():
        out = nn(hidden[...], dn_ref[...])
        for i in range(count):
            gates = pick_gates(table_refs[i][...], place[0], experts)
            out_refs[i][...] = (gates * out[part * i : part * (i + 1)]).astype(jnp.bfloat16)


def ffn_call(place, pieces, tables, planes, weights_dn, experts):
    count = len(pieces)
    part = pieces[0].shape[0]
    hidden_count, width = weights_dn.shape
    spare = tables[0].shape[1] - width
    size = hidden_block(hidden_count)
    steps = hidden_count // size
    tile = 1024
    row_count = part * count
    table_at = width // spare
    return pl.pallas_call(
        functools.partial(ffn_kernel, count=count, experts=experts, steps=steps, size=size),
        grid_spec=pltpu.PrefetchScalarGridSpec(
            num_scalar_prefetch=1,
            grid=(steps + width // tile,),
            in_specs=[pl.BlockSpec((part, width), lambda j, p: (0, 0))] * count
            + [pl.BlockSpec((part, spare), lambda j, p: (0, table_at))] * count
            + [
                pl.BlockSpec((2, width, size), lambda j, p: (0, 0, jnp.minimum(j, steps - 1))),
                pl.BlockSpec((hidden_count, tile), lambda j, p: (0, jnp.maximum(j - steps, 0))),
            ],
            out_specs=[pl.BlockSpec((part, tile), lambda j, p: (0, jnp.maximum(j - steps, 0)))]
            * count,
            scratch_shapes=[
                pltpu.VMEM((row_count, width), jnp.bfloat16),
                pltpu.VMEM((row_count, hidden_count), jnp.bfloat16),
            ],
        ),
        out_shape=[jax.ShapeDtypeStruct((part, width), jnp.bfloat16)] * count,
        compiler_params=pltpu.CompilerParams(vmem_limit_bytes=40 << 20),
        cost_estimate=pl.CostEstimate(
            flops=6 * row_count * hidden_count * width,
            bytes_accessed=6 * hidden_count * width,
            transcendentals=row_count * hidden_count,
        ),
        name="ffn",
    )(place, *pieces, *tables, planes, weights_dn)


def learn_kernel(place, *refs, count, experts, rates):
    rows_refs, table_refs, cot_refs = refs[:count], refs[count : 2 * count], refs[2 * count : 3 * count]
    gu_ref, dn_ref = refs[3 * count : 3 * count + 2]
    dx_refs = refs[3 * count + 2 : 4 * count + 2]
    new_gu_ref, new_dn_ref = refs[4 * count + 2 : 4 * count + 4]
    rows, turned, pulls, pulls_turned, total, grads, grads_dn = refs[4 * count + 4 :]
    step = pl.program_id(0)
    part, width = rows_refs[0].shape
    tile = 1024
    cuts = [slice(lower, lower + tile) for lower in range(0, width, tile)]

    @pl.when(step == 0)
    def _():
        for i in range(count):
            here = slice(part * i, part * (i + 1))
            gates = pick_gates(table_refs[i][...], place[0], experts)
            rows[here, :] = rows_refs[i][...]
            pulls[here, :] = (gates * cot_refs[i][...].astype(jnp.float32)).astype(jnp.bfloat16)
        for cut in cuts:
            turned[cut, :] = rows[:, cut].T
            pulls_turned[cut, :] = pulls[:, cut].T
        total[...] = jnp.zeros_like(total)

    active = nn(rows[...], gu_ref[0])
    upward = nn(rows[...], gu_ref[1])
    back = nn(dn_ref[...], pulls_turned[...]).T
    sigma = jax.nn.sigmoid(active)
    swish = active * sigma
    hidden = (swish * upward).astype(jnp.bfloat16)
    d_active = (back * upward * sigma * (1.0 + active * (1.0 - sigma))).astype(jnp.bfloat16)
    d_upward = (back * swish).astype(jnp.bfloat16)
    hidden_turned = hidden.T
    d_active_turned = d_active.T
    d_upward_turned = d_upward.T

    for cut in cuts:
        total[cut, :] += nn(gu_ref[0, cut, :], d_active_turned) + nn(
            gu_ref[1, cut, :], d_upward_turned
        )

    for half, sent in ((0, d_active), (1, d_upward)):
        squares = jnp.zeros((8, sent.shape[1]), jnp.float32)
        for cut in cuts:
            fresh = nn(turned[cut, :], sent)
            grads[cut, :] = fresh
            squares = squares + jnp.sum((fresh * fresh).reshape(-1, 8, sent.shape[1]), axis=0)
        squares = jnp.sum(squares, axis=0, keepdims=True)
        scale = rates[0] / jnp.sqrt(squares / width + EPSILON)
        for cut in cuts:
            old = gu_ref[half, cut, :].astype(jnp.float32)
            new_gu_ref[half, cut, :] = (old - grads[cut, :] * scale).astype(jnp.bfloat16)

    squares = jnp.zeros((dn_ref.shape[0], 1), jnp.float32)
    for cut in cuts:
        fresh = nn(hidden_turned, pulls[:, cut])
        grads_dn[:, cut] = fresh
        squares = squares + jnp.sum(fresh * fresh, axis=1, keepdims=True)
    scale = rates[1] / jnp.sqrt(squares / width + EPSILON)
    for cut in cuts:
        old = dn_ref[:, cut].astype(jnp.float32)
        new_dn_ref[:, cut] = (old - grads_dn[:, cut] * scale).astype(jnp.bfloat16)

    @pl.when(step == pl.num_programs(0) - 1)
    def _():
        for cut in cuts:
            done = total[cut, :].T.astype(jnp.bfloat16)
            for i in range(count):
                dx_refs[i][:, cut] = done[part * i : part * (i + 1)]


def learn_call(place, pieces, tables, cots, planes, weights_dn, experts, rates):
    count = len(pieces)
    part = pieces[0].shape[0]
    hidden_count, width = weights_dn.shape
    spare = tables[0].shape[1] - width
    size = hidden_block(hidden_count)
    row_count = part * count
    table_at = width // spare
    once = pl.Buffered(1)
    piece = pl.BlockSpec((part, width), lambda j, p: (0, 0), pipeline_mode=once)
    return pl.pallas_call(
        functools.partial(learn_kernel, count=count, experts=experts, rates=rates),
        grid_spec=pltpu.PrefetchScalarGridSpec(
            num_scalar_prefetch=1,
            grid=(hidden_count // size,),
            in_specs=[piece] * count
            + [pl.BlockSpec((part, spare), lambda j, p: (0, table_at))] * count
            + [piece] * count
            + [
                pl.BlockSpec((2, width, size), lambda j, p: (0, 0, j)),
                pl.BlockSpec((size, width), lambda j, p: (j, 0)),
            ],
            out_specs=[pl.BlockSpec((part, width), lambda j, p: (0, 0))] * count
            + [
                pl.BlockSpec((2, width, size), lambda j, p: (0, 0, j)),
                pl.BlockSpec((size, width), lambda j, p: (j, 0)),
            ],
            scratch_shapes=[
                pltpu.VMEM((row_count, width), jnp.bfloat16),
                pltpu.VMEM((width, row_count), jnp.bfloat16),
                pltpu.VMEM((row_count, width), jnp.bfloat16),
                pltpu.VMEM((width, row_count), jnp.bfloat16),
                pltpu.VMEM((width, row_count), jnp.float32),
                pltpu.VMEM((width, size), jnp.float32),
                pltpu.VMEM((size, width), jnp.float32),
            ],
        ),
        out_shape=[jax.ShapeDtypeStruct((part, width), jnp.bfloat16)] * count
        + [
            jax.ShapeDtypeStruct(planes.shape, jnp.bfloat16),
            jax.ShapeDtypeStruct(weights_dn.shape, jnp.bfloat16),
        ],
        compiler_params=pltpu.CompilerParams(vmem_limit_bytes=60 << 20),
        cost_estimate=pl.CostEstimate(
            flops=16 * row_count * hidden_count * width,
            bytes_accessed=12 * hidden_count * width,
            transcendentals=row_count * hidden_count,
        ),
        name="learn",
    )(place, *pieces, *tables, *cots, planes, weights_dn)


def unset(like):
    return pl.pallas_call(
        lambda out_ref: None,
        out_shape=jax.ShapeDtypeStruct(like.shape, like.dtype),
        out_specs=pl.BlockSpec(memory_space=pl.ANY),
        name="unset",
    )()


def ffn_plain(place, pieces, tables, planes, weights_dn, experts):
    width = weights_dn.shape[1]
    rows = pieces[0][:, :width]
    gates = pick_gates(tables[0][:, width:], place[0], experts)
    active = nn(rows, planes[0])
    upward = nn(rows, planes[1])
    hidden = (active * jax.nn.sigmoid(active) * upward).astype(jnp.bfloat16)
    return [(gates * nn(hidden, weights_dn)).astype(jnp.bfloat16)]


def learn_plain(place, pieces, tables, cots, planes, weights_dn, experts, rates):
    width = weights_dn.shape[1]
    rows = pieces[0][:, :width]
    gates = pick_gates(tables[0][:, width:], place[0], experts)
    pulls = (gates * cots[0].astype(jnp.float32)).astype(jnp.bfloat16)
    active = nn(rows, planes[0])
    upward = nn(rows, planes[1])
    back = nt(pulls, weights_dn)
    sigma = jax.nn.sigmoid(active)
    swish = active * sigma
    hidden = (swish * upward).astype(jnp.bfloat16)
    d_active = (back * upward * sigma * (1.0 + active * (1.0 - sigma))).astype(jnp.bfloat16)
    d_upward = (back * swish).astype(jnp.bfloat16)
    dx_part = (nt(d_active, planes[0]) + nt(d_upward, planes[1])).astype(jnp.bfloat16)
    new_planes = jnp.stack(
        [
            renew(planes[0], wide(rows, d_active, ((0,), (0,))), 0, rates[0]),
            renew(planes[1], wide(rows, d_upward, ((0,), (0,))), 0, rates[0]),
        ],
        axis=0,
    )
    new_dn = renew(weights_dn, wide(hidden, pulls, ((0,), (0,))), 1, rates[1])
    return [dx_part, new_planes, new_dn]


def per_device(
    rows_in,
    cotangent,
    lengths,
    train_experts,
    train_gates,
    decode_experts,
    decode_gates,
    gate_up,
    down,
):
    ep_count = lax.axis_size("ep")
    dp_count = lax.axis_size("dp")
    device_count = ep_count * dp_count
    row_count, model_width = cotangent.shape
    role = lax.axis_index("grp").astype(jnp.int32)
    is_learner = role == 0
    mine = lax.axis_index("ep").astype(jnp.int32)
    own_dn = down[0, 0]
    planes = jnp.transpose(gate_up[0, 0], (1, 0, 2))
    total_rows = row_count * device_count
    longest = 2 * total_rows // lengths.shape[0]
    rates = (0.5 / model_width**0.5, 0.5 / (own_dn.shape[0] * dp_count) ** 0.5)
    small = device_count == 16
    run_ffn, run_learn = (ffn_call, learn_call) if small else (ffn_plain, learn_plain)
    first_place = mine.reshape(1)
    fresh_place = first_place + 2 * ep_count

    where = jnp.stack([mine * dp_count + lax.axis_index("dp").astype(jnp.int32), role])
    block, base = prep_call(
        where, lengths, rows_in[0], cotangent, train_experts, train_gates, decode_experts,
        decode_gates, ep_count, longest,
    )
    every, planes = gather(block, device_count, (0, 1), planes)
    count = len(every)
    cotangent, every[0] = tied(cotangent, every[0])
    cots, _ = gather(cotangent, device_count, (0,))

    def learn(every, cots, planes, own_dn):
        out = list(run_learn(first_place, every, every, cots, planes, own_dn, ep_count, rates))
        return ([unset(o) for o in out[:count]], out[:count], out[count], out[count + 1])

    def decode(every, cots, planes, own_dn):
        out = list(run_ffn(first_place, every, every, planes, own_dn, ep_count))
        return (out, [unset(o) for o in out], unset(planes), unset(own_dn))

    part, dx_part, new_planes, new_dn = lax.cond(
        is_learner, learn, decode, every, cots, planes, own_dn
    )
    stale_sum = scatter_sum(part, device_count, (1,))
    current = (base + stale_sum).astype(jnp.bfloat16)
    hopped = across(current, 1, 0)
    if small:
        dx_near, dx_away = sum_core(dx_part, (0,))
    arrived, _ = gather(hopped, device_count, (0,))
    if small:
        arrived[0], dx_near, dx_away = tied(arrived[0], dx_near, dx_away)
        dx_near, dx_away = sum_y(dx_near, dx_away, (0,))

    fresh_part = lax.cond(
        is_learner,
        lambda r, e, g, d: list(run_ffn(fresh_place, r, e, g, d, ep_count)),
        lambda r, e, g, d: [unset(o) for o in r],
        arrived,
        every,
        new_planes,
        new_dn,
    )
    if small:
        near, away = sum_core(fresh_part, (0,))
        near, away, dx_near, dx_away = tied(near, away, dx_near, dx_away)
        dx_sum = sum_z(dx_near, dx_away, (0,))
        near, away = sum_y(near, away, (0,))
        fresh_sum = sum_z(near, away, (0,))
    else:
        dx_sum = scatter_sum(dx_part, device_count, (0,))
        fresh_sum = scatter_sum(fresh_part, device_count, (0,))
    moved = across(fresh_sum.astype(jnp.bfloat16), 0, 1).astype(jnp.float32)
    final_rows = jnp.where(is_learner, base + dx_sum, current.astype(jnp.float32) + moved)
    return final_rows.astype(jnp.bfloat16)[None]


def solution(mesh):
    placed = (
        P("grp", ("ep", "dp"), None),
        P(("ep", "dp"), None),
        P(),
        P(("ep", "dp"), None),
        P(("ep", "dp"), None),
        P(None, ("ep", "dp"), None),
        P(None, ("ep", "dp"), None),
        P("grp", "ep", None, None, "dp"),
        P("grp", "ep", "dp", None),
    )
    return jax.shard_map(
        per_device,
        mesh=mesh,
        in_specs=placed,
        out_specs=P("grp", ("ep", "dp"), None),
        check_vma=False,
    )
```

```python
import functools

import jax
import jax.numpy as jnp
from jax import lax
from jax.experimental import pallas as pl
from jax.experimental.pallas import tpu as pltpu
from jax.sharding import PartitionSpec as P

EPSILON = 1e-06
AXES = ("ep", "dp")


def across(block, source, target):
    return lax.ppermute(block, "grp", [(source, target)])


def stages(device_count):
    sizes = []
    rest = device_count
    while rest > 1:
        size = 2 if len(sizes) < 2 or rest % 4 else 4
        sizes.append(size)
        rest //= size
    strides = []
    stride = device_count
    for size in sizes[::-1]:
        stride //= size
        strides.append((stride, size))
    return strides


def swap(block, device_count, flip, role):
    pairs = [
        (part * device_count + i, part * device_count + (i ^ flip))
        for part in role
        for i in range(device_count)
    ]
    return lax.ppermute(block, ("grp",) + AXES, pairs)


def tied(*values):
    return lax.optimization_barrier(values)


def gather(block, device_count, role, beside=None):
    if device_count != 16:
        for stride, size in stages(device_count):
            got = [swap(block, device_count, turn * stride, role) for turn in range(1, size)]
            block = jnp.concatenate([block] + got, axis=0)
        return [block], beside
    far = [swap(block, 16, turn * 4, role) for turn in (1, 2, 3)]
    near = jnp.concatenate([block, far[0]], axis=0)
    if beside is not None:
        near, beside = tied(near, beside)
    away = jnp.concatenate(far[1:], axis=0)
    near = jnp.concatenate([near, swap(near, 16, 2, role)], axis=0)
    away = jnp.concatenate([away, swap(away, 16, 2, role)], axis=0)
    return [near, swap(near, 16, 1, role), away, swap(away, 16, 1, role)], beside


def piece_places():
    near = (0, 4, 2, 6)
    away = (8, 12, 10, 14)
    return [near, [i ^ 1 for i in near], away, [i ^ 1 for i in away]]


def plus(kept, *sent):
    total = kept.astype(jnp.float32)
    for one in sent:
        total = total + one.astype(jnp.float32)
    return total


def halves(array):
    return jnp.split(array, 2, axis=0)


def scatter_sum_wide(part, device_count, role):
    for stride, size in stages(device_count)[::-1]:
        cuts = jnp.split(part, size, axis=0)
        got = [swap(cuts[turn], device_count, turn * stride, role) for turn in range(1, size)]
        total = plus(cuts[0], *got)
        part = total.astype(jnp.bfloat16)
    return total


def sum_core(pieces, role):
    away = plus(pieces[2], swap(pieces[3], 16, 1, role)).astype(jnp.bfloat16)
    near = plus(pieces[0], swap(pieces[1], 16, 1, role)).astype(jnp.bfloat16)
    return near, away


def sum_y(near, away, role):
    kept, sent = halves(away)
    away = plus(kept, swap(sent, 16, 2, role)).astype(jnp.bfloat16)
    kept, sent = halves(near)
    near = plus(kept, swap(sent, 16, 2, role)).astype(jnp.bfloat16)
    return near, away


def sum_z(near, away, role):
    second, third = [swap(h, 16, f, role) for h, f in zip(halves(away), (8, 12))]
    kept, sent = halves(near)
    return plus(kept, swap(sent, 16, 4, role), second, third)


def scatter_sum(pieces, device_count, role):
    if device_count != 16:
        return scatter_sum_wide(pieces[0], device_count, role)
    near, away = sum_core(pieces, role)
    near, away = sum_y(near, away, role)
    return sum_z(near, away, role)


def renew(weights, grads, axis_number, rate):
    scale = jnp.sqrt(jnp.mean(grads * grads, axis=axis_number, keepdims=True) + EPSILON)
    return (weights.astype(jnp.float32) - rate * grads / scale).astype(jnp.bfloat16)


def wide(a, b, contract):
    return lax.dot_general(a, b, (contract, ((), ())), preferred_element_type=jnp.float32)


def nn(a, b):
    return wide(a, b, ((1,), (0,)))


def nt(a, b):
    return wide(a, b, ((1,), (1,)))


def prep_kernel(
    place, lengths, rows_ref, cot_ref, ids_ref, gates_ref, dec_ids_ref, dec_gates_ref,
    out_ref, base_ref, *, experts, longest,
):
    width = rows_ref.shape[1]
    row_count = rows_ref.shape[0]
    learner = place[1] == 0
    places = place[0] * row_count + lax.broadcasted_iota(jnp.int32, (1, row_count), 1)
    start = jnp.int32(0)
    seq_len = jnp.zeros((1, row_count), jnp.int32)
    for i in range(lengths.shape[0]):
        end = start + lengths[i]
        seq_len = jnp.where((places >= start) & (places < end), lengths[i], seq_len)
        start = end
    weight = 2.0 * longest / (seq_len.astype(jnp.float32) + longest)
    names = lax.broadcasted_iota(jnp.int32, (experts, row_count), 0)

    def table(ids, gates):
        total = jnp.zeros((experts, row_count), jnp.float32)
        for k in range(ids.shape[0]):
            total = total + jnp.where(names == ids[k : k + 1], gates[k : k + 1], 0.0)
        return total

    train = table(ids_ref[...], gates_ref[...]) * weight
    stale = table(dec_ids_ref[0], dec_gates_ref[0])
    first = jnp.where(learner, train, stale)
    fresh = table(dec_ids_ref[1], dec_gates_ref[1])
    parts = []
    for one in (first, fresh):
        upper = one.astype(jnp.bfloat16).astype(jnp.float32)
        parts += [upper, one - upper]
    spare = out_ref.shape[1] - width
    if spare > 4 * experts:
        parts.append(jnp.zeros((spare - 4 * experts, row_count), jnp.float32))
    stacked = jnp.concatenate(parts, axis=0)
    weights = jnp.broadcast_to(weight, (128, row_count))
    square = jnp.concatenate([stacked, weights], axis=0)
    square = jnp.concatenate(
        [square, jnp.zeros((square.shape[0], 128 - row_count), jnp.float32)], axis=1
    )
    for i in range(spare // 128):
        turned = square[128 * i : 128 * (i + 1)].T
        out_ref[:, width + 128 * i : width + 128 * (i + 1)] = turned[:row_count].astype(
            jnp.bfloat16
        )
    column = square[spare:].T[:row_count, 0:1]
    out_ref[:, :width] = rows_ref[...]
    base_ref[...] = jnp.where(
        learner, column * cot_ref[...].astype(jnp.float32), rows_ref[...].astype(jnp.float32)
    )


def prep_call(place, lengths, rows, cot, ids, gates, dec_ids, dec_gates, experts, longest):
    row_count, width = rows.shape
    spare = -(-4 * experts // 128) * 128
    scalars = pl.BlockSpec(memory_space=pltpu.SMEM)
    whole = pl.BlockSpec(memory_space=pltpu.VMEM)
    return pl.pallas_call(
        functools.partial(prep_kernel, experts=experts, longest=longest),
        in_specs=[scalars, scalars] + [whole] * 6,
        out_specs=[whole, whole],
        out_shape=[
            jax.ShapeDtypeStruct((row_count, width + spare), jnp.bfloat16),
            jax.ShapeDtypeStruct((row_count, width), jnp.float32),
        ],
        name="prep",
    )(place, lengths, rows, cot, ids.T, gates.T, jnp.swapaxes(dec_ids, 1, 2), jnp.swapaxes(dec_gates, 1, 2))


def pick_gates(table, column, step):
    places = lax.broadcasted_iota(jnp.int32, table.shape, 1)
    taken = (places == column) | (places == column + step)
    return jnp.sum(jnp.where(taken, table.astype(jnp.float32), 0.0), axis=1, keepdims=True)


def hidden_block(hidden_count):
    return 256 if hidden_count % 256 == 0 else 128


def ffn_kernel(place, *refs, count, experts, steps):
    rows_refs, table_refs = refs[:count], refs[count : 2 * count]
    gu_ref, dn_ref = refs[2 * count : 2 * count + 2]
    out_refs = refs[2 * count + 2 : 3 * count + 2]
    active, upward, hidden = refs[3 * count + 2 :]
    step = pl.program_id(0)
    part = rows_refs[0].shape[0]

    def products():
        rows = jnp.concatenate([r[...] for r in rows_refs], axis=0)
        return nn(rows, gu_ref[0]), nn(rows, gu_ref[1])

    @pl.when(step == 0)
    def _():
        active[...], upward[...] = products()

    @pl.when((step > 0) & (step < steps - 1))
    def _():
        more_active, more_upward = products()
        active[...] += more_active
        upward[...] += more_upward

    @pl.when(step == steps - 1)
    def _():
        more_active, more_upward = products()
        whole = active[...] + more_active
        hidden[...] = (whole * jax.nn.sigmoid(whole) * (upward[...] + more_upward)).astype(
            jnp.bfloat16
        )

    @pl.when(step >= steps)
    def _():
        out = nn(hidden[...], dn_ref[...])
        for i in range(count):
            gates = pick_gates(table_refs[i][...], place[0], experts)
            out_refs[i][...] = (gates * out[part * i : part * (i + 1)]).astype(jnp.bfloat16)


def ffn_call(place, pieces, tables, planes, weights_dn, experts):
    count = len(pieces)
    part = pieces[0].shape[0]
    hidden_count, width = weights_dn.shape
    spare = tables[0].shape[1] - width
    tile = 1024
    steps = width // tile
    row_count = part * count
    table_at = width // spare
    return pl.pallas_call(
        functools.partial(ffn_kernel, count=count, experts=experts, steps=steps),
        grid_spec=pltpu.PrefetchScalarGridSpec(
            num_scalar_prefetch=1,
            grid=(2 * steps,),
            in_specs=[pl.BlockSpec((part, tile), lambda j, p: (0, jnp.minimum(j, steps - 1)))]
            * count
            + [pl.BlockSpec((part, spare), lambda j, p: (0, table_at))] * count
            + [
                pl.BlockSpec(
                    (2, tile, hidden_count), lambda j, p: (0, jnp.minimum(j, steps - 1), 0)
                ),
                pl.BlockSpec((hidden_count, tile), lambda j, p: (0, jnp.maximum(j - steps, 0))),
            ],
            out_specs=[pl.BlockSpec((part, tile), lambda j, p: (0, jnp.maximum(j - steps, 0)))]
            * count,
            scratch_shapes=[
                pltpu.VMEM((row_count, hidden_count), jnp.float32),
                pltpu.VMEM((row_count, hidden_count), jnp.float32),
                pltpu.VMEM((row_count, hidden_count), jnp.bfloat16),
            ],
        ),
        out_shape=[jax.ShapeDtypeStruct((part, width), jnp.bfloat16)] * count,
        compiler_params=pltpu.CompilerParams(vmem_limit_bytes=40 << 20),
        cost_estimate=pl.CostEstimate(
            flops=6 * row_count * hidden_count * width,
            bytes_accessed=6 * hidden_count * width,
            transcendentals=row_count * hidden_count,
        ),
        name="ffn",
    )(place, *pieces, *tables, planes, weights_dn)


def learn_kernel(place, *refs, count, experts, rates):
    rows_refs, table_refs = refs[:count], refs[count : 2 * count]
    cot_ref, gu_ref, dn_ref, dx_ref, new_gu_ref, new_dn_ref = refs[2 * count : 2 * count + 6]
    rows, turned, pulls, pulls_turned, total, grads_gu, grads_dn = refs[2 * count + 6 :]
    step = pl.program_id(0)
    part = rows_refs[0].shape[0]
    width = dn_ref.shape[1]
    sources = piece_places()
    block = part // len(sources[0])
    tile = 1024
    cuts = [slice(lower, lower + tile) for lower in range(0, width, tile)]

    @pl.when(step == 0)
    def _():
        for i in range(count):
            here = slice(part * i, part * (i + 1))
            gates = pick_gates(table_refs[i][...], place[0], experts)
            rows[here, :] = rows_refs[i][...]
            for j, source in enumerate(sources[i]):
                lower = part * i + block * j
                cots = cot_ref[pl.ds(pl.multiple_of((place[0] ^ source) * block, block), block), :]
                pulls[lower : lower + block, :] = (
                    gates[block * j : block * (j + 1)] * cots.astype(jnp.float32)
                ).astype(jnp.bfloat16)
        for cut in cuts:
            turned[cut, :] = rows[:, cut].T
            pulls_turned[cut, :] = pulls[:, cut].T
        total[...] = jnp.zeros_like(total)

    active = nn(rows[...], gu_ref[0])
    upward = nn(rows[...], gu_ref[1])
    back = nn(dn_ref[...], pulls_turned[...]).T
    sigma = jax.nn.sigmoid(active)
    swish = active * sigma
    hidden = (swish * upward).astype(jnp.bfloat16)
    d_active = (back * upward * sigma * (1.0 + active * (1.0 - sigma))).astype(jnp.bfloat16)
    d_upward = (back * swish).astype(jnp.bfloat16)
    hidden_turned = hidden.T
    d_active_turned = d_active.T
    d_upward_turned = d_upward.T

    for cut in cuts:
        total[cut, :] += nn(gu_ref[0, cut, :], d_active_turned) + nn(
            gu_ref[1, cut, :], d_upward_turned
        )

    for half, sent in ((0, d_active), (1, d_upward)):
        grads = grads_gu.at[half]
        squares = jnp.zeros((8, sent.shape[1]), jnp.float32)
        for cut in cuts:
            fresh = nn(turned[cut, :], sent)
            grads[cut, :] = fresh
            squares = squares + jnp.sum((fresh * fresh).reshape(-1, 8, sent.shape[1]), axis=0)
        squares = jnp.sum(squares, axis=0, keepdims=True)
        scale = rates[0] / jnp.sqrt(squares / width + EPSILON)
        for cut in cuts:
            old = gu_ref[half, cut, :].astype(jnp.float32)
            new_gu_ref[half, cut, :] = (old - grads[cut, :] * scale).astype(jnp.bfloat16)

    squares = jnp.zeros((dn_ref.shape[0], 1), jnp.float32)
    for cut in cuts:
        fresh = nn(hidden_turned, pulls[:, cut])
        grads_dn[:, cut] = fresh
        squares = squares + jnp.sum(fresh * fresh, axis=1, keepdims=True)
    scale = rates[1] / jnp.sqrt(squares / width + EPSILON)
    for cut in cuts:
        old = dn_ref[:, cut].astype(jnp.float32)
        new_dn_ref[:, cut] = (old - grads_dn[:, cut] * scale).astype(jnp.bfloat16)

    @pl.when(step == pl.num_programs(0) - 1)
    def _():
        for cut in cuts:
            done = total[cut, :].T.astype(jnp.bfloat16)
            for i in range(count):
                for j, source in enumerate(sources[i]):
                    lower = part * i + block * j
                    goal = pl.ds(pl.multiple_of((place[0] ^ source) * block, block), block)
                    dx_ref[goal, cut] = done[lower : lower + block]


def learn_call(place, pieces, tables, cots, planes, weights_dn, experts, rates):
    count = len(pieces)
    part = pieces[0].shape[0]
    hidden_count, width = weights_dn.shape
    spare = tables[0].shape[1] - width
    size = hidden_block(hidden_count)
    row_count = part * count
    table_at = width // spare
    once = pl.Buffered(1)
    piece = pl.BlockSpec((part, width), lambda j, p: (0, 0), pipeline_mode=once)
    return pl.pallas_call(
        functools.partial(learn_kernel, count=count, experts=experts, rates=rates),
        grid_spec=pltpu.PrefetchScalarGridSpec(
            num_scalar_prefetch=1,
            grid=(hidden_count // size,),
            in_specs=[piece] * count
            + [pl.BlockSpec((part, spare), lambda j, p: (0, table_at))] * count
            + [
                pl.BlockSpec((row_count, width), lambda j, p: (0, 0), pipeline_mode=once),
                pl.BlockSpec((2, width, size), lambda j, p: (0, 0, j)),
                pl.BlockSpec((size, width), lambda j, p: (j, 0)),
            ],
            out_specs=[
                pl.BlockSpec((row_count, width), lambda j, p: (0, 0), pipeline_mode=once),
                pl.BlockSpec((2, width, size), lambda j, p: (0, 0, j)),
                pl.BlockSpec((size, width), lambda j, p: (j, 0)),
            ],
            scratch_shapes=[
                pltpu.VMEM((row_count, width), jnp.bfloat16),
                pltpu.VMEM((width, row_count), jnp.bfloat16),
                pltpu.VMEM((row_count, width), jnp.bfloat16),
                pltpu.VMEM((width, row_count), jnp.bfloat16),
                pltpu.VMEM((width, row_count), jnp.float32),
                pltpu.VMEM((2, width, size), jnp.float32),
                pltpu.VMEM((size, width), jnp.float32),
            ],
        ),
        out_shape=[
            jax.ShapeDtypeStruct((row_count, width), jnp.bfloat16),
            jax.ShapeDtypeStruct(planes.shape, jnp.bfloat16),
            jax.ShapeDtypeStruct(weights_dn.shape, jnp.bfloat16),
        ],
        compiler_params=pltpu.CompilerParams(vmem_limit_bytes=60 << 20),
        cost_estimate=pl.CostEstimate(
            flops=16 * row_count * hidden_count * width,
            bytes_accessed=12 * hidden_count * width,
            transcendentals=row_count * hidden_count,
        ),
        name="learn",
    )(place, *pieces, *tables, cots, planes, weights_dn)


def unset(like):
    return pl.pallas_call(
        lambda out_ref: None,
        out_shape=jax.ShapeDtypeStruct(like.shape, like.dtype),
        out_specs=pl.BlockSpec(memory_space=pl.ANY),
        name="unset",
    )()


def ffn_plain(place, pieces, tables, planes, weights_dn, experts):
    width = weights_dn.shape[1]
    rows = pieces[0][:, :width]
    gates = pick_gates(tables[0][:, width:], place[0], experts)
    active = nn(rows, planes[0])
    upward = nn(rows, planes[1])
    hidden = (active * jax.nn.sigmoid(active) * upward).astype(jnp.bfloat16)
    return [(gates * nn(hidden, weights_dn)).astype(jnp.bfloat16)]


def learn_plain(place, pieces, tables, cots, planes, weights_dn, experts, rates):
    width = weights_dn.shape[1]
    rows = pieces[0][:, :width]
    gates = pick_gates(tables[0][:, width:], place[0], experts)
    pulls = (gates * cots.astype(jnp.float32)).astype(jnp.bfloat16)
    active = nn(rows, planes[0])
    upward = nn(rows, planes[1])
    back = nt(pulls, weights_dn)
    sigma = jax.nn.sigmoid(active)
    swish = active * sigma
    hidden = (swish * upward).astype(jnp.bfloat16)
    d_active = (back * upward * sigma * (1.0 + active * (1.0 - sigma))).astype(jnp.bfloat16)
    d_upward = (back * swish).astype(jnp.bfloat16)
    dx_part = (nt(d_active, planes[0]) + nt(d_upward, planes[1])).astype(jnp.bfloat16)
    new_planes = jnp.stack(
        [
            renew(planes[0], wide(rows, d_active, ((0,), (0,))), 0, rates[0]),
            renew(planes[1], wide(rows, d_upward, ((0,), (0,))), 0, rates[0]),
        ],
        axis=0,
    )
    new_dn = renew(weights_dn, wide(hidden, pulls, ((0,), (0,))), 1, rates[1])
    return [dx_part, new_planes, new_dn]


def per_device(
    rows_in,
    cotangent,
    lengths,
    train_experts,
    train_gates,
    decode_experts,
    decode_gates,
    gate_up,
    down,
):
    ep_count = lax.axis_size("ep")
    dp_count = lax.axis_size("dp")
    device_count = ep_count * dp_count
    row_count, model_width = cotangent.shape
    role = lax.axis_index("grp").astype(jnp.int32)
    is_learner = role == 0
    mine = lax.axis_index("ep").astype(jnp.int32)
    own_dn = down[0, 0]
    planes = jnp.transpose(gate_up[0, 0], (1, 0, 2))
    total_rows = row_count * device_count
    longest = 2 * total_rows // lengths.shape[0]
    rates = (0.5 / model_width**0.5, 0.5 / (own_dn.shape[0] * dp_count) ** 0.5)
    small = device_count == 16
    run_ffn, run_learn = (ffn_call, learn_call) if small else (ffn_plain, learn_plain)
    first_place = mine.reshape(1)
    fresh_place = first_place + 2 * ep_count

    where = jnp.stack([mine * dp_count + lax.axis_index("dp").astype(jnp.int32), role])
    block, base = prep_call(
        where, lengths, rows_in[0], cotangent, train_experts, train_gates, decode_experts,
        decode_gates, ep_count, longest,
    )
    every, planes = gather(block, device_count, (0, 1), planes)
    count = len(every)
    if small:
        cots = lax.all_gather(cotangent, AXES, tiled=True)
    else:
        cots = gather(cotangent, device_count, (0,))[0][0]

    def learn(every, cots, planes, own_dn):
        out = list(run_learn(first_place, every, every, cots, planes, own_dn, ep_count, rates))
        blank = jax.ShapeDtypeStruct((total_rows // count, model_width), jnp.bfloat16)
        return ([unset(blank)] * count, out[0], out[1], out[2])

    def decode(every, cots, planes, own_dn):
        out = list(run_ffn(first_place, every, every, planes, own_dn, ep_count))
        return (out, unset(cots), unset(planes), unset(own_dn))

    part, dx_part, new_planes, new_dn = lax.cond(
        is_learner, learn, decode, every, cots, planes, own_dn
    )
    stale_sum = scatter_sum(part, device_count, (1,))
    current = (base + stale_sum).astype(jnp.bfloat16)
    if small:
        current, dx_part = tied(current, dx_part)
        dx_sum = lax.psum_scatter(dx_part, AXES, scatter_dimension=0, tiled=True)
        dx_sum = dx_sum.astype(jnp.float32)
    else:
        dx_sum = scatter_sum([dx_part], device_count, (0,))
    arrived, _ = gather(across(current, 1, 0), device_count, (0,))
    fresh_part = lax.cond(
        is_learner,
        lambda r, e, g, d: list(run_ffn(fresh_place, r, e, g, d, ep_count)),
        lambda r, e, g, d: [unset(o) for o in r],
        arrived,
        every,
        new_planes,
        new_dn,
    )
    fresh_sum = scatter_sum(fresh_part, device_count, (0,))
    moved = across(fresh_sum.astype(jnp.bfloat16), 0, 1).astype(jnp.float32)
    final_rows = jnp.where(is_learner, base + dx_sum, current.astype(jnp.float32) + moved)
    return final_rows.astype(jnp.bfloat16)[None]


def solution(mesh):
    placed = (
        P("grp", ("ep", "dp"), None),
        P(("ep", "dp"), None),
        P(),
        P(("ep", "dp"), None),
        P(("ep", "dp"), None),
        P(None, ("ep", "dp"), None),
        P(None, ("ep", "dp"), None),
        P("grp", "ep", None, None, "dp"),
        P("grp", "ep", "dp", None),
    )
    return jax.shard_map(
        per_device,
        mesh=mesh,
        in_specs=placed,
        out_specs=P("grp", ("ep", "dp"), None),
        check_vma=False,
    )
```

```python
import functools

import jax
import jax.numpy as jnp
from jax import lax
from jax.experimental import pallas as pl
from jax.experimental.pallas import tpu as pltpu
from jax.sharding import PartitionSpec as P

EPSILON = 1e-06
AXES = ("ep", "dp")


def across(block, source, target):
    return lax.ppermute(block, "grp", [(source, target)])


def stages(device_count):
    sizes = []
    rest = device_count
    while rest > 1:
        size = 2 if len(sizes) < 2 or rest % 4 else 4
        sizes.append(size)
        rest //= size
    strides = []
    stride = device_count
    for size in sizes[::-1]:
        stride //= size
        strides.append((stride, size))
    return strides


def swap(block, device_count, flip, role):
    pairs = [
        (part * device_count + i, part * device_count + (i ^ flip))
        for part in role
        for i in range(device_count)
    ]
    return lax.ppermute(block, ("grp",) + AXES, pairs)


def tied(*values):
    return lax.optimization_barrier(values)


def gather(block, device_count, role):
    for stride, size in stages(device_count):
        got = [swap(block, device_count, turn * stride, role) for turn in range(1, size)]
        block = jnp.concatenate([block] + got, axis=0)
    return block


def send_z(block, role):
    far = [swap(block, 16, flip, role) for flip in (4, 8, 12)]
    return jnp.concatenate([block, far[0]], axis=0), jnp.concatenate(far[1:], axis=0)


def send_y(near, away, role):
    return [jnp.concatenate([part, swap(part, 16, 2, role)], axis=0) for part in (near, away)]


def send_core(near, away, role):
    return [near, swap(near, 16, 1, role), away, swap(away, 16, 1, role)]


def plus(kept, *sent):
    total = kept.astype(jnp.float32)
    for one in sent:
        total = total + one.astype(jnp.float32)
    return total


def halves(array):
    return jnp.split(array, 2, axis=0)


def scatter_sum(part, device_count, role):
    for stride, size in stages(device_count)[::-1]:
        cuts = jnp.split(part, size, axis=0)
        got = [swap(cuts[turn], device_count, turn * stride, role) for turn in range(1, size)]
        total = plus(cuts[0], *got)
        part = total.astype(jnp.bfloat16)
    return total


def sum_core(pieces, role):
    away = plus(pieces[2], swap(pieces[3], 16, 1, role)).astype(jnp.bfloat16)
    near = plus(pieces[0], swap(pieces[1], 16, 1, role)).astype(jnp.bfloat16)
    return near, away


def sum_y(near, away, role):
    kept, sent = halves(away)
    away = plus(kept, swap(sent, 16, 2, role)).astype(jnp.bfloat16)
    kept, sent = halves(near)
    near = plus(kept, swap(sent, 16, 2, role)).astype(jnp.bfloat16)
    return near, away


def sum_z(near, away, role):
    second, third = [swap(h, 16, f, role) for h, f in zip(halves(away), (8, 12))]
    kept, sent = halves(near)
    return plus(kept, swap(sent, 16, 4, role), second, third)


def renew(weights, grads, axis_number, rate):
    scale = jnp.sqrt(jnp.mean(grads * grads, axis=axis_number, keepdims=True) + EPSILON)
    return (weights.astype(jnp.float32) - rate * grads / scale).astype(jnp.bfloat16)


def wide(a, b, contract):
    return lax.dot_general(a, b, (contract, ((), ())), preferred_element_type=jnp.float32)


def nn(a, b):
    return wide(a, b, ((1,), (0,)))


def nt(a, b):
    return wide(a, b, ((1,), (1,)))


def prep_kernel(
    place, lengths, rows_ref, cot_ref, ids_ref, gates_ref, dec_ids_ref, dec_gates_ref,
    out_ref, base_ref, *, experts, longest,
):
    width = rows_ref.shape[1]
    row_count = rows_ref.shape[0]
    learner = place[1] == 0
    places = place[0] * row_count + lax.broadcasted_iota(jnp.int32, (1, row_count), 1)
    start = jnp.int32(0)
    seq_len = jnp.zeros((1, row_count), jnp.int32)
    for i in range(lengths.shape[0]):
        end = start + lengths[i]
        seq_len = jnp.where((places >= start) & (places < end), lengths[i], seq_len)
        start = end
    weight = 2.0 * longest / (seq_len.astype(jnp.float32) + longest)
    names = lax.broadcasted_iota(jnp.int32, (experts, row_count), 0)

    def table(ids, gates):
        total = jnp.zeros((experts, row_count), jnp.float32)
        for k in range(ids.shape[0]):
            total = total + jnp.where(names == ids[k : k + 1], gates[k : k + 1], 0.0)
        return total

    train = table(ids_ref[...], gates_ref[...]) * weight
    stale = table(dec_ids_ref[0], dec_gates_ref[0])
    first = jnp.where(learner, train, stale)
    fresh = table(dec_ids_ref[1], dec_gates_ref[1])
    parts = []
    for one in (first, fresh):
        upper = one.astype(jnp.bfloat16).astype(jnp.float32)
        parts += [upper, one - upper]
    spare = out_ref.shape[1] - width
    if spare > 4 * experts:
        parts.append(jnp.zeros((spare - 4 * experts, row_count), jnp.float32))
    stacked = jnp.concatenate(parts, axis=0)
    weights = jnp.broadcast_to(weight, (128, row_count))
    square = jnp.concatenate([stacked, weights], axis=0)
    square = jnp.concatenate(
        [square, jnp.zeros((square.shape[0], 128 - row_count), jnp.float32)], axis=1
    )
    for i in range(spare // 128):
        turned = square[128 * i : 128 * (i + 1)].T
        out_ref[:, width + 128 * i : width + 128 * (i + 1)] = turned[:row_count].astype(
            jnp.bfloat16
        )
    column = square[spare:].T[:row_count, 0:1]
    out_ref[:, :width] = rows_ref[...]
    base_ref[...] = jnp.where(
        learner, column * cot_ref[...].astype(jnp.float32), rows_ref[...].astype(jnp.float32)
    )


def prep_call(place, lengths, rows, cot, ids, gates, dec_ids, dec_gates, experts, longest):
    row_count, width = rows.shape
    spare = -(-4 * experts // 128) * 128
    scalars = pl.BlockSpec(memory_space=pltpu.SMEM)
    whole = pl.BlockSpec(memory_space=pltpu.VMEM)
    return pl.pallas_call(
        functools.partial(prep_kernel, experts=experts, longest=longest),
        in_specs=[scalars, scalars] + [whole] * 6,
        out_specs=[whole, whole],
        out_shape=[
            jax.ShapeDtypeStruct((row_count, width + spare), jnp.bfloat16),
            jax.ShapeDtypeStruct((row_count, width), jnp.float32),
        ],
        name="prep",
    )(place, lengths, rows, cot, ids.T, gates.T, jnp.swapaxes(dec_ids, 1, 2), jnp.swapaxes(dec_gates, 1, 2))


def pick_gates(table, column, step):
    places = lax.broadcasted_iota(jnp.int32, table.shape, 1)
    taken = (places == column) | (places == column + step)
    return jnp.sum(jnp.where(taken, table.astype(jnp.float32), 0.0), axis=1, keepdims=True)


def parts_of(array, count):
    parts = []
    for _ in range(count):
        parts.append(array.astype(jnp.bfloat16))
        array = array - parts[-1].astype(jnp.float32)
    return parts


def fine(array, other, count):
    total = None
    for part in parts_of(array, count):
        product = nn(part, other)
        total = product if total is None else total + product
    return total


def ffn_kernel(place, *refs, count, experts, changed):
    rows_refs, table_refs = refs[:count], refs[count : 2 * count]
    gu_ref, dn_ref = refs[2 * count : 2 * count + 2]
    refs = refs[2 * count + 2 :]
    if changed:
        turned_ref, pulls_ref, sent_ref, hidden_turned_ref, rates_ref = refs[:5]
        refs = refs[5:]
    out_refs, rows = refs[:count], refs[count]
    part, width = rows_refs[0].shape
    for i in range(count):
        rows[part * i : part * (i + 1), :] = rows_refs[i][...]
    active = nn(rows[...], gu_ref[0])
    upward = nn(rows[...], gu_ref[1])
    if changed:
        alike = nn(rows[...], turned_ref[...])
        active = active - fine(alike, sent_ref[0], 2) * rates_ref[0:1]
        upward = upward - fine(alike, sent_ref[1], 2) * rates_ref[1:2]
    swish = active * jax.nn.sigmoid(active)
    hidden = (swish * upward).astype(jnp.bfloat16)
    if changed:
        scaled = hidden.astype(jnp.float32) * rates_ref[2:3]
        mixed = parts_of(fine(scaled, hidden_turned_ref[...], 2), 2)
    gates = [pick_gates(table_refs[i][...], place[0], experts) for i in range(count)]
    tile = 1024
    for lower in range(0, width, tile):
        cut = slice(lower, lower + tile)
        out = nn(hidden, dn_ref[:, cut])
        if changed:
            for one in mixed:
                out = out - nn(one, pulls_ref[:, cut])
        for i in range(count):
            here = out[part * i : part * (i + 1)]
            out_refs[i][:, cut] = (gates[i] * here).astype(jnp.bfloat16)


def ffn_call(place, pieces, tables, planes, weights_dn, experts, change=()):
    count = len(pieces)
    part = pieces[0].shape[0]
    hidden_count, width = weights_dn.shape
    row_count = part * count
    whole = pl.BlockSpec(memory_space=pltpu.VMEM)
    return pl.pallas_call(
        functools.partial(ffn_kernel, count=count, experts=experts, changed=bool(change)),
        in_specs=[pl.BlockSpec(memory_space=pltpu.SMEM)] + [whole] * (2 * count + 2 + len(change)),
        out_specs=[whole] * count,
        scratch_shapes=[pltpu.VMEM((row_count, width), jnp.bfloat16)],
        out_shape=[jax.ShapeDtypeStruct((part, width), jnp.bfloat16)] * count,
        compiler_params=pltpu.CompilerParams(vmem_limit_bytes=44 << 20),
        cost_estimate=pl.CostEstimate(
            flops=6 * row_count * hidden_count * width if change else 1,
            bytes_accessed=4 * row_count * width if change else 1,
            transcendentals=row_count * hidden_count if change else 1,
        ),
        name="ffn_changed" if change else "ffn",
    )(place, *pieces, *tables, planes, weights_dn, *change)


def learn_kernel(place, *refs, count, experts, rates):
    rows_refs, table_refs = refs[:count], refs[count : 2 * count]
    cot_refs = refs[2 * count : 3 * count]
    gu_ref, dn_ref = refs[3 * count : 3 * count + 2]
    dx_refs = refs[3 * count + 2 : 4 * count + 2]
    turned, pulls, sent, hidden_turned_ref, rates_ref = refs[4 * count + 2 : 4 * count + 7]
    rows, pulls_turned = refs[4 * count + 7 :]
    part = rows_refs[0].shape[0]
    hidden_count, width = dn_ref.shape
    tile = 1024
    cuts = [slice(lower, lower + tile) for lower in range(0, width, tile)]
    for i in range(count):
        here = slice(part * i, part * (i + 1))
        gates = pick_gates(table_refs[i][...], place[0], experts)
        rows[here, :] = rows_refs[i][...]
        pulls[here, :] = (gates * cot_refs[i][...].astype(jnp.float32)).astype(jnp.bfloat16)
    for cut in cuts:
        turned[cut, :] = rows[:, cut].T
        pulls_turned[cut, :] = pulls[:, cut].T

    active = nn(rows[...], gu_ref[0])
    upward = nn(rows[...], gu_ref[1])
    back = nn(dn_ref[...], pulls_turned[...]).T
    sigma = jax.nn.sigmoid(active)
    swish = active * sigma
    hidden = (swish * upward).astype(jnp.bfloat16)
    d_active = (back * upward * sigma * (1.0 + active * (1.0 - sigma))).astype(jnp.bfloat16)
    d_upward = (back * swish).astype(jnp.bfloat16)
    sent[0] = d_active
    sent[1] = d_upward
    hidden_turned_ref[...] = hidden.T
    d_active_turned = d_active.T
    d_upward_turned = d_upward.T

    for cut in cuts:
        done = nn(gu_ref[0, cut, :], d_active_turned) + nn(gu_ref[1, cut, :], d_upward_turned)
        done = done.T.astype(jnp.bfloat16)
        for i in range(count):
            dx_refs[i][:, cut] = done[part * i : part * (i + 1)]

    def mean_square(alike, factor):
        wide_factor = factor.astype(jnp.float32)
        squares = jnp.sum(wide_factor * fine(alike, factor, 3), axis=0, keepdims=True)
        return jnp.maximum(squares, 0.0) / width

    alike = nn(rows[...], turned[...])
    rates_ref[0:1] = rates[0] / jnp.sqrt(mean_square(alike, d_active) + EPSILON)
    rates_ref[1:2] = rates[0] / jnp.sqrt(mean_square(alike, d_upward) + EPSILON)
    alike = nn(pulls[...], pulls_turned[...])
    rates_ref[2:3] = rates[1] / jnp.sqrt(mean_square(alike, hidden) + EPSILON)


def learn_call(place, pieces, tables, cots, planes, weights_dn, experts, rates):
    count = len(pieces)
    part = pieces[0].shape[0]
    hidden_count, width = weights_dn.shape
    row_count = part * count
    whole = pl.BlockSpec(memory_space=pltpu.VMEM)
    out_shape = [jax.ShapeDtypeStruct((part, width), jnp.bfloat16)] * count + [
        jax.ShapeDtypeStruct((width, row_count), jnp.bfloat16),
        jax.ShapeDtypeStruct((row_count, width), jnp.bfloat16),
        jax.ShapeDtypeStruct((2, row_count, hidden_count), jnp.bfloat16),
        jax.ShapeDtypeStruct((hidden_count, row_count), jnp.bfloat16),
        jax.ShapeDtypeStruct((8, hidden_count), jnp.float32),
    ]
    return pl.pallas_call(
        functools.partial(learn_kernel, count=count, experts=experts, rates=rates),
        in_specs=[pl.BlockSpec(memory_space=pltpu.SMEM)] + [whole] * (3 * count + 2),
        out_specs=[whole] * len(out_shape),
        scratch_shapes=[
            pltpu.VMEM((row_count, width), jnp.bfloat16),
            pltpu.VMEM((width, row_count), jnp.bfloat16),
        ],
        out_shape=out_shape,
        compiler_params=pltpu.CompilerParams(vmem_limit_bytes=44 << 20),
        cost_estimate=pl.CostEstimate(
            flops=12 * row_count * hidden_count * width,
            bytes_accessed=8 * row_count * width,
            transcendentals=row_count * hidden_count,
        ),
        name="learn",
    )(place, *pieces, *tables, *cots, planes, weights_dn)


def unset(like):
    return pl.pallas_call(
        lambda out_ref: None,
        out_shape=jax.ShapeDtypeStruct(like.shape, like.dtype),
        out_specs=pl.BlockSpec(memory_space=pl.ANY),
        name="unset",
    )()


def ffn_plain(place, pieces, tables, planes, weights_dn, experts):
    width = weights_dn.shape[1]
    rows = pieces[0][:, :width]
    gates = pick_gates(tables[0][:, width:], place[0], experts)
    active = nn(rows, planes[0])
    upward = nn(rows, planes[1])
    hidden = (active * jax.nn.sigmoid(active) * upward).astype(jnp.bfloat16)
    return [(gates * nn(hidden, weights_dn)).astype(jnp.bfloat16)]


def learn_plain(place, pieces, tables, cots, planes, weights_dn, experts, rates):
    width = weights_dn.shape[1]
    rows = pieces[0][:, :width]
    gates = pick_gates(tables[0][:, width:], place[0], experts)
    pulls = (gates * cots.astype(jnp.float32)).astype(jnp.bfloat16)
    active = nn(rows, planes[0])
    upward = nn(rows, planes[1])
    back = nt(pulls, weights_dn)
    sigma = jax.nn.sigmoid(active)
    swish = active * sigma
    hidden = (swish * upward).astype(jnp.bfloat16)
    d_active = (back * upward * sigma * (1.0 + active * (1.0 - sigma))).astype(jnp.bfloat16)
    d_upward = (back * swish).astype(jnp.bfloat16)
    dx_part = (nt(d_active, planes[0]) + nt(d_upward, planes[1])).astype(jnp.bfloat16)
    new_planes = jnp.stack(
        [
            renew(planes[0], wide(rows, d_active, ((0,), (0,))), 0, rates[0]),
            renew(planes[1], wide(rows, d_upward, ((0,), (0,))), 0, rates[0]),
        ],
        axis=0,
    )
    new_dn = renew(weights_dn, wide(hidden, pulls, ((0,), (0,))), 1, rates[1])
    return [dx_part, new_planes, new_dn]


def per_device(
    rows_in,
    cotangent,
    lengths,
    train_experts,
    train_gates,
    decode_experts,
    decode_gates,
    gate_up,
    down,
):
    ep_count = lax.axis_size("ep")
    dp_count = lax.axis_size("dp")
    device_count = ep_count * dp_count
    row_count, model_width = cotangent.shape
    role = lax.axis_index("grp").astype(jnp.int32)
    is_learner = role == 0
    mine = lax.axis_index("ep").astype(jnp.int32)
    own_dn = down[0, 0]
    planes = jnp.transpose(gate_up[0, 0], (1, 0, 2))
    total_rows = row_count * device_count
    longest = 2 * total_rows // lengths.shape[0]
    rates = (0.5 / model_width**0.5, 0.5 / (own_dn.shape[0] * dp_count) ** 0.5)
    small = device_count == 16 and dp_count == 1
    first_place = mine.reshape(1)
    fresh_place = first_place + 2 * ep_count

    where = jnp.stack([mine * dp_count + lax.axis_index("dp").astype(jnp.int32), role])
    block, base = prep_call(
        where, lengths, rows_in[0], cotangent, train_experts, train_gates, decode_experts,
        decode_gates, ep_count, longest,
    )
    if small:
        near, away = send_z(block, (0, 1))
        near, planes, cotangent = tied(near, planes, cotangent)
        cot_near, cot_away = send_z(cotangent, (0,))
        near, away = send_y(near, away, (0, 1))
        every = send_core(near, away, (0, 1))

        def blank(*shape, of=jnp.bfloat16):
            return unset(jax.ShapeDtypeStruct(shape, of))

        rows = [piece[:, :model_width] for piece in every]
        gates = [piece[:, model_width:] for piece in every]
        part = lax.cond(
            is_learner,
            lambda r, t, g, d: [blank(*one.shape) for one in r],
            lambda r, t, g, d: list(ffn_call(first_place, r, t, g, d, ep_count)),
            rows,
            gates,
            planes,
            own_dn,
        )
        near, away = sum_core(part, (1,))
        near, away, cot_near, cot_away = tied(near, away, cot_near, cot_away)
        cot_near, cot_away = send_y(cot_near, cot_away, (0,))
        near, away = sum_y(near, away, (1,))
        near, away, cot_near, cot_away = tied(near, away, cot_near, cot_away)
        cots = send_core(cot_near, cot_away, (0,))
        current = (base + sum_z(near, away, (1,))).astype(jnp.bfloat16)
        hopped = across(current, 1, 0)
        hidden_count = own_dn.shape[0]
        learned = lax.cond(
            is_learner,
            lambda r, t, c, g, d: list(learn_call(first_place, r, t, c, g, d, ep_count, rates)),
            lambda r, t, c, g, d: [blank(*one.shape) for one in r]
            + [
                blank(model_width, total_rows),
                blank(total_rows, model_width),
                blank(2, total_rows, hidden_count),
                blank(hidden_count, total_rows),
                blank(8, hidden_count, of=jnp.float32),
            ],
            rows,
            gates,
            cots,
            planes,
            own_dn,
        )
        near, away = sum_core(learned[:4], (0,))
        near, away = sum_y(near, away, (0,))
        near, away, hopped = tied(near, away, hopped)
        dx_sum = sum_z(near, away, (0,))
        near, away = send_z(hopped, (0,))
        near, away = send_y(near, away, (0,))
        arrived = send_core(near, away, (0,))
        fresh_part = lax.cond(
            is_learner,
            lambda r, t, g, d, *c: list(ffn_call(fresh_place, r, t, g, d, ep_count, c)),
            lambda r, t, g, d, *c: [blank(*one.shape) for one in r],
            arrived,
            gates,
            planes,
            own_dn,
            *learned[4:],
        )
        near, away = sum_core(fresh_part, (0,))
        near, away, dx_sum = tied(near, away, dx_sum)
        near, away = sum_y(near, away, (0,))
        fresh_sum = sum_z(near, away, (0,))
    else:
        every = [gather(block, device_count, (0, 1))]
        cots = gather(cotangent, device_count, (0,))

        def learn(every, cots, planes, own_dn):
            out = list(learn_plain(first_place, every, every, cots, planes, own_dn, ep_count, rates))
            return ([unset(out[0])], out[0], out[1], out[2])

        def decode(every, cots, planes, own_dn):
            out = list(ffn_plain(first_place, every, every, planes, own_dn, ep_count))
            return (out, unset(cots), unset(planes), unset(own_dn))

        part, dx_part, new_planes, new_dn = lax.cond(
            is_learner, learn, decode, every, cots, planes, own_dn
        )
        stale_sum = scatter_sum(part[0], device_count, (1,))
        current = (base + stale_sum).astype(jnp.bfloat16)
        dx_sum = scatter_sum(dx_part, device_count, (0,))
        arrived = [gather(across(current, 1, 0), device_count, (0,))]
        fresh_part = lax.cond(
            is_learner,
            lambda r, e, g, d: list(ffn_plain(fresh_place, r, e, g, d, ep_count)),
            lambda r, e, g, d: [unset(o) for o in r],
            arrived,
            every,
            new_planes,
            new_dn,
        )
        fresh_sum = scatter_sum(fresh_part[0], device_count, (0,))
    moved = across(fresh_sum.astype(jnp.bfloat16), 0, 1).astype(jnp.float32)
    final_rows = jnp.where(is_learner, base + dx_sum, current.astype(jnp.float32) + moved)
    return final_rows.astype(jnp.bfloat16)[None]


def solution(mesh):
    placed = (
        P("grp", ("ep", "dp"), None),
        P(("ep", "dp"), None),
        P(),
        P(("ep", "dp"), None),
        P(("ep", "dp"), None),
        P(None, ("ep", "dp"), None),
        P(None, ("ep", "dp"), None),
        P("grp", "ep", None, None, "dp"),
        P("grp", "ep", "dp", None),
    )
    return jax.shard_map(
        per_device,
        mesh=mesh,
        in_specs=placed,
        out_specs=P("grp", ("ep", "dp"), None),
        check_vma=False,
    )
```

```python
import functools

import jax
import jax.numpy as jnp
from jax import lax
from jax.experimental import pallas as pl
from jax.experimental.pallas import tpu as pltpu
from jax.sharding import PartitionSpec as P

EPSILON = 1e-06
AXES = ("ep", "dp")


def across(block, source, target):
    return lax.ppermute(block, "grp", [(source, target)])


def stages(device_count):
    sizes = []
    rest = device_count
    while rest > 1:
        size = 2 if len(sizes) < 2 or rest % 4 else 4
        sizes.append(size)
        rest //= size
    strides = []
    stride = device_count
    for size in sizes[::-1]:
        stride //= size
        strides.append((stride, size))
    return strides


def swap(block, device_count, flip, role):
    pairs = [
        (part * device_count + i, part * device_count + (i ^ flip))
        for part in role
        for i in range(device_count)
    ]
    return lax.ppermute(block, ("grp",) + AXES, pairs)


def tied(*values):
    return lax.optimization_barrier(values)


def gather(block, device_count, role):
    for stride, size in stages(device_count):
        got = [swap(block, device_count, turn * stride, role) for turn in range(1, size)]
        block = jnp.concatenate([block] + got, axis=0)
    return block


def send_z(block, role):
    far = [swap(block, 16, flip, role) for flip in (4, 8, 12)]
    return jnp.concatenate([block, far[0]], axis=0), jnp.concatenate(far[1:], axis=0)


def send_y(near, away, role):
    return [jnp.concatenate([part, swap(part, 16, 2, role)], axis=0) for part in (near, away)]


def send_core(near, away, role):
    return [near, swap(near, 16, 1, role), away, swap(away, 16, 1, role)]


def plus(kept, *sent):
    total = kept.astype(jnp.float32)
    for one in sent:
        total = total + one.astype(jnp.float32)
    return total


def halves(array):
    return jnp.split(array, 2, axis=0)


def scatter_sum(part, device_count, role):
    for stride, size in stages(device_count)[::-1]:
        cuts = jnp.split(part, size, axis=0)
        got = [swap(cuts[turn], device_count, turn * stride, role) for turn in range(1, size)]
        total = plus(cuts[0], *got)
        part = total.astype(jnp.bfloat16)
    return total


def sum_core(pieces, role):
    away = plus(pieces[2], swap(pieces[3], 16, 1, role)).astype(jnp.bfloat16)
    near = plus(pieces[0], swap(pieces[1], 16, 1, role)).astype(jnp.bfloat16)
    return near, away


def sum_y(near, away, role):
    kept, sent = halves(away)
    away = plus(kept, swap(sent, 16, 2, role)).astype(jnp.bfloat16)
    kept, sent = halves(near)
    near = plus(kept, swap(sent, 16, 2, role)).astype(jnp.bfloat16)
    return near, away


def sum_z(near, away, role):
    second, third = [swap(h, 16, f, role) for h, f in zip(halves(away), (8, 12))]
    kept, sent = halves(near)
    return plus(kept, swap(sent, 16, 4, role), second, third)


def renew(weights, grads, axis_number, rate):
    scale = jnp.sqrt(jnp.mean(grads * grads, axis=axis_number, keepdims=True) + EPSILON)
    return (weights.astype(jnp.float32) - rate * grads / scale).astype(jnp.bfloat16)


def wide(a, b, contract):
    return lax.dot_general(a, b, (contract, ((), ())), preferred_element_type=jnp.float32)


def nn(a, b):
    return wide(a, b, ((1,), (0,)))


def nt(a, b):
    return wide(a, b, ((1,), (1,)))


def prep_kernel(
    place, lengths, rows_ref, cot_ref, ids_ref, gates_ref, dec_ids_ref, dec_gates_ref,
    out_ref, base_ref, *, experts, longest,
):
    width = rows_ref.shape[1]
    row_count = rows_ref.shape[0]
    learner = place[1] == 0
    places = place[0] * row_count + lax.broadcasted_iota(jnp.int32, (1, row_count), 1)
    start = jnp.int32(0)
    seq_len = jnp.zeros((1, row_count), jnp.int32)
    for i in range(lengths.shape[0]):
        end = start + lengths[i]
        seq_len = jnp.where((places >= start) & (places < end), lengths[i], seq_len)
        start = end
    weight = 2.0 * longest / (seq_len.astype(jnp.float32) + longest)
    names = lax.broadcasted_iota(jnp.int32, (experts, row_count), 0)

    def table(ids, gates):
        total = jnp.zeros((experts, row_count), jnp.float32)
        for k in range(ids.shape[0]):
            total = total + jnp.where(names == ids[k : k + 1], gates[k : k + 1], 0.0)
        return total

    train = table(ids_ref[...], gates_ref[...]) * weight
    stale = table(dec_ids_ref[0], dec_gates_ref[0])
    first = jnp.where(learner, train, stale)
    fresh = table(dec_ids_ref[1], dec_gates_ref[1])
    parts = []
    for one in (first, fresh):
        upper = one.astype(jnp.bfloat16).astype(jnp.float32)
        parts += [upper, one - upper]
    spare = out_ref.shape[1] - width
    if spare > 4 * experts:
        parts.append(jnp.zeros((spare - 4 * experts, row_count), jnp.float32))
    stacked = jnp.concatenate(parts, axis=0)
    weights = jnp.broadcast_to(weight, (128, row_count))
    square = jnp.concatenate([stacked, weights], axis=0)
    square = jnp.concatenate(
        [square, jnp.zeros((square.shape[0], 128 - row_count), jnp.float32)], axis=1
    )
    for i in range(spare // 128):
        turned = square[128 * i : 128 * (i + 1)].T
        out_ref[:, width + 128 * i : width + 128 * (i + 1)] = turned[:row_count].astype(
            jnp.bfloat16
        )
    column = square[spare:].T[:row_count, 0:1]
    out_ref[:, :width] = rows_ref[...]
    base_ref[...] = jnp.where(
        learner, column * cot_ref[...].astype(jnp.float32), rows_ref[...].astype(jnp.float32)
    )


def prep_call(place, lengths, rows, cot, ids, gates, dec_ids, dec_gates, experts, longest):
    row_count, width = rows.shape
    spare = -(-4 * experts // 128) * 128
    scalars = pl.BlockSpec(memory_space=pltpu.SMEM)
    whole = pl.BlockSpec(memory_space=pltpu.VMEM)
    return pl.pallas_call(
        functools.partial(prep_kernel, experts=experts, longest=longest),
        in_specs=[scalars, scalars] + [whole] * 6,
        out_specs=[whole, whole],
        out_shape=[
            jax.ShapeDtypeStruct((row_count, width + spare), jnp.bfloat16),
            jax.ShapeDtypeStruct((row_count, width), jnp.float32),
        ],
        name="prep",
    )(place, lengths, rows, cot, ids.T, gates.T, jnp.swapaxes(dec_ids, 1, 2), jnp.swapaxes(dec_gates, 1, 2))


def pick_gates(table, column, step):
    places = lax.broadcasted_iota(jnp.int32, table.shape, 1)
    taken = (places == column) | (places == column + step)
    return jnp.sum(jnp.where(taken, table.astype(jnp.float32), 0.0), axis=1, keepdims=True)


def parts_of(array, count):
    parts = []
    for _ in range(count):
        parts.append(array.astype(jnp.bfloat16))
        array = array - parts[-1].astype(jnp.float32)
    return parts


def fine(array, other, count):
    total = None
    for part in parts_of(array, count):
        product = nn(part, other)
        total = product if total is None else total + product
    return total


TILE = 1024


def tiles_of(width):
    return [slice(lower, lower + TILE) for lower in range(0, width, TILE)]


def reads(pairs, sems):
    return [pltpu.make_async_copy(src, dst, sems.at[i]) for i, (src, dst) in enumerate(pairs)]


def row_reads(refs, count, width, rows, table):
    part = rows.shape[0] // count
    spare = table.shape[1]
    here = [pl.ds(part * i, part) for i in range(count)]
    wide_pairs = [(refs[i].at[:, pl.ds(0, width)], rows.at[here[i]]) for i in range(count)]
    thin_pairs = [
        (refs[count + i].at[:, pl.ds(width, spare)], table.at[here[i]]) for i in range(count)
    ]
    return wide_pairs + thin_pairs


def weight_reads(gu_ref, dn_ref, gu, dn):
    cuts = [pl.ds(lower, TILE) for lower in range(0, dn.shape[1], TILE)]
    return [(gu_ref.at[:, cut], gu.at[:, cut]) for cut in cuts], [
        (dn_ref.at[:, cut], dn.at[:, cut]) for cut in cuts
    ]


def added(total, product):
    return product if total is None else total + product


def ffn_kernel(place, *refs, count, experts, changed):
    gu_ref, dn_ref = refs[2 * count : 2 * count + 2]
    extra = 5 if changed else 0
    extra_refs = refs[2 * count + 2 : 2 * count + 2 + extra]
    refs_left = refs[2 * count + 2 + extra :]
    out_refs = refs_left[:count]
    rows, table, gu, dn = refs_left[count : count + 4]
    extras = refs_left[count + 4 : count + 4 + extra]
    sems = refs_left[count + 4 + extra]
    width = dn.shape[1]
    cuts = tiles_of(width)
    first = row_reads(refs, count, width, rows, table)
    gu_pairs, dn_pairs = weight_reads(gu_ref, dn_ref, gu, dn)
    more = list(zip(extra_refs, extras))
    copies = reads(first + more[:1] + gu_pairs + more[1:] + dn_pairs, sems)
    for copy in copies:
        copy.start()
    done = len(first) + len(more[:1])
    for copy in copies[:done]:
        copy.wait()
    active = upward = alike = None
    for cut in cuts:
        copies[done].wait()
        done += 1
        active = added(active, nn(rows[:, cut], gu[0, cut]))
        upward = added(upward, nn(rows[:, cut], gu[1, cut]))
        if changed:
            alike = added(alike, nn(rows[:, cut], extras[0][cut]))
    for copy in copies[done : done + len(more[1:])]:
        copy.wait()
    done += len(more[1:])
    if changed:
        turned, sent, hidden_turned, rates, pulls = extras
        active = active - fine(alike, sent[0], 2) * rates[0:1]
        upward = upward - fine(alike, sent[1], 2) * rates[1:2]
    hidden = (active * jax.nn.sigmoid(active) * upward).astype(jnp.bfloat16)
    if changed:
        scaled = hidden.astype(jnp.float32) * rates[2:3]
        mixed = parts_of(fine(scaled, hidden_turned[...], 2), 2)
    gates = pick_gates(table[...], place[0], experts)
    part = rows.shape[0] // count
    for cut in cuts:
        copies[done].wait()
        done += 1
        out = nn(hidden, dn[:, cut])
        if changed:
            for one in mixed:
                out = out - nn(one, pulls[:, cut])
        out = (gates * out).astype(jnp.bfloat16)
        for i in range(count):
            out_refs[i][:, cut] = out[part * i : part * (i + 1)]


def ffn_call(place, pieces, tables, planes, weights_dn, experts, change=()):
    count = len(pieces)
    part = pieces[0].shape[0]
    hidden_count, width = weights_dn.shape
    row_count = part * count
    anywhere = pl.BlockSpec(memory_space=pl.ANY)
    whole = pl.BlockSpec(memory_space=pltpu.VMEM)
    return pl.pallas_call(
        functools.partial(ffn_kernel, count=count, experts=experts, changed=bool(change)),
        in_specs=[pl.BlockSpec(memory_space=pltpu.SMEM)]
        + [anywhere] * (2 * count + 2 + len(change)),
        out_specs=[whole] * count,
        scratch_shapes=[
            pltpu.VMEM((row_count, width), jnp.bfloat16),
            pltpu.VMEM((row_count, tables[0].shape[1] - width), jnp.bfloat16),
            pltpu.VMEM(planes.shape, jnp.bfloat16),
            pltpu.VMEM(weights_dn.shape, jnp.bfloat16),
        ]
        + [pltpu.VMEM(one.shape, one.dtype) for one in change]
        + [pltpu.SemaphoreType.DMA((2 * count + len(change) + 2 * (width // TILE),))],
        out_shape=[jax.ShapeDtypeStruct((part, width), jnp.bfloat16)] * count,
        compiler_params=pltpu.CompilerParams(vmem_limit_bytes=44 << 20),
        cost_estimate=pl.CostEstimate(
            flops=6 * row_count * hidden_count * width,
            bytes_accessed=6 * hidden_count * width,
            transcendentals=row_count * hidden_count,
        ),
        name="ffn_changed" if change else "ffn",
    )(place, *pieces, *tables, planes, weights_dn, *change)


def learn_kernel(place, *refs, count, experts, rates):
    cot_refs = refs[2 * count : 3 * count]
    gu_ref, dn_ref = refs[3 * count : 3 * count + 2]
    dx_ref, turned, sent, hidden_turned_ref, rates_ref, pulls = refs[3 * count + 2 : 3 * count + 8]
    rows, table, cots, pulls_turned, gu, dn, sems = refs[3 * count + 8 :]
    hidden_count, width = dn.shape
    part = rows.shape[0] // count
    cuts = tiles_of(width)
    first = row_reads(refs, count, width, rows, table)
    first += [(cot_refs[i], cots.at[pl.ds(part * i, part)]) for i in range(count)]
    gu_pairs, dn_pairs = weight_reads(gu_ref, dn_ref, gu, dn)
    both = [pair for pairs in zip(gu_pairs, dn_pairs) for pair in pairs]
    copies = reads(first + both, sems)
    for copy in copies:
        copy.start()
    done = len(first)
    for copy in copies[:done]:
        copy.wait()
    gates = pick_gates(table[...], place[0], experts)
    for cut in cuts:
        pulls[:, cut] = (gates * cots[:, cut].astype(jnp.float32)).astype(jnp.bfloat16)
        turned[cut, :] = rows[:, cut].T
        pulls_turned[cut, :] = pulls[:, cut].T
    alike_rows = nn(rows[...], turned[...])
    alike_pulls = nn(pulls[...], pulls_turned[...])
    active = upward = back = None
    for cut in cuts:
        copies[done].wait()
        copies[done + 1].wait()
        done += 2
        active = added(active, nn(rows[:, cut], gu[0, cut]))
        upward = added(upward, nn(rows[:, cut], gu[1, cut]))
        back = added(back, nn(dn[:, cut], pulls_turned[cut]))
    back = back.T
    sigma = jax.nn.sigmoid(active)
    swish = active * sigma
    hidden = (swish * upward).astype(jnp.bfloat16)
    d_active = (back * upward * sigma * (1.0 + active * (1.0 - sigma))).astype(jnp.bfloat16)
    d_upward = (back * swish).astype(jnp.bfloat16)
    sent[0] = d_active
    sent[1] = d_upward
    hidden_turned_ref[...] = hidden.T
    d_active_turned = d_active.T
    d_upward_turned = d_upward.T

    for cut in cuts:
        out = nn(gu[0, cut], d_active_turned) + nn(gu[1, cut], d_upward_turned)
        dx_ref[:, cut] = out.T.astype(jnp.bfloat16)

    def mean_square(alike, factor):
        wide_factor = factor.astype(jnp.float32)
        squares = jnp.sum(wide_factor * fine(alike, factor, 3), axis=0, keepdims=True)
        return jnp.maximum(squares, 0.0) / width

    rates_ref[0:1] = rates[0] / jnp.sqrt(mean_square(alike_rows, d_active) + EPSILON)
    rates_ref[1:2] = rates[0] / jnp.sqrt(mean_square(alike_rows, d_upward) + EPSILON)
    rates_ref[2:3] = rates[1] / jnp.sqrt(mean_square(alike_pulls, hidden) + EPSILON)
    rates_ref[3:8] = jnp.zeros((5, hidden_count), jnp.float32)


def learn_shapes(row_count, hidden_count, width):
    return [
        jax.ShapeDtypeStruct((row_count, width), jnp.bfloat16),
        jax.ShapeDtypeStruct((width, row_count), jnp.bfloat16),
        jax.ShapeDtypeStruct((2, row_count, hidden_count), jnp.bfloat16),
        jax.ShapeDtypeStruct((hidden_count, row_count), jnp.bfloat16),
        jax.ShapeDtypeStruct((8, hidden_count), jnp.float32),
        jax.ShapeDtypeStruct((row_count, width), jnp.bfloat16),
    ]


def learn_call(place, pieces, tables, cots, planes, weights_dn, experts, rates):
    count = len(pieces)
    hidden_count, width = weights_dn.shape
    row_count = pieces[0].shape[0] * count
    anywhere = pl.BlockSpec(memory_space=pl.ANY)
    whole = pl.BlockSpec(memory_space=pltpu.VMEM)
    out_shape = learn_shapes(row_count, hidden_count, width)
    return pl.pallas_call(
        functools.partial(learn_kernel, count=count, experts=experts, rates=rates),
        in_specs=[pl.BlockSpec(memory_space=pltpu.SMEM)] + [anywhere] * (3 * count + 2),
        out_specs=[whole] * len(out_shape),
        scratch_shapes=[
            pltpu.VMEM((row_count, width), jnp.bfloat16),
            pltpu.VMEM((row_count, tables[0].shape[1] - width), jnp.bfloat16),
            pltpu.VMEM((row_count, width), jnp.bfloat16),
            pltpu.VMEM((width, row_count), jnp.bfloat16),
            pltpu.VMEM(planes.shape, jnp.bfloat16),
            pltpu.VMEM(weights_dn.shape, jnp.bfloat16),
            pltpu.SemaphoreType.DMA((3 * count + 2 * (width // TILE),)),
        ],
        out_shape=out_shape,
        compiler_params=pltpu.CompilerParams(vmem_limit_bytes=48 << 20),
        cost_estimate=pl.CostEstimate(
            flops=12 * row_count * hidden_count * width,
            bytes_accessed=6 * hidden_count * width,
            transcendentals=row_count * hidden_count,
        ),
        name="learn",
    )(place, *pieces, *tables, *cots, planes, weights_dn)


def unset(like):
    return pl.pallas_call(
        lambda out_ref: None,
        out_shape=jax.ShapeDtypeStruct(like.shape, like.dtype),
        out_specs=pl.BlockSpec(memory_space=pl.ANY),
        name="unset",
    )()


def ffn_plain(place, pieces, tables, planes, weights_dn, experts):
    width = weights_dn.shape[1]
    rows = pieces[0][:, :width]
    gates = pick_gates(tables[0][:, width:], place[0], experts)
    active = nn(rows, planes[0])
    upward = nn(rows, planes[1])
    hidden = (active * jax.nn.sigmoid(active) * upward).astype(jnp.bfloat16)
    return [(gates * nn(hidden, weights_dn)).astype(jnp.bfloat16)]


def learn_plain(place, pieces, tables, cots, planes, weights_dn, experts, rates):
    width = weights_dn.shape[1]
    rows = pieces[0][:, :width]
    gates = pick_gates(tables[0][:, width:], place[0], experts)
    pulls = (gates * cots.astype(jnp.float32)).astype(jnp.bfloat16)
    active = nn(rows, planes[0])
    upward = nn(rows, planes[1])
    back = nt(pulls, weights_dn)
    sigma = jax.nn.sigmoid(active)
    swish = active * sigma
    hidden = (swish * upward).astype(jnp.bfloat16)
    d_active = (back * upward * sigma * (1.0 + active * (1.0 - sigma))).astype(jnp.bfloat16)
    d_upward = (back * swish).astype(jnp.bfloat16)
    dx_part = (nt(d_active, planes[0]) + nt(d_upward, planes[1])).astype(jnp.bfloat16)
    new_planes = jnp.stack(
        [
            renew(planes[0], wide(rows, d_active, ((0,), (0,))), 0, rates[0]),
            renew(planes[1], wide(rows, d_upward, ((0,), (0,))), 0, rates[0]),
        ],
        axis=0,
    )
    new_dn = renew(weights_dn, wide(hidden, pulls, ((0,), (0,))), 1, rates[1])
    return [dx_part, new_planes, new_dn]


def per_device(
    rows_in,
    cotangent,
    lengths,
    train_experts,
    train_gates,
    decode_experts,
    decode_gates,
    gate_up,
    down,
):
    ep_count = lax.axis_size("ep")
    dp_count = lax.axis_size("dp")
    device_count = ep_count * dp_count
    row_count, model_width = cotangent.shape
    role = lax.axis_index("grp").astype(jnp.int32)
    is_learner = role == 0
    mine = lax.axis_index("ep").astype(jnp.int32)
    own_dn = down[0, 0]
    planes = jnp.transpose(gate_up[0, 0], (1, 0, 2))
    total_rows = row_count * device_count
    longest = 2 * total_rows // lengths.shape[0]
    rates = (0.5 / model_width**0.5, 0.5 / (own_dn.shape[0] * dp_count) ** 0.5)
    small = device_count == 16 and dp_count == 1
    first_place = mine.reshape(1)
    fresh_place = first_place + 2 * ep_count

    where = jnp.stack([mine * dp_count + lax.axis_index("dp").astype(jnp.int32), role])
    block, base = prep_call(
        where, lengths, rows_in[0], cotangent, train_experts, train_gates, decode_experts,
        decode_gates, ep_count, longest,
    )
    if small:
        near, away = send_z(block, (0, 1))
        near, planes = tied(near, planes)
        near, away = send_y(near, away, (0, 1))
        near, cotangent = tied(near, cotangent)
        every = send_core(near, away, (0, 1))
        cots = send_core(*send_y(*send_z(cotangent, (0,)), (0,)), (0,))
        hidden_count = own_dn.shape[0]
        part_shape = jax.ShapeDtypeStruct(cots[0].shape, jnp.bfloat16)

        def learn(every, cots, planes, own_dn):
            out = learn_call(first_place, every, every, cots, planes, own_dn, ep_count, rates)
            return ([unset(part_shape)] * 4, list(out))

        def decode(every, cots, planes, own_dn):
            out = ffn_call(first_place, every, every, planes, own_dn, ep_count)
            shapes = learn_shapes(total_rows, hidden_count, model_width)
            return (list(out), [unset(one) for one in shapes])

        part, learned = lax.cond(is_learner, learn, decode, every, cots, planes, own_dn)
        dx_part = across(learned[0], 0, 1)
        near, away = sum_y(*sum_core(part, (1,)), (1,))
        current = (base + sum_z(near, away, (1,))).astype(jnp.bfloat16)
        hopped = across(current, 1, 0)
        near, away = send_y(*send_z(hopped, (0,)), (0,))
        arrived = send_core(near, away, (0,))
        fresh_part = lax.cond(
            is_learner,
            lambda r, t, g, d, *c: list(ffn_call(fresh_place, r, t, g, d, ep_count, c)),
            lambda r, t, g, d, *c: [unset(one) for one in r],
            arrived,
            every,
            planes,
            own_dn,
            *learned[1:],
        )
        fresh_part[3], dx_part = tied(fresh_part[3], dx_part)
        dx_near, dx_away = sum_y(*sum_core(jnp.split(dx_part, 4, axis=0), (1,)), (1,))
        dx_sum = sum_z(dx_near, dx_away, (1,)).astype(jnp.bfloat16)
        dx_sum = across(dx_sum, 1, 0).astype(jnp.float32)
        near, away = sum_y(*sum_core(fresh_part, (0,)), (0,))
        fresh_sum = sum_z(near, away, (0,))
    else:
        every = [gather(block, device_count, (0, 1))]
        cots = gather(cotangent, device_count, (0,))

        def learn(every, cots, planes, own_dn):
            out = list(learn_plain(first_place, every, every, cots, planes, own_dn, ep_count, rates))
            return ([unset(out[0])], out[0], out[1], out[2])

        def decode(every, cots, planes, own_dn):
            out = list(ffn_plain(first_place, every, every, planes, own_dn, ep_count))
            return (out, unset(cots), unset(planes), unset(own_dn))

        part, dx_part, new_planes, new_dn = lax.cond(
            is_learner, learn, decode, every, cots, planes, own_dn
        )
        stale_sum = scatter_sum(part[0], device_count, (1,))
        current = (base + stale_sum).astype(jnp.bfloat16)
        dx_sum = scatter_sum(dx_part, device_count, (0,))
        arrived = [gather(across(current, 1, 0), device_count, (0,))]
        fresh_part = lax.cond(
            is_learner,
            lambda r, e, g, d: list(ffn_plain(fresh_place, r, e, g, d, ep_count)),
            lambda r, e, g, d: [unset(o) for o in r],
            arrived,
            every,
            new_planes,
            new_dn,
        )
        fresh_sum = scatter_sum(fresh_part[0], device_count, (0,))
    moved = across(fresh_sum.astype(jnp.bfloat16), 0, 1).astype(jnp.float32)
    final_rows = jnp.where(is_learner, base + dx_sum, current.astype(jnp.float32) + moved)
    return final_rows.astype(jnp.bfloat16)[None]


def solution(mesh):
    placed = (
        P("grp", ("ep", "dp"), None),
        P(("ep", "dp"), None),
        P(),
        P(("ep", "dp"), None),
        P(("ep", "dp"), None),
        P(None, ("ep", "dp"), None),
        P(None, ("ep", "dp"), None),
        P("grp", "ep", None, None, "dp"),
        P("grp", "ep", "dp", None),
    )
    return jax.shard_map(
        per_device,
        mesh=mesh,
        in_specs=placed,
        out_specs=P("grp", ("ep", "dp"), None),
        check_vma=False,
    )
```

```python
import functools

import jax
import jax.numpy as jnp
from jax import lax
from jax.experimental import pallas as pl
from jax.experimental.pallas import tpu as pltpu
from jax.sharding import PartitionSpec as P

EPSILON = 1e-06
AXES = ("ep", "dp")


def across(block, source, target):
    return lax.ppermute(block, "grp", [(source, target)])


def stages(device_count):
    sizes = []
    rest = device_count
    while rest > 1:
        size = 2 if len(sizes) < 2 or rest % 4 else 4
        sizes.append(size)
        rest //= size
    strides = []
    stride = device_count
    for size in sizes[::-1]:
        stride //= size
        strides.append((stride, size))
    return strides


def swap(block, device_count, flip, role, onward=0):
    pairs = [
        (part * device_count + i, (part + onward) * device_count + (i ^ flip))
        for part in role
        for i in range(device_count)
    ]
    return lax.ppermute(block, ("grp",) + AXES, pairs)


def tied(*values):
    return lax.optimization_barrier(values)


def gather(block, device_count, role):
    for stride, size in stages(device_count):
        got = [swap(block, device_count, turn * stride, role) for turn in range(1, size)]
        block = jnp.concatenate([block] + got, axis=0)
    return block


def send_z(block, role):
    far = [swap(block, 16, flip, role) for flip in (4, 8, 12)]
    return jnp.concatenate([block, far[0]], axis=0), jnp.concatenate(far[1:], axis=0)


def send_y(near, away, role):
    return [jnp.concatenate([part, swap(part, 16, 2, role)], axis=0) for part in (near, away)]


def send_core(near, away, role):
    return [near, swap(near, 16, 1, role), away, swap(away, 16, 1, role)]


def plus(kept, *sent):
    total = kept.astype(jnp.float32)
    for one in sent:
        total = total + one.astype(jnp.float32)
    return total


def halves(array):
    return jnp.split(array, 2, axis=0)


def scatter_sum(part, device_count, role):
    for stride, size in stages(device_count)[::-1]:
        cuts = jnp.split(part, size, axis=0)
        got = [swap(cuts[turn], device_count, turn * stride, role) for turn in range(1, size)]
        total = plus(cuts[0], *got)
        part = total.astype(jnp.bfloat16)
    return total


def sum_core(pieces, role):
    away = plus(pieces[2], swap(pieces[3], 16, 1, role)).astype(jnp.bfloat16)
    near = plus(pieces[0], swap(pieces[1], 16, 1, role)).astype(jnp.bfloat16)
    return near, away


def sum_y(near, away, role):
    kept, sent = halves(away)
    away = plus(kept, swap(sent, 16, 2, role)).astype(jnp.bfloat16)
    kept, sent = halves(near)
    near = plus(kept, swap(sent, 16, 2, role)).astype(jnp.bfloat16)
    return near, away


def sum_z(near, away, role):
    second, third = [swap(h, 16, f, role) for h, f in zip(halves(away), (8, 12))]
    kept, sent = halves(near)
    return plus(kept, swap(sent, 16, 4, role), second, third)


def renew(weights, grads, axis_number, rate):
    scale = jnp.sqrt(jnp.mean(grads * grads, axis=axis_number, keepdims=True) + EPSILON)
    return (weights.astype(jnp.float32) - rate * grads / scale).astype(jnp.bfloat16)


def wide(a, b, contract):
    return lax.dot_general(a, b, (contract, ((), ())), preferred_element_type=jnp.float32)


def nn(a, b):
    return wide(a, b, ((1,), (0,)))


def nt(a, b):
    return wide(a, b, ((1,), (1,)))


def prep_kernel(
    place, lengths, rows_ref, cot_ref, ids_ref, gates_ref, dec_ids_ref, dec_gates_ref,
    out_ref, base_ref, *, experts, longest,
):
    width = rows_ref.shape[1]
    row_count = rows_ref.shape[0]
    learner = place[1] == 0
    places = place[0] * row_count + lax.broadcasted_iota(jnp.int32, (1, row_count), 1)
    start = jnp.int32(0)
    seq_len = jnp.zeros((1, row_count), jnp.int32)
    for i in range(lengths.shape[0]):
        end = start + lengths[i]
        seq_len = jnp.where((places >= start) & (places < end), lengths[i], seq_len)
        start = end
    weight = 2.0 * longest / (seq_len.astype(jnp.float32) + longest)
    names = lax.broadcasted_iota(jnp.int32, (experts, row_count), 0)

    def table(ids, gates):
        total = jnp.zeros((experts, row_count), jnp.float32)
        for k in range(ids.shape[0]):
            total = total + jnp.where(names == ids[k : k + 1], gates[k : k + 1], 0.0)
        return total

    train = table(ids_ref[...], gates_ref[...]) * weight
    stale = table(dec_ids_ref[0], dec_gates_ref[0])
    first = jnp.where(learner, train, stale)
    fresh = table(dec_ids_ref[1], dec_gates_ref[1])
    parts = []
    for one in (first, fresh):
        upper = one.astype(jnp.bfloat16).astype(jnp.float32)
        parts += [upper, one - upper]
    spare = out_ref.shape[1] - width
    if spare > 4 * experts:
        parts.append(jnp.zeros((spare - 4 * experts, row_count), jnp.float32))
    stacked = jnp.concatenate(parts, axis=0)
    weights = jnp.broadcast_to(weight, (128, row_count))
    square = jnp.concatenate([stacked, weights], axis=0)
    square = jnp.concatenate(
        [square, jnp.zeros((square.shape[0], 128 - row_count), jnp.float32)], axis=1
    )
    for i in range(spare // 128):
        turned = square[128 * i : 128 * (i + 1)].T
        out_ref[:, width + 128 * i : width + 128 * (i + 1)] = turned[:row_count].astype(
            jnp.bfloat16
        )
    column = square[spare:].T[:row_count, 0:1]
    out_ref[:, :width] = rows_ref[...]
    base_ref[...] = jnp.where(
        learner, column * cot_ref[...].astype(jnp.float32), rows_ref[...].astype(jnp.float32)
    )


def prep_call(place, lengths, rows, cot, ids, gates, dec_ids, dec_gates, experts, longest):
    row_count, width = rows.shape
    spare = -(-4 * experts // 128) * 128
    scalars = pl.BlockSpec(memory_space=pltpu.SMEM)
    whole = pl.BlockSpec(memory_space=pltpu.VMEM)
    return pl.pallas_call(
        functools.partial(prep_kernel, experts=experts, longest=longest),
        in_specs=[scalars, scalars] + [whole] * 6,
        out_specs=[whole, whole],
        out_shape=[
            jax.ShapeDtypeStruct((row_count, width + spare), jnp.bfloat16),
            jax.ShapeDtypeStruct((row_count, width), jnp.float32),
        ],
        name="prep",
    )(place, lengths, rows, cot, ids.T, gates.T, jnp.swapaxes(dec_ids, 1, 2), jnp.swapaxes(dec_gates, 1, 2))


def pick_gates(table, column, step):
    places = lax.broadcasted_iota(jnp.int32, table.shape, 1)
    taken = (places == column) | (places == column + step)
    return jnp.sum(jnp.where(taken, table.astype(jnp.float32), 0.0), axis=1, keepdims=True)


def parts_of(array, count):
    parts = []
    for _ in range(count):
        parts.append(array.astype(jnp.bfloat16))
        array = array - parts[-1].astype(jnp.float32)
    return parts


def fine(array, other, count):
    total = None
    for part in parts_of(array, count):
        product = nn(part, other)
        total = product if total is None else total + product
    return total


TILE = 1024


def tiles_of(width):
    return [slice(lower, lower + TILE) for lower in range(0, width, TILE)]


def reads(pairs, sems):
    return [pltpu.make_async_copy(src, dst, sems.at[i]) for i, (src, dst) in enumerate(pairs)]


def row_reads(refs, count, width, rows, table):
    part = rows.shape[0] // count
    spare = table.shape[1]
    here = [pl.ds(part * i, part) for i in range(count)]
    wide_pairs = [(refs[i].at[:, pl.ds(0, width)], rows.at[here[i]]) for i in range(count)]
    thin_pairs = [
        (refs[count + i].at[:, pl.ds(width, spare)], table.at[here[i]]) for i in range(count)
    ]
    return wide_pairs + thin_pairs


def weight_reads(gu_ref, dn_ref, gu, dn):
    cuts = [pl.ds(lower, TILE) for lower in range(0, dn.shape[1], TILE)]
    return [(gu_ref.at[:, cut], gu.at[:, cut]) for cut in cuts], [
        (dn_ref.at[:, cut], dn.at[:, cut]) for cut in cuts
    ]


def added(total, product):
    return product if total is None else total + product


def ffn_kernel(place, *refs, count, experts, changed):
    gu_ref, dn_ref = refs[2 * count : 2 * count + 2]
    extra = 5 if changed else 0
    extra_refs = refs[2 * count + 2 : 2 * count + 2 + extra]
    refs_left = refs[2 * count + 2 + extra :]
    out_refs = refs_left[:count]
    rows, table, gu, dn = refs_left[count : count + 4]
    extras = refs_left[count + 4 : count + 4 + extra]
    sems = refs_left[count + 4 + extra]
    width = dn.shape[1]
    cuts = tiles_of(width)
    first = row_reads(refs, count, width, rows, table)
    gu_pairs, dn_pairs = weight_reads(gu_ref, dn_ref, gu, dn)
    more = list(zip(extra_refs, extras))
    copies = reads(first + more[:1] + gu_pairs + more[1:] + dn_pairs, sems)
    for copy in copies:
        copy.start()
    done = len(first) + len(more[:1])
    for copy in copies[:done]:
        copy.wait()
    active = upward = alike = None
    for cut in cuts:
        copies[done].wait()
        done += 1
        active = added(active, nn(rows[:, cut], gu[0, cut]))
        upward = added(upward, nn(rows[:, cut], gu[1, cut]))
        if changed:
            alike = added(alike, nn(rows[:, cut], extras[0][cut]))
    for copy in copies[done : done + len(more[1:])]:
        copy.wait()
    done += len(more[1:])
    if changed:
        turned, sent, hidden_turned, rates, pulls = extras
        active = active - fine(alike, sent[0], 2) * rates[0:1]
        upward = upward - fine(alike, sent[1], 2) * rates[1:2]
    hidden = (active * jax.nn.sigmoid(active) * upward).astype(jnp.bfloat16)
    if changed:
        scaled = hidden.astype(jnp.float32) * rates[2:3]
        mixed = parts_of(fine(scaled, hidden_turned[...], 2), 2)
    gates = pick_gates(table[...], place[0], experts)
    part = rows.shape[0] // count
    for cut in cuts:
        copies[done].wait()
        done += 1
        out = nn(hidden, dn[:, cut])
        if changed:
            for one in mixed:
                out = out - nn(one, pulls[:, cut])
        out = (gates * out).astype(jnp.bfloat16)
        for i in range(count):
            out_refs[i][:, cut] = out[part * i : part * (i + 1)]


def ffn_call(place, pieces, tables, planes, weights_dn, experts, change=()):
    count = len(pieces)
    part = pieces[0].shape[0]
    hidden_count, width = weights_dn.shape
    row_count = part * count
    anywhere = pl.BlockSpec(memory_space=pl.ANY)
    whole = pl.BlockSpec(memory_space=pltpu.VMEM)
    return pl.pallas_call(
        functools.partial(ffn_kernel, count=count, experts=experts, changed=bool(change)),
        in_specs=[pl.BlockSpec(memory_space=pltpu.SMEM)]
        + [anywhere] * (2 * count + 2 + len(change)),
        out_specs=[whole] * count,
        scratch_shapes=[
            pltpu.VMEM((row_count, width), jnp.bfloat16),
            pltpu.VMEM((row_count, tables[0].shape[1] - width), jnp.bfloat16),
            pltpu.VMEM(planes.shape, jnp.bfloat16),
            pltpu.VMEM(weights_dn.shape, jnp.bfloat16),
        ]
        + [pltpu.VMEM(one.shape, one.dtype) for one in change]
        + [pltpu.SemaphoreType.DMA((2 * count + len(change) + 2 * (width // TILE),))],
        out_shape=[jax.ShapeDtypeStruct((part, width), jnp.bfloat16)] * count,
        compiler_params=pltpu.CompilerParams(vmem_limit_bytes=44 << 20),
        cost_estimate=pl.CostEstimate(
            flops=6 * row_count * hidden_count * width,
            bytes_accessed=6 * hidden_count * width,
            transcendentals=row_count * hidden_count,
        ),
        name="ffn_changed" if change else "ffn",
    )(place, *pieces, *tables, planes, weights_dn, *change)


def learn_kernel(place, *refs, count, experts, rates):
    cot_refs = refs[2 * count : 3 * count]
    gu_ref, dn_ref = refs[3 * count : 3 * count + 2]
    goals = refs[3 * count + 2 : 3 * count + 8]
    rows, table, cots, pulls_turned, gu, dn, sems, out_sems = refs[3 * count + 8 : 3 * count + 16]
    held = refs[3 * count + 16 :]
    dx, turned, sent, hidden_turned, factors, pulls = held
    hidden_count, width = dn.shape
    part = rows.shape[0] // count
    cuts = tiles_of(width)
    first = row_reads(refs, count, width, rows, table)
    first += [(cot_refs[i], cots.at[pl.ds(part * i, part)]) for i in range(count)]
    gu_pairs, dn_pairs = weight_reads(gu_ref, dn_ref, gu, dn)
    both = [pair for pairs in zip(gu_pairs, dn_pairs) for pair in pairs]
    copies = reads(first + both, sems)
    for copy in copies:
        copy.start()
    done = len(first)
    for copy in copies[:done]:
        copy.wait()
    gates = pick_gates(table[...], place[0], experts)
    for cut in cuts:
        pulls[:, cut] = (gates * cots[:, cut].astype(jnp.float32)).astype(jnp.bfloat16)
        turned[cut, :] = rows[:, cut].T
        pulls_turned[cut, :] = pulls[:, cut].T
    writes = []

    def write(source, goal):
        copy = pltpu.make_async_copy(source, goal, out_sems.at[len(writes)])
        copy.start()
        writes.append(copy)

    write(turned, goals[1])
    write(pulls, goals[5])
    alike_rows = nn(rows[...], turned[...])
    alike_pulls = nn(pulls[...], pulls_turned[...])
    active = upward = back = None
    for cut in cuts:
        copies[done].wait()
        copies[done + 1].wait()
        done += 2
        active = added(active, nn(rows[:, cut], gu[0, cut]))
        upward = added(upward, nn(rows[:, cut], gu[1, cut]))
        back = added(back, nn(dn[:, cut], pulls_turned[cut]))
    back = back.T
    sigma = jax.nn.sigmoid(active)
    swish = active * sigma
    hidden = (swish * upward).astype(jnp.bfloat16)
    d_active = (back * upward * sigma * (1.0 + active * (1.0 - sigma))).astype(jnp.bfloat16)
    d_upward = (back * swish).astype(jnp.bfloat16)
    sent[0] = d_active
    sent[1] = d_upward
    hidden_turned[...] = hidden.T
    write(sent, goals[2])
    write(hidden_turned, goals[3])
    d_active_turned = d_active.T
    d_upward_turned = d_upward.T

    for cut in cuts:
        out = nn(gu[0, cut], d_active_turned) + nn(gu[1, cut], d_upward_turned)
        out = out.T.astype(jnp.bfloat16)
        slab = part // 2
        for i in range(count):
            for half in range(2):
                lower = ((i % 2) * 2 + half) * part + (i // 2) * slab
                here = part * i + slab * half
                dx[lower : lower + slab, cut] = out[here : here + slab]
        columns = pl.ds(cut.start, TILE)
        write(dx.at[:, columns], goals[0].at[:, columns])

    def mean_square(alike, factor):
        wide_factor = factor.astype(jnp.float32)
        squares = jnp.sum(wide_factor * fine(alike, factor, 3), axis=0, keepdims=True)
        return jnp.maximum(squares, 0.0) / width

    factors[0:1] = rates[0] / jnp.sqrt(mean_square(alike_rows, d_active) + EPSILON)
    factors[1:2] = rates[0] / jnp.sqrt(mean_square(alike_rows, d_upward) + EPSILON)
    factors[2:3] = rates[1] / jnp.sqrt(mean_square(alike_pulls, hidden) + EPSILON)
    factors[3:8] = jnp.zeros((5, hidden_count), jnp.float32)
    write(factors, goals[4])
    for copy in writes:
        copy.wait()


def learn_shapes(row_count, hidden_count, width):
    return [
        jax.ShapeDtypeStruct((row_count, width), jnp.bfloat16),
        jax.ShapeDtypeStruct((width, row_count), jnp.bfloat16),
        jax.ShapeDtypeStruct((2, row_count, hidden_count), jnp.bfloat16),
        jax.ShapeDtypeStruct((hidden_count, row_count), jnp.bfloat16),
        jax.ShapeDtypeStruct((8, hidden_count), jnp.float32),
        jax.ShapeDtypeStruct((row_count, width), jnp.bfloat16),
    ]


def learn_call(place, pieces, tables, cots, planes, weights_dn, experts, rates):
    count = len(pieces)
    hidden_count, width = weights_dn.shape
    row_count = pieces[0].shape[0] * count
    anywhere = pl.BlockSpec(memory_space=pl.ANY)
    out_shape = learn_shapes(row_count, hidden_count, width)
    return pl.pallas_call(
        functools.partial(learn_kernel, count=count, experts=experts, rates=rates),
        in_specs=[pl.BlockSpec(memory_space=pltpu.SMEM)] + [anywhere] * (3 * count + 2),
        out_specs=[anywhere] * len(out_shape),
        scratch_shapes=[
            pltpu.VMEM((row_count, width), jnp.bfloat16),
            pltpu.VMEM((row_count, tables[0].shape[1] - width), jnp.bfloat16),
            pltpu.VMEM((row_count, width), jnp.bfloat16),
            pltpu.VMEM((width, row_count), jnp.bfloat16),
            pltpu.VMEM(planes.shape, jnp.bfloat16),
            pltpu.VMEM(weights_dn.shape, jnp.bfloat16),
            pltpu.SemaphoreType.DMA((3 * count + 2 * (width // TILE),)),
            pltpu.SemaphoreType.DMA((5 + width // TILE,)),
        ]
        + [pltpu.VMEM(one.shape, one.dtype) for one in out_shape],
        out_shape=out_shape,
        compiler_params=pltpu.CompilerParams(vmem_limit_bytes=48 << 20),
        cost_estimate=pl.CostEstimate(
            flops=12 * row_count * hidden_count * width,
            bytes_accessed=6 * hidden_count * width,
            transcendentals=row_count * hidden_count,
        ),
        name="learn",
    )(place, *pieces, *tables, *cots, planes, weights_dn)


def unset(like):
    return pl.pallas_call(
        lambda out_ref: None,
        out_shape=jax.ShapeDtypeStruct(like.shape, like.dtype),
        out_specs=pl.BlockSpec(memory_space=pl.ANY),
        name="unset",
    )()


def ffn_plain(place, pieces, tables, planes, weights_dn, experts):
    width = weights_dn.shape[1]
    rows = pieces[0][:, :width]
    gates = pick_gates(tables[0][:, width:], place[0], experts)
    active = nn(rows, planes[0])
    upward = nn(rows, planes[1])
    hidden = (active * jax.nn.sigmoid(active) * upward).astype(jnp.bfloat16)
    return [(gates * nn(hidden, weights_dn)).astype(jnp.bfloat16)]


def learn_plain(place, pieces, tables, cots, planes, weights_dn, experts, rates):
    width = weights_dn.shape[1]
    rows = pieces[0][:, :width]
    gates = pick_gates(tables[0][:, width:], place[0], experts)
    pulls = (gates * cots.astype(jnp.float32)).astype(jnp.bfloat16)
    active = nn(rows, planes[0])
    upward = nn(rows, planes[1])
    back = nt(pulls, weights_dn)
    sigma = jax.nn.sigmoid(active)
    swish = active * sigma
    hidden = (swish * upward).astype(jnp.bfloat16)
    d_active = (back * upward * sigma * (1.0 + active * (1.0 - sigma))).astype(jnp.bfloat16)
    d_upward = (back * swish).astype(jnp.bfloat16)
    dx_part = (nt(d_active, planes[0]) + nt(d_upward, planes[1])).astype(jnp.bfloat16)
    new_planes = jnp.stack(
        [
            renew(planes[0], wide(rows, d_active, ((0,), (0,))), 0, rates[0]),
            renew(planes[1], wide(rows, d_upward, ((0,), (0,))), 0, rates[0]),
        ],
        axis=0,
    )
    new_dn = renew(weights_dn, wide(hidden, pulls, ((0,), (0,))), 1, rates[1])
    return [dx_part, new_planes, new_dn]


def per_device(
    rows_in,
    cotangent,
    lengths,
    train_experts,
    train_gates,
    decode_experts,
    decode_gates,
    gate_up,
    down,
):
    ep_count = lax.axis_size("ep")
    dp_count = lax.axis_size("dp")
    device_count = ep_count * dp_count
    row_count, model_width = cotangent.shape
    role = lax.axis_index("grp").astype(jnp.int32)
    is_learner = role == 0
    mine = lax.axis_index("ep").astype(jnp.int32)
    own_dn = down[0, 0]
    planes = jnp.transpose(gate_up[0, 0], (1, 0, 2))
    total_rows = row_count * device_count
    longest = 2 * total_rows // lengths.shape[0]
    rates = (0.5 / model_width**0.5, 0.5 / (own_dn.shape[0] * dp_count) ** 0.5)
    small = device_count == 16 and dp_count == 1
    first_place = mine.reshape(1)
    fresh_place = first_place + 2 * ep_count

    where = jnp.stack([mine * dp_count + lax.axis_index("dp").astype(jnp.int32), role])
    block, base = prep_call(
        where, lengths, rows_in[0], cotangent, train_experts, train_gates, decode_experts,
        decode_gates, ep_count, longest,
    )
    if small:
        near, away = send_z(block, (0, 1))
        near, planes = tied(near, planes)
        cot_near, cot_away = send_z(tied(cotangent, near)[0], (0,))
        near, away = send_y(near, away, (0, 1))
        near, away, cot_near, cot_away = tied(near, away, cot_near, cot_away)
        every = send_core(near, away, (0, 1))
        cots = send_core(*send_y(cot_near, cot_away, (0,)), (0,))
        hidden_count = own_dn.shape[0]
        part_shape = jax.ShapeDtypeStruct(cots[0].shape, jnp.bfloat16)

        def learn(every, cots, planes, own_dn):
            out = learn_call(first_place, every, every, cots, planes, own_dn, ep_count, rates)
            return ([unset(part_shape)] * 4, list(out))

        def decode(every, cots, planes, own_dn):
            out = ffn_call(first_place, every, every, planes, own_dn, ep_count)
            shapes = learn_shapes(total_rows, hidden_count, model_width)
            return (list(out), [unset(one) for one in shapes])

        part, learned = lax.cond(is_learner, learn, decode, every, cots, planes, own_dn)
        dx_part = across(learned[0], 0, 1)
        near, away = sum_y(*sum_core(part, (1,)), (1,))
        current = (base + sum_z(near, away, (1,))).astype(jnp.bfloat16)
        hopped = across(current, 1, 0)
        near, away = send_y(*send_z(hopped, (0,)), (0,))
        arrived = send_core(near, away, (0,))
        fresh_part = lax.cond(
            is_learner,
            lambda r, t, g, d, *c: list(ffn_call(fresh_place, r, t, g, d, ep_count, c)),
            lambda r, t, g, d, *c: [unset(one) for one in r],
            arrived,
            every,
            planes,
            own_dn,
            *learned[1:],
        )
        fresh_part[3], dx_part = tied(fresh_part[3], dx_part)
        dx_sum = scatter_sum(dx_part, 16, (1,)).astype(jnp.bfloat16)
        dx_sum = across(dx_sum, 1, 0).astype(jnp.float32)
        near, away = sum_y(*sum_core(fresh_part, (0,)), (0,))
        blocks = halves(away) + halves(near)[::-1]
        moved = plus(*[swap(b, 16, f, (0,), 1) for b, f in zip(blocks, (8, 12, 4, 0))])
    else:
        every = [gather(block, device_count, (0, 1))]
        cots = gather(cotangent, device_count, (0,))

        def learn(every, cots, planes, own_dn):
            out = list(learn_plain(first_place, every, every, cots, planes, own_dn, ep_count, rates))
            return ([unset(out[0])], out[0], out[1], out[2])

        def decode(every, cots, planes, own_dn):
            out = list(ffn_plain(first_place, every, every, planes, own_dn, ep_count))
            return (out, unset(cots), unset(planes), unset(own_dn))

        part, dx_part, new_planes, new_dn = lax.cond(
            is_learner, learn, decode, every, cots, planes, own_dn
        )
        stale_sum = scatter_sum(part[0], device_count, (1,))
        current = (base + stale_sum).astype(jnp.bfloat16)
        dx_sum = scatter_sum(dx_part, device_count, (0,))
        arrived = [gather(across(current, 1, 0), device_count, (0,))]
        fresh_part = lax.cond(
            is_learner,
            lambda r, e, g, d: list(ffn_plain(fresh_place, r, e, g, d, ep_count)),
            lambda r, e, g, d: [unset(o) for o in r],
            arrived,
            every,
            new_planes,
            new_dn,
        )
        fresh_sum = scatter_sum(fresh_part[0], device_count, (0,))
        moved = across(fresh_sum.astype(jnp.bfloat16), 0, 1).astype(jnp.float32)
    final_rows = jnp.where(is_learner, base + dx_sum, current.astype(jnp.float32) + moved)
    return final_rows.astype(jnp.bfloat16)[None]


def solution(mesh):
    placed = (
        P("grp", ("ep", "dp"), None),
        P(("ep", "dp"), None),
        P(),
        P(("ep", "dp"), None),
        P(("ep", "dp"), None),
        P(None, ("ep", "dp"), None),
        P(None, ("ep", "dp"), None),
        P("grp", "ep", None, None, "dp"),
        P("grp", "ep", "dp", None),
    )
    return jax.shard_map(
        per_device,
        mesh=mesh,
        in_specs=placed,
        out_specs=P("grp", ("ep", "dp"), None),
        check_vma=False,
    )
```

```python
import functools

import jax
import jax.numpy as jnp
from jax import lax
from jax.experimental import pallas as pl
from jax.experimental.pallas import tpu as pltpu
from jax.sharding import PartitionSpec as P

EPSILON = 1e-06
AXES = ("ep", "dp")


def across(block, source, target):
    return lax.ppermute(block, "grp", [(source, target)])


def stages(device_count):
    sizes = []
    rest = device_count
    while rest > 1:
        size = 2 if len(sizes) < 2 or rest % 4 else 4
        sizes.append(size)
        rest //= size
    strides = []
    stride = device_count
    for size in sizes[::-1]:
        stride //= size
        strides.append((stride, size))
    return strides


def swap(block, device_count, flip, role, onward=0):
    pairs = [
        (part * device_count + i, (part + onward) * device_count + (i ^ flip))
        for part in role
        for i in range(device_count)
    ]
    return lax.ppermute(block, ("grp",) + AXES, pairs)


def tied(*values):
    return lax.optimization_barrier(values)


def gather(block, device_count, role):
    for stride, size in stages(device_count):
        got = [swap(block, device_count, turn * stride, role) for turn in range(1, size)]
        block = jnp.concatenate([block] + got, axis=0)
    return block


def send_z(block, role):
    far = [swap(block, 16, flip, role) for flip in (4, 8, 12)]
    return jnp.concatenate([block, far[0]], axis=0), jnp.concatenate(far[1:], axis=0)


def send_y(near, away, role):
    return [jnp.concatenate([part, swap(part, 16, 2, role)], axis=0) for part in (near, away)]


def send_core(near, away, role):
    return [near, swap(near, 16, 1, role), away, swap(away, 16, 1, role)]


def plus(kept, *sent):
    total = kept.astype(jnp.float32)
    for one in sent:
        total = total + one.astype(jnp.float32)
    return total


def halves(array):
    return jnp.split(array, 2, axis=0)


def scatter_sum(part, device_count, role):
    for stride, size in stages(device_count)[::-1]:
        cuts = jnp.split(part, size, axis=0)
        got = [swap(cuts[turn], device_count, turn * stride, role) for turn in range(1, size)]
        total = plus(cuts[0], *got)
        part = total.astype(jnp.bfloat16)
    return total


def sum_core(pieces, role):
    away = plus(pieces[2], swap(pieces[3], 16, 1, role)).astype(jnp.bfloat16)
    near = plus(pieces[0], swap(pieces[1], 16, 1, role)).astype(jnp.bfloat16)
    return near, away


def sum_y(near, away, role):
    kept, sent = halves(away)
    away = plus(kept, swap(sent, 16, 2, role)).astype(jnp.bfloat16)
    kept, sent = halves(near)
    near = plus(kept, swap(sent, 16, 2, role)).astype(jnp.bfloat16)
    return near, away


def sum_z(near, away, role):
    second, third = [swap(h, 16, f, role) for h, f in zip(halves(away), (8, 12))]
    kept, sent = halves(near)
    return plus(kept, swap(sent, 16, 4, role), second, third)


def renew(weights, grads, axis_number, rate):
    scale = jnp.sqrt(jnp.mean(grads * grads, axis=axis_number, keepdims=True) + EPSILON)
    return (weights.astype(jnp.float32) - rate * grads / scale).astype(jnp.bfloat16)


def wide(a, b, contract):
    return lax.dot_general(a, b, (contract, ((), ())), preferred_element_type=jnp.float32)


def nn(a, b):
    return wide(a, b, ((1,), (0,)))


def nt(a, b):
    return wide(a, b, ((1,), (1,)))


def prep_kernel(
    place, lengths, rows_ref, cot_ref, ids_ref, gates_ref, dec_ids_ref, dec_gates_ref,
    out_ref, base_ref, *, experts, longest,
):
    width = rows_ref.shape[1]
    row_count = rows_ref.shape[0]
    learner = place[1] == 0
    places = place[0] * row_count + lax.broadcasted_iota(jnp.int32, (1, row_count), 1)
    start = jnp.int32(0)
    seq_len = jnp.zeros((1, row_count), jnp.int32)
    for i in range(lengths.shape[0]):
        end = start + lengths[i]
        seq_len = jnp.where((places >= start) & (places < end), lengths[i], seq_len)
        start = end
    weight = 2.0 * longest / (seq_len.astype(jnp.float32) + longest)
    names = lax.broadcasted_iota(jnp.int32, (experts, row_count), 0)

    def table(ids, gates):
        total = jnp.zeros((experts, row_count), jnp.float32)
        for k in range(ids.shape[0]):
            total = total + jnp.where(names == ids[k : k + 1], gates[k : k + 1], 0.0)
        return total

    train = table(ids_ref[...], gates_ref[...]) * weight
    stale = table(dec_ids_ref[0], dec_gates_ref[0])
    first = jnp.where(learner, train, stale)
    fresh = table(dec_ids_ref[1], dec_gates_ref[1])
    parts = []
    for one in (first, fresh):
        upper = one.astype(jnp.bfloat16).astype(jnp.float32)
        parts += [upper, one - upper]
    spare = out_ref.shape[1] - width
    if spare > 4 * experts:
        parts.append(jnp.zeros((spare - 4 * experts, row_count), jnp.float32))
    stacked = jnp.concatenate(parts, axis=0)
    weights = jnp.broadcast_to(weight, (128, row_count))
    square = jnp.concatenate([stacked, weights], axis=0)
    square = jnp.concatenate(
        [square, jnp.zeros((square.shape[0], 128 - row_count), jnp.float32)], axis=1
    )
    for i in range(spare // 128):
        turned = square[128 * i : 128 * (i + 1)].T
        out_ref[:, width + 128 * i : width + 128 * (i + 1)] = turned[:row_count].astype(
            jnp.bfloat16
        )
    column = square[spare:].T[:row_count, 0:1]
    out_ref[:, :width] = rows_ref[...]
    base_ref[...] = jnp.where(
        learner, column * cot_ref[...].astype(jnp.float32), rows_ref[...].astype(jnp.float32)
    )


def prep_call(place, lengths, rows, cot, ids, gates, dec_ids, dec_gates, experts, longest):
    row_count, width = rows.shape
    spare = -(-4 * experts // 128) * 128
    scalars = pl.BlockSpec(memory_space=pltpu.SMEM)
    whole = pl.BlockSpec(memory_space=pltpu.VMEM)
    return pl.pallas_call(
        functools.partial(prep_kernel, experts=experts, longest=longest),
        in_specs=[scalars, scalars] + [whole] * 6,
        out_specs=[whole, whole],
        out_shape=[
            jax.ShapeDtypeStruct((row_count, width + spare), jnp.bfloat16),
            jax.ShapeDtypeStruct((row_count, width), jnp.float32),
        ],
        name="prep",
    )(place, lengths, rows, cot, ids.T, gates.T, jnp.swapaxes(dec_ids, 1, 2), jnp.swapaxes(dec_gates, 1, 2))


def pick_gates(table, column, step):
    places = lax.broadcasted_iota(jnp.int32, table.shape, 1)
    taken = (places == column) | (places == column + step)
    return jnp.sum(jnp.where(taken, table.astype(jnp.float32), 0.0), axis=1, keepdims=True)


def parts_of(array, count):
    parts = []
    for _ in range(count):
        parts.append(array.astype(jnp.bfloat16))
        array = array - parts[-1].astype(jnp.float32)
    return parts


def fine(array, other, count):
    total = None
    for part in parts_of(array, count):
        product = nn(part, other)
        total = product if total is None else total + product
    return total


TILE = 1024


def tiles_of(width):
    return [slice(lower, lower + TILE) for lower in range(0, width, TILE)]


def reads(pairs, sems):
    return [pltpu.make_async_copy(src, dst, sems.at[i]) for i, (src, dst) in enumerate(pairs)]


def row_reads(refs, count, width, rows, table):
    part = rows.shape[0] // count
    spare = table.shape[1]
    here = [pl.ds(part * i, part) for i in range(count)]
    wide_pairs = [(refs[i].at[:, pl.ds(0, width)], rows.at[here[i]]) for i in range(count)]
    thin_pairs = [
        (refs[count + i].at[:, pl.ds(width, spare)], table.at[here[i]]) for i in range(count)
    ]
    return wide_pairs + thin_pairs


def weight_reads(gu_ref, dn_ref, gu, dn):
    cuts = [pl.ds(lower, TILE) for lower in range(0, dn.shape[1], TILE)]
    return [(gu_ref.at[:, cut], gu.at[:, cut]) for cut in cuts], [
        (dn_ref.at[:, cut], dn.at[:, cut]) for cut in cuts
    ]


def added(total, product):
    return product if total is None else total + product


def ffn_kernel(place, *refs, count, experts, changed):
    gu_ref, dn_ref = refs[2 * count : 2 * count + 2]
    extra = 5 if changed else 0
    extra_refs = refs[2 * count + 2 : 2 * count + 2 + extra]
    refs_left = refs[2 * count + 2 + extra :]
    out_refs = refs_left[:count]
    rows, table, gu, dn = refs_left[count : count + 4]
    extras = refs_left[count + 4 : count + 4 + extra]
    sems = refs_left[count + 4 + extra]
    width = dn.shape[1]
    cuts = tiles_of(width)
    first = row_reads(refs, count, width, rows, table)
    gu_pairs, dn_pairs = weight_reads(gu_ref, dn_ref, gu, dn)
    more = list(zip(extra_refs, extras))
    copies = reads(first + more[:1] + gu_pairs + more[1:] + dn_pairs, sems)
    for copy in copies:
        copy.start()
    done = len(first) + len(more[:1])
    for copy in copies[:done]:
        copy.wait()
    active = upward = alike = None
    for cut in cuts:
        copies[done].wait()
        done += 1
        active = added(active, nn(rows[:, cut], gu[0, cut]))
        upward = added(upward, nn(rows[:, cut], gu[1, cut]))
        if changed:
            alike = added(alike, nn(rows[:, cut], extras[0][cut]))
    for copy in copies[done : done + len(more[1:])]:
        copy.wait()
    done += len(more[1:])
    if changed:
        turned, sent, hidden_turned, rates, pulls = extras
        active = active - fine(alike, sent[0], 2) * rates[0:1]
        upward = upward - fine(alike, sent[1], 2) * rates[1:2]
    hidden = (active * jax.nn.sigmoid(active) * upward).astype(jnp.bfloat16)
    if changed:
        scaled = hidden.astype(jnp.float32) * rates[2:3]
        mixed = parts_of(fine(scaled, hidden_turned[...], 2), 2)
    gates = pick_gates(table[...], place[0], experts)
    part = rows.shape[0] // count
    for cut in cuts:
        copies[done].wait()
        done += 1
        out = nn(hidden, dn[:, cut])
        if changed:
            for one in mixed:
                out = out - nn(one, pulls[:, cut])
        out = (gates * out).astype(jnp.bfloat16)
        for i in range(count):
            out_refs[i][:, cut] = out[part * i : part * (i + 1)]


def ffn_call(place, pieces, tables, planes, weights_dn, experts, change=()):
    count = len(pieces)
    part = pieces[0].shape[0]
    hidden_count, width = weights_dn.shape
    row_count = part * count
    anywhere = pl.BlockSpec(memory_space=pl.ANY)
    whole = pl.BlockSpec(memory_space=pltpu.VMEM)
    return pl.pallas_call(
        functools.partial(ffn_kernel, count=count, experts=experts, changed=bool(change)),
        in_specs=[pl.BlockSpec(memory_space=pltpu.SMEM)]
        + [anywhere] * (2 * count + 2 + len(change)),
        out_specs=[whole] * count,
        scratch_shapes=[
            pltpu.VMEM((row_count, width), jnp.bfloat16),
            pltpu.VMEM((row_count, tables[0].shape[1] - width), jnp.bfloat16),
            pltpu.VMEM(planes.shape, jnp.bfloat16),
            pltpu.VMEM(weights_dn.shape, jnp.bfloat16),
        ]
        + [pltpu.VMEM(one.shape, one.dtype) for one in change]
        + [pltpu.SemaphoreType.DMA((2 * count + len(change) + 2 * (width // TILE),))],
        out_shape=[jax.ShapeDtypeStruct((part, width), jnp.bfloat16)] * count,
        compiler_params=pltpu.CompilerParams(vmem_limit_bytes=44 << 20),
        cost_estimate=pl.CostEstimate(
            flops=6 * row_count * hidden_count * width,
            bytes_accessed=6 * hidden_count * width,
            transcendentals=row_count * hidden_count,
        ),
        name="ffn_changed" if change else "ffn",
    )(place, *pieces, *tables, planes, weights_dn, *change)


def learn_kernel(place, *refs, count, experts, rates):
    cot_refs = refs[2 * count : 3 * count]
    gu_ref, dn_ref = refs[3 * count : 3 * count + 2]
    goals = refs[3 * count + 2 : 3 * count + 8]
    rows, table, cots, pulls_turned, gu, dn, sems, out_sems = refs[3 * count + 8 : 3 * count + 16]
    held = refs[3 * count + 16 :]
    dx, turned, sent, hidden_turned, factors, pulls = held
    hidden_count, width = dn.shape
    part = rows.shape[0] // count
    cuts = tiles_of(width)
    first = row_reads(refs, count, width, rows, table)
    first += [(cot_refs[i], cots.at[pl.ds(part * i, part)]) for i in range(count)]
    gu_pairs, dn_pairs = weight_reads(gu_ref, dn_ref, gu, dn)
    both = [pair for pairs in zip(gu_pairs, dn_pairs) for pair in pairs]
    copies = reads(first + both, sems)
    for copy in copies:
        copy.start()
    done = len(first)
    for copy in copies[:done]:
        copy.wait()
    gates = pick_gates(table[...], place[0], experts)
    for cut in cuts:
        pulls[:, cut] = (gates * cots[:, cut].astype(jnp.float32)).astype(jnp.bfloat16)
        turned[cut, :] = rows[:, cut].T
        pulls_turned[cut, :] = pulls[:, cut].T
    writes = []

    def write(source, goal):
        copy = pltpu.make_async_copy(source, goal, out_sems.at[len(writes)])
        copy.start()
        writes.append(copy)

    write(turned, goals[1])
    write(pulls, goals[5])
    alike_rows = nn(rows[...], turned[...])
    alike_pulls = nn(pulls[...], pulls_turned[...])
    active = upward = back = None
    for cut in cuts:
        copies[done].wait()
        copies[done + 1].wait()
        done += 2
        active = added(active, nn(rows[:, cut], gu[0, cut]))
        upward = added(upward, nn(rows[:, cut], gu[1, cut]))
        back = added(back, nn(dn[:, cut], pulls_turned[cut]))
    back = back.T
    sigma = jax.nn.sigmoid(active)
    swish = active * sigma
    hidden = (swish * upward).astype(jnp.bfloat16)
    d_active = (back * upward * sigma * (1.0 + active * (1.0 - sigma))).astype(jnp.bfloat16)
    d_upward = (back * swish).astype(jnp.bfloat16)
    sent[0] = d_active
    sent[1] = d_upward
    hidden_turned[...] = hidden.T
    write(sent, goals[2])
    write(hidden_turned, goals[3])
    d_active_turned = d_active.T
    d_upward_turned = d_upward.T

    for cut in cuts:
        out = nn(gu[0, cut], d_active_turned) + nn(gu[1, cut], d_upward_turned)
        out = out.T.astype(jnp.bfloat16)
        slab = part // 2
        for i in range(count):
            for half in range(2):
                lower = ((i % 2) * 2 + half) * part + (i // 2) * slab
                here = part * i + slab * half
                dx[lower : lower + slab, cut] = out[here : here + slab]
        columns = pl.ds(cut.start, TILE)
        write(dx.at[:, columns], goals[0].at[:, columns])

    def mean_square(alike, factor):
        wide_factor = factor.astype(jnp.float32)
        squares = jnp.sum(wide_factor * fine(alike, factor, 3), axis=0, keepdims=True)
        return jnp.maximum(squares, 0.0) / width

    factors[0:1] = rates[0] / jnp.sqrt(mean_square(alike_rows, d_active) + EPSILON)
    factors[1:2] = rates[0] / jnp.sqrt(mean_square(alike_rows, d_upward) + EPSILON)
    factors[2:3] = rates[1] / jnp.sqrt(mean_square(alike_pulls, hidden) + EPSILON)
    factors[3:8] = jnp.zeros((5, hidden_count), jnp.float32)
    write(factors, goals[4])
    for copy in writes:
        copy.wait()


def learn_shapes(row_count, hidden_count, width):
    return [
        jax.ShapeDtypeStruct((row_count, width), jnp.bfloat16),
        jax.ShapeDtypeStruct((width, row_count), jnp.bfloat16),
        jax.ShapeDtypeStruct((2, row_count, hidden_count), jnp.bfloat16),
        jax.ShapeDtypeStruct((hidden_count, row_count), jnp.bfloat16),
        jax.ShapeDtypeStruct((8, hidden_count), jnp.float32),
        jax.ShapeDtypeStruct((row_count, width), jnp.bfloat16),
    ]


def learn_call(place, pieces, tables, cots, planes, weights_dn, experts, rates):
    count = len(pieces)
    hidden_count, width = weights_dn.shape
    row_count = pieces[0].shape[0] * count
    anywhere = pl.BlockSpec(memory_space=pl.ANY)
    out_shape = learn_shapes(row_count, hidden_count, width)
    return pl.pallas_call(
        functools.partial(learn_kernel, count=count, experts=experts, rates=rates),
        in_specs=[pl.BlockSpec(memory_space=pltpu.SMEM)] + [anywhere] * (3 * count + 2),
        out_specs=[anywhere] * len(out_shape),
        scratch_shapes=[
            pltpu.VMEM((row_count, width), jnp.bfloat16),
            pltpu.VMEM((row_count, tables[0].shape[1] - width), jnp.bfloat16),
            pltpu.VMEM((row_count, width), jnp.bfloat16),
            pltpu.VMEM((width, row_count), jnp.bfloat16),
            pltpu.VMEM(planes.shape, jnp.bfloat16),
            pltpu.VMEM(weights_dn.shape, jnp.bfloat16),
            pltpu.SemaphoreType.DMA((3 * count + 2 * (width // TILE),)),
            pltpu.SemaphoreType.DMA((5 + width // TILE,)),
        ]
        + [pltpu.VMEM(one.shape, one.dtype) for one in out_shape],
        out_shape=out_shape,
        compiler_params=pltpu.CompilerParams(vmem_limit_bytes=48 << 20),
        cost_estimate=pl.CostEstimate(
            flops=12 * row_count * hidden_count * width,
            bytes_accessed=6 * hidden_count * width,
            transcendentals=row_count * hidden_count,
        ),
        name="learn",
    )(place, *pieces, *tables, *cots, planes, weights_dn)


def unset(like):
    return pl.pallas_call(
        lambda out_ref: None,
        out_shape=jax.ShapeDtypeStruct(like.shape, like.dtype),
        out_specs=pl.BlockSpec(memory_space=pl.ANY),
        name="unset",
    )()


def ffn_plain(place, pieces, tables, planes, weights_dn, experts):
    width = weights_dn.shape[1]
    rows = pieces[0][:, :width]
    gates = pick_gates(tables[0][:, width:], place[0], experts)
    active = nn(rows, planes[0])
    upward = nn(rows, planes[1])
    hidden = (active * jax.nn.sigmoid(active) * upward).astype(jnp.bfloat16)
    return [(gates * nn(hidden, weights_dn)).astype(jnp.bfloat16)]


def learn_plain(place, pieces, tables, cots, planes, weights_dn, experts, rates):
    width = weights_dn.shape[1]
    rows = pieces[0][:, :width]
    gates = pick_gates(tables[0][:, width:], place[0], experts)
    pulls = (gates * cots.astype(jnp.float32)).astype(jnp.bfloat16)
    active = nn(rows, planes[0])
    upward = nn(rows, planes[1])
    back = nt(pulls, weights_dn)
    sigma = jax.nn.sigmoid(active)
    swish = active * sigma
    hidden = (swish * upward).astype(jnp.bfloat16)
    d_active = (back * upward * sigma * (1.0 + active * (1.0 - sigma))).astype(jnp.bfloat16)
    d_upward = (back * swish).astype(jnp.bfloat16)
    dx_part = (nt(d_active, planes[0]) + nt(d_upward, planes[1])).astype(jnp.bfloat16)
    new_planes = jnp.stack(
        [
            renew(planes[0], wide(rows, d_active, ((0,), (0,))), 0, rates[0]),
            renew(planes[1], wide(rows, d_upward, ((0,), (0,))), 0, rates[0]),
        ],
        axis=0,
    )
    new_dn = renew(weights_dn, wide(hidden, pulls, ((0,), (0,))), 1, rates[1])
    return [dx_part, new_planes, new_dn]


def per_device(
    rows_in,
    cotangent,
    lengths,
    train_experts,
    train_gates,
    decode_experts,
    decode_gates,
    gate_up,
    down,
):
    ep_count = lax.axis_size("ep")
    dp_count = lax.axis_size("dp")
    device_count = ep_count * dp_count
    row_count, model_width = cotangent.shape
    role = lax.axis_index("grp").astype(jnp.int32)
    is_learner = role == 0
    mine = lax.axis_index("ep").astype(jnp.int32)
    own_dn = down[0, 0]
    planes = jnp.transpose(gate_up[0, 0], (1, 0, 2))
    total_rows = row_count * device_count
    longest = 2 * total_rows // lengths.shape[0]
    rates = (0.5 / model_width**0.5, 0.5 / (own_dn.shape[0] * dp_count) ** 0.5)
    small = device_count == 16 and dp_count == 1
    first_place = mine.reshape(1)
    fresh_place = first_place + 2 * ep_count

    where = jnp.stack([mine * dp_count + lax.axis_index("dp").astype(jnp.int32), role])
    block, base = prep_call(
        where, lengths, rows_in[0], cotangent, train_experts, train_gates, decode_experts,
        decode_gates, ep_count, longest,
    )
    if small:
        near, away = send_z(block, (0, 1))
        near, planes = tied(near, planes)
        cot_near, cot_away = send_z(tied(cotangent, near)[0], (0,))
        near, away = send_y(near, away, (0, 1))
        near, away, cot_near, cot_away = tied(near, away, cot_near, cot_away)
        every = send_core(near, away, (0, 1))
        cots = send_core(*send_y(cot_near, cot_away, (0,)), (0,))
        hidden_count = own_dn.shape[0]
        part_shape = jax.ShapeDtypeStruct(cots[0].shape, jnp.bfloat16)

        def learn(every, cots, planes, own_dn):
            out = learn_call(first_place, every, every, cots, planes, own_dn, ep_count, rates)
            return ([unset(part_shape) for _ in range(4)], list(out))

        def decode(every, cots, planes, own_dn):
            out = ffn_call(first_place, every, every, planes, own_dn, ep_count)
            shapes = learn_shapes(total_rows, hidden_count, model_width)
            return (list(out), [unset(one) for one in shapes])

        part, learned = lax.cond(is_learner, learn, decode, every, cots, planes, own_dn)
        dx_part = across(learned[0], 0, 1)
        near, away = sum_y(*sum_core(part, (1,)), (1,))
        current = (base + sum_z(near, away, (1,))).astype(jnp.bfloat16)
        hopped = across(current, 1, 0)
        near, away = send_y(*send_z(hopped, (0,)), (0,))
        arrived = send_core(near, away, (0,))
        fresh_part = lax.cond(
            is_learner,
            lambda r, t, g, d, *c: list(ffn_call(fresh_place, r, t, g, d, ep_count, c)),
            lambda r, t, g, d, *c: [unset(one) for one in r],
            arrived,
            every,
            planes,
            own_dn,
            *learned[1:],
        )
        fresh_part[3], dx_part = tied(fresh_part[3], dx_part)
        dx_sum = scatter_sum(dx_part, 16, (1,)).astype(jnp.bfloat16)
        dx_sum = across(dx_sum, 1, 0).astype(jnp.float32)
        near, away = sum_y(*sum_core(fresh_part, (0,)), (0,))
        moved = across(sum_z(near, away, (0,)).astype(jnp.bfloat16), 0, 1).astype(jnp.float32)
    else:
        every = [gather(block, device_count, (0, 1))]
        cots = gather(cotangent, device_count, (0,))

        def learn(every, cots, planes, own_dn):
            out = list(learn_plain(first_place, every, every, cots, planes, own_dn, ep_count, rates))
            return ([unset(out[0])], out[0], out[1], out[2])

        def decode(every, cots, planes, own_dn):
            out = list(ffn_plain(first_place, every, every, planes, own_dn, ep_count))
            return (out, unset(cots), unset(planes), unset(own_dn))

        part, dx_part, new_planes, new_dn = lax.cond(
            is_learner, learn, decode, every, cots, planes, own_dn
        )
        stale_sum = scatter_sum(part[0], device_count, (1,))
        current = (base + stale_sum).astype(jnp.bfloat16)
        dx_sum = scatter_sum(dx_part, device_count, (0,))
        arrived = [gather(across(current, 1, 0), device_count, (0,))]
        fresh_part = lax.cond(
            is_learner,
            lambda r, e, g, d: list(ffn_plain(fresh_place, r, e, g, d, ep_count)),
            lambda r, e, g, d: [unset(o) for o in r],
            arrived,
            every,
            new_planes,
            new_dn,
        )
        fresh_sum = scatter_sum(fresh_part[0], device_count, (0,))
        moved = across(fresh_sum.astype(jnp.bfloat16), 0, 1).astype(jnp.float32)
    final_rows = jnp.where(is_learner, base + dx_sum, current.astype(jnp.float32) + moved)
    return final_rows.astype(jnp.bfloat16)[None]


def solution(mesh):
    placed = (
        P("grp", ("ep", "dp"), None),
        P(("ep", "dp"), None),
        P(),
        P(("ep", "dp"), None),
        P(("ep", "dp"), None),
        P(None, ("ep", "dp"), None),
        P(None, ("ep", "dp"), None),
        P("grp", "ep", None, None, "dp"),
        P("grp", "ep", "dp", None),
    )
    return jax.shard_map(
        per_device,
        mesh=mesh,
        in_specs=placed,
        out_specs=P("grp", ("ep", "dp"), None),
        check_vma=False,
    )
```

```python
import functools

import jax
import jax.numpy as jnp
from jax import lax
from jax.experimental import pallas as pl
from jax.experimental.pallas import tpu as pltpu
from jax.sharding import PartitionSpec as P

EPSILON = 1e-06
AXES = ("ep", "dp")


def across(block, source, target):
    return lax.ppermute(block, "grp", [(source, target)])


def stages(device_count):
    sizes = []
    rest = device_count
    while rest > 1:
        size = 2 if len(sizes) < 2 or rest % 4 else 4
        sizes.append(size)
        rest //= size
    strides = []
    stride = device_count
    for size in sizes[::-1]:
        stride //= size
        strides.append((stride, size))
    return strides


def swap(block, device_count, flip, role, onward=0):
    pairs = [
        (part * device_count + i, (part + onward) * device_count + (i ^ flip))
        for part in role
        for i in range(device_count)
    ]
    return lax.ppermute(block, ("grp",) + AXES, pairs)


def tied(*values):
    return lax.optimization_barrier(values)


def gather(block, device_count, role):
    for stride, size in stages(device_count):
        got = [swap(block, device_count, turn * stride, role) for turn in range(1, size)]
        block = jnp.concatenate([block] + got, axis=0)
    return block


def send_z(block, role):
    far = [swap(block, 16, flip, role) for flip in (4, 8, 12)]
    return jnp.concatenate([block, far[0]], axis=0), jnp.concatenate(far[1:], axis=0)


def send_y(near, away, role):
    return [jnp.concatenate([part, swap(part, 16, 2, role)], axis=0) for part in (near, away)]


def send_core(near, away, role):
    return [near, swap(near, 16, 1, role), away, swap(away, 16, 1, role)]


def plus(kept, *sent):
    total = kept.astype(jnp.float32)
    for one in sent:
        total = total + one.astype(jnp.float32)
    return total


def halves(array):
    return jnp.split(array, 2, axis=0)


def scatter_sum(part, device_count, role):
    for stride, size in stages(device_count)[::-1]:
        cuts = jnp.split(part, size, axis=0)
        got = [swap(cuts[turn], device_count, turn * stride, role) for turn in range(1, size)]
        total = plus(cuts[0], *got)
        part = total.astype(jnp.bfloat16)
    return total


def sum_core(pieces, role):
    away = plus(pieces[2], swap(pieces[3], 16, 1, role)).astype(jnp.bfloat16)
    near = plus(pieces[0], swap(pieces[1], 16, 1, role)).astype(jnp.bfloat16)
    return near, away


def sum_y(near, away, role):
    kept, sent = halves(away)
    away = plus(kept, swap(sent, 16, 2, role)).astype(jnp.bfloat16)
    kept, sent = halves(near)
    near = plus(kept, swap(sent, 16, 2, role)).astype(jnp.bfloat16)
    return near, away


def sum_z(near, away, role):
    second, third = [swap(h, 16, f, role) for h, f in zip(halves(away), (8, 12))]
    kept, sent = halves(near)
    return plus(kept, swap(sent, 16, 4, role), second, third)


def renew(weights, grads, axis_number, rate):
    scale = jnp.sqrt(jnp.mean(grads * grads, axis=axis_number, keepdims=True) + EPSILON)
    return (weights.astype(jnp.float32) - rate * grads / scale).astype(jnp.bfloat16)


def wide(a, b, contract):
    return lax.dot_general(a, b, (contract, ((), ())), preferred_element_type=jnp.float32)


def nn(a, b):
    return wide(a, b, ((1,), (0,)))


def nt(a, b):
    return wide(a, b, ((1,), (1,)))


def prep_kernel(
    place, lengths, rows_ref, cot_ref, ids_ref, gates_ref, dec_ids_ref, dec_gates_ref,
    out_ref, base_ref, *, experts, longest,
):
    width = rows_ref.shape[1]
    row_count = rows_ref.shape[0]
    learner = place[1] == 0
    places = place[0] * row_count + lax.broadcasted_iota(jnp.int32, (1, row_count), 1)
    start = jnp.int32(0)
    seq_len = jnp.zeros((1, row_count), jnp.int32)
    for i in range(lengths.shape[0]):
        end = start + lengths[i]
        seq_len = jnp.where((places >= start) & (places < end), lengths[i], seq_len)
        start = end
    weight = 2.0 * longest / (seq_len.astype(jnp.float32) + longest)
    names = lax.broadcasted_iota(jnp.int32, (experts, row_count), 0)

    def table(ids, gates):
        total = jnp.zeros((experts, row_count), jnp.float32)
        for k in range(ids.shape[0]):
            total = total + jnp.where(names == ids[k : k + 1], gates[k : k + 1], 0.0)
        return total

    train = table(ids_ref[...], gates_ref[...]) * weight
    stale = table(dec_ids_ref[0], dec_gates_ref[0])
    first = jnp.where(learner, train, stale)
    fresh = table(dec_ids_ref[1], dec_gates_ref[1])
    parts = []
    for one in (first, fresh):
        upper = one.astype(jnp.bfloat16).astype(jnp.float32)
        parts += [upper, one - upper]
    spare = out_ref.shape[1] - width
    if spare > 4 * experts:
        parts.append(jnp.zeros((spare - 4 * experts, row_count), jnp.float32))
    stacked = jnp.concatenate(parts, axis=0)
    weights = jnp.broadcast_to(weight, (128, row_count))
    square = jnp.concatenate([stacked, weights], axis=0)
    square = jnp.concatenate(
        [square, jnp.zeros((square.shape[0], 128 - row_count), jnp.float32)], axis=1
    )
    for i in range(spare // 128):
        turned = square[128 * i : 128 * (i + 1)].T
        out_ref[:, width + 128 * i : width + 128 * (i + 1)] = turned[:row_count].astype(
            jnp.bfloat16
        )
    column = square[spare:].T[:row_count, 0:1]
    out_ref[:, :width] = rows_ref[...]
    base_ref[...] = jnp.where(
        learner, column * cot_ref[...].astype(jnp.float32), rows_ref[...].astype(jnp.float32)
    )


def prep_call(place, lengths, rows, cot, ids, gates, dec_ids, dec_gates, experts, longest):
    row_count, width = rows.shape
    spare = -(-4 * experts // 128) * 128
    scalars = pl.BlockSpec(memory_space=pltpu.SMEM)
    whole = pl.BlockSpec(memory_space=pltpu.VMEM)
    return pl.pallas_call(
        functools.partial(prep_kernel, experts=experts, longest=longest),
        in_specs=[scalars, scalars] + [whole] * 6,
        out_specs=[whole, whole],
        out_shape=[
            jax.ShapeDtypeStruct((row_count, width + spare), jnp.bfloat16),
            jax.ShapeDtypeStruct((row_count, width), jnp.float32),
        ],
        name="prep",
    )(place, lengths, rows, cot, ids.T, gates.T, jnp.swapaxes(dec_ids, 1, 2), jnp.swapaxes(dec_gates, 1, 2))


def pick_gates(table, column, step):
    places = lax.broadcasted_iota(jnp.int32, table.shape, 1)
    taken = (places == column) | (places == column + step)
    return jnp.sum(jnp.where(taken, table.astype(jnp.float32), 0.0), axis=1, keepdims=True)


def parts_of(array, count):
    parts = []
    for _ in range(count):
        parts.append(array.astype(jnp.bfloat16))
        array = array - parts[-1].astype(jnp.float32)
    return parts


def fine(array, other, count):
    total = None
    for part in parts_of(array, count):
        product = nn(part, other)
        total = product if total is None else total + product
    return total


TILE = 1024


def tiles_of(width):
    return [slice(lower, lower + TILE) for lower in range(0, width, TILE)]


def reads(pairs, sems):
    return [pltpu.make_async_copy(src, dst, sems.at[i]) for i, (src, dst) in enumerate(pairs)]


def row_reads(refs, count, width, rows, table):
    part = rows.shape[0] // count
    spare = table.shape[1]
    here = [pl.ds(part * i, part) for i in range(count)]
    wide_pairs = [(refs[i].at[:, pl.ds(0, width)], rows.at[here[i]]) for i in range(count)]
    thin_pairs = [
        (refs[count + i].at[:, pl.ds(width, spare)], table.at[here[i]]) for i in range(count)
    ]
    return wide_pairs + thin_pairs


def weight_reads(gu_ref, dn_ref, gu, dn):
    cuts = [pl.ds(lower, TILE) for lower in range(0, dn.shape[1], TILE)]
    return [(gu_ref.at[:, cut], gu.at[:, cut]) for cut in cuts], [
        (dn_ref.at[:, cut], dn.at[:, cut]) for cut in cuts
    ]


def added(total, product):
    return product if total is None else total + product


def ffn_kernel(place, *refs, count, experts, changed):
    gu_ref, dn_ref = refs[2 * count : 2 * count + 2]
    extra = 5 if changed else 0
    extra_refs = refs[2 * count + 2 : 2 * count + 2 + extra]
    refs_left = refs[2 * count + 2 + extra :]
    out_refs = refs_left[:count]
    rows, table, gu, dn = refs_left[count : count + 4]
    extras = refs_left[count + 4 : count + 4 + extra]
    sems = refs_left[count + 4 + extra]
    width = dn.shape[1]
    cuts = tiles_of(width)
    first = row_reads(refs, count, width, rows, table)
    gu_pairs, dn_pairs = weight_reads(gu_ref, dn_ref, gu, dn)
    more = list(zip(extra_refs, extras))
    copies = reads(first + more[:1] + gu_pairs + more[1:] + dn_pairs, sems)
    for copy in copies:
        copy.start()
    done = len(first) + len(more[:1])
    for copy in copies[:done]:
        copy.wait()
    active = upward = alike = None
    for cut in cuts:
        copies[done].wait()
        done += 1
        active = added(active, nn(rows[:, cut], gu[0, cut]))
        upward = added(upward, nn(rows[:, cut], gu[1, cut]))
        if changed:
            alike = added(alike, nn(rows[:, cut], extras[0][cut]))
    for copy in copies[done : done + len(more[1:])]:
        copy.wait()
    done += len(more[1:])
    if changed:
        turned, sent, hidden_turned, rates, pulls = extras
        active = active - fine(alike, sent[0], 2) * rates[0:1]
        upward = upward - fine(alike, sent[1], 2) * rates[1:2]
    hidden = (active * jax.nn.sigmoid(active) * upward).astype(jnp.bfloat16)
    if changed:
        scaled = hidden.astype(jnp.float32) * rates[2:3]
        mixed = parts_of(fine(scaled, hidden_turned[...], 2), 2)
    gates = pick_gates(table[...], place[0], experts)
    part = rows.shape[0] // count
    for cut in cuts:
        copies[done].wait()
        done += 1
        out = nn(hidden, dn[:, cut])
        if changed:
            for one in mixed:
                out = out - nn(one, pulls[:, cut])
        out = (gates * out).astype(jnp.bfloat16)
        for i in range(count):
            out_refs[i][:, cut] = out[part * i : part * (i + 1)]


def ffn_call(place, pieces, tables, planes, weights_dn, experts, change=()):
    count = len(pieces)
    part = pieces[0].shape[0]
    hidden_count, width = weights_dn.shape
    row_count = part * count
    anywhere = pl.BlockSpec(memory_space=pl.ANY)
    whole = pl.BlockSpec(memory_space=pltpu.VMEM)
    return pl.pallas_call(
        functools.partial(ffn_kernel, count=count, experts=experts, changed=bool(change)),
        in_specs=[pl.BlockSpec(memory_space=pltpu.SMEM)]
        + [anywhere] * (2 * count + 2 + len(change)),
        out_specs=[whole] * count,
        scratch_shapes=[
            pltpu.VMEM((row_count, width), jnp.bfloat16),
            pltpu.VMEM((row_count, tables[0].shape[1] - width), jnp.bfloat16),
            pltpu.VMEM(planes.shape, jnp.bfloat16),
            pltpu.VMEM(weights_dn.shape, jnp.bfloat16),
        ]
        + [pltpu.VMEM(one.shape, one.dtype) for one in change]
        + [pltpu.SemaphoreType.DMA((2 * count + len(change) + 2 * (width // TILE),))],
        out_shape=[jax.ShapeDtypeStruct((part, width), jnp.bfloat16)] * count,
        compiler_params=pltpu.CompilerParams(vmem_limit_bytes=44 << 20),
        cost_estimate=pl.CostEstimate(
            flops=6 * row_count * hidden_count * width,
            bytes_accessed=6 * hidden_count * width,
            transcendentals=row_count * hidden_count,
        ),
        name="ffn_changed" if change else "ffn",
    )(place, *pieces, *tables, planes, weights_dn, *change)


def learn_kernel(place, *refs, count, experts, rates):
    cot_refs = refs[2 * count : 3 * count]
    gu_ref, dn_ref = refs[3 * count : 3 * count + 2]
    goals = refs[3 * count + 2 : 3 * count + 8]
    rows, table, cots, pulls_turned, gu, dn, sems, out_sems = refs[3 * count + 8 : 3 * count + 16]
    held = refs[3 * count + 16 :]
    dx, turned, sent, hidden_turned, factors, pulls = held
    hidden_count, width = dn.shape
    part = rows.shape[0] // count
    cuts = tiles_of(width)
    first = row_reads(refs, count, width, rows, table)
    first += [(cot_refs[i], cots.at[pl.ds(part * i, part)]) for i in range(count)]
    gu_pairs, dn_pairs = weight_reads(gu_ref, dn_ref, gu, dn)
    both = [pair for pairs in zip(gu_pairs, dn_pairs) for pair in pairs]
    copies = reads(first + both, sems)
    for copy in copies:
        copy.start()
    done = len(first)
    for copy in copies[:done]:
        copy.wait()
    gates = pick_gates(table[...], place[0], experts)
    for cut in cuts:
        pulls[:, cut] = (gates * cots[:, cut].astype(jnp.float32)).astype(jnp.bfloat16)
        turned[cut, :] = rows[:, cut].T
        pulls_turned[cut, :] = pulls[:, cut].T
    writes = []

    def write(source, goal):
        copy = pltpu.make_async_copy(source, goal, out_sems.at[len(writes)])
        copy.start()
        writes.append(copy)

    write(turned, goals[1])
    write(pulls, goals[5])
    alike_rows = nn(rows[...], turned[...])
    alike_pulls = nn(pulls[...], pulls_turned[...])
    active = upward = back = None
    for cut in cuts:
        copies[done].wait()
        copies[done + 1].wait()
        done += 2
        active = added(active, nn(rows[:, cut], gu[0, cut]))
        upward = added(upward, nn(rows[:, cut], gu[1, cut]))
        back = added(back, nn(dn[:, cut], pulls_turned[cut]))
    back = back.T
    sigma = jax.nn.sigmoid(active)
    swish = active * sigma
    hidden = (swish * upward).astype(jnp.bfloat16)
    d_active = (back * upward * sigma * (1.0 + active * (1.0 - sigma))).astype(jnp.bfloat16)
    d_upward = (back * swish).astype(jnp.bfloat16)
    sent[0] = d_active
    sent[1] = d_upward
    hidden_turned[...] = hidden.T
    write(sent, goals[2])
    write(hidden_turned, goals[3])
    d_active_turned = d_active.T
    d_upward_turned = d_upward.T

    for cut in cuts:
        out = nn(gu[0, cut], d_active_turned) + nn(gu[1, cut], d_upward_turned)
        out = out.T.astype(jnp.bfloat16)
        slab = part // 2
        for i in range(count):
            for half in range(2):
                lower = ((i % 2) * 2 + half) * part + (i // 2) * slab
                here = part * i + slab * half
                dx[lower : lower + slab, cut] = out[here : here + slab]
        columns = pl.ds(cut.start, TILE)
        write(dx.at[:, columns], goals[0].at[:, columns])

    def mean_square(alike, factor):
        wide_factor = factor.astype(jnp.float32)
        squares = jnp.sum(wide_factor * fine(alike, factor, 3), axis=0, keepdims=True)
        return jnp.maximum(squares, 0.0) / width

    factors[0:1] = rates[0] / jnp.sqrt(mean_square(alike_rows, d_active) + EPSILON)
    factors[1:2] = rates[0] / jnp.sqrt(mean_square(alike_rows, d_upward) + EPSILON)
    factors[2:3] = rates[1] / jnp.sqrt(mean_square(alike_pulls, hidden) + EPSILON)
    factors[3:8] = jnp.zeros((5, hidden_count), jnp.float32)
    write(factors, goals[4])
    for copy in writes:
        copy.wait()


def learn_shapes(row_count, hidden_count, width):
    return [
        jax.ShapeDtypeStruct((row_count, width), jnp.bfloat16),
        jax.ShapeDtypeStruct((width, row_count), jnp.bfloat16),
        jax.ShapeDtypeStruct((2, row_count, hidden_count), jnp.bfloat16),
        jax.ShapeDtypeStruct((hidden_count, row_count), jnp.bfloat16),
        jax.ShapeDtypeStruct((8, hidden_count), jnp.float32),
        jax.ShapeDtypeStruct((row_count, width), jnp.bfloat16),
    ]


def learn_call(place, pieces, tables, cots, planes, weights_dn, experts, rates):
    count = len(pieces)
    hidden_count, width = weights_dn.shape
    row_count = pieces[0].shape[0] * count
    anywhere = pl.BlockSpec(memory_space=pl.ANY)
    out_shape = learn_shapes(row_count, hidden_count, width)
    return pl.pallas_call(
        functools.partial(learn_kernel, count=count, experts=experts, rates=rates),
        in_specs=[pl.BlockSpec(memory_space=pltpu.SMEM)] + [anywhere] * (3 * count + 2),
        out_specs=[anywhere] * len(out_shape),
        scratch_shapes=[
            pltpu.VMEM((row_count, width), jnp.bfloat16),
            pltpu.VMEM((row_count, tables[0].shape[1] - width), jnp.bfloat16),
            pltpu.VMEM((row_count, width), jnp.bfloat16),
            pltpu.VMEM((width, row_count), jnp.bfloat16),
            pltpu.VMEM(planes.shape, jnp.bfloat16),
            pltpu.VMEM(weights_dn.shape, jnp.bfloat16),
            pltpu.SemaphoreType.DMA((3 * count + 2 * (width // TILE),)),
            pltpu.SemaphoreType.DMA((5 + width // TILE,)),
        ]
        + [pltpu.VMEM(one.shape, one.dtype) for one in out_shape],
        out_shape=out_shape,
        compiler_params=pltpu.CompilerParams(vmem_limit_bytes=48 << 20),
        cost_estimate=pl.CostEstimate(
            flops=12 * row_count * hidden_count * width,
            bytes_accessed=6 * hidden_count * width,
            transcendentals=row_count * hidden_count,
        ),
        name="learn",
    )(place, *pieces, *tables, *cots, planes, weights_dn)


def unset(like):
    return pl.pallas_call(
        lambda out_ref: None,
        out_shape=jax.ShapeDtypeStruct(like.shape, like.dtype),
        out_specs=pl.BlockSpec(memory_space=pl.ANY),
        name="unset",
    )()


def ffn_plain(place, pieces, tables, planes, weights_dn, experts):
    width = weights_dn.shape[1]
    rows = pieces[0][:, :width]
    gates = pick_gates(tables[0][:, width:], place[0], experts)
    active = nn(rows, planes[0])
    upward = nn(rows, planes[1])
    hidden = (active * jax.nn.sigmoid(active) * upward).astype(jnp.bfloat16)
    return [(gates * nn(hidden, weights_dn)).astype(jnp.bfloat16)]


def learn_plain(place, pieces, tables, cots, planes, weights_dn, experts, rates):
    width = weights_dn.shape[1]
    rows = pieces[0][:, :width]
    gates = pick_gates(tables[0][:, width:], place[0], experts)
    pulls = (gates * cots.astype(jnp.float32)).astype(jnp.bfloat16)
    active = nn(rows, planes[0])
    upward = nn(rows, planes[1])
    back = nt(pulls, weights_dn)
    sigma = jax.nn.sigmoid(active)
    swish = active * sigma
    hidden = (swish * upward).astype(jnp.bfloat16)
    d_active = (back * upward * sigma * (1.0 + active * (1.0 - sigma))).astype(jnp.bfloat16)
    d_upward = (back * swish).astype(jnp.bfloat16)
    dx_part = (nt(d_active, planes[0]) + nt(d_upward, planes[1])).astype(jnp.bfloat16)
    new_planes = jnp.stack(
        [
            renew(planes[0], wide(rows, d_active, ((0,), (0,))), 0, rates[0]),
            renew(planes[1], wide(rows, d_upward, ((0,), (0,))), 0, rates[0]),
        ],
        axis=0,
    )
    new_dn = renew(weights_dn, wide(hidden, pulls, ((0,), (0,))), 1, rates[1])
    return [dx_part, new_planes, new_dn]


def per_device(
    rows_in,
    cotangent,
    lengths,
    train_experts,
    train_gates,
    decode_experts,
    decode_gates,
    gate_up,
    down,
):
    ep_count = lax.axis_size("ep")
    dp_count = lax.axis_size("dp")
    device_count = ep_count * dp_count
    row_count, model_width = cotangent.shape
    role = lax.axis_index("grp").astype(jnp.int32)
    is_learner = role == 0
    mine = lax.axis_index("ep").astype(jnp.int32)
    own_dn = down[0, 0]
    planes = jnp.transpose(gate_up[0, 0], (1, 0, 2))
    total_rows = row_count * device_count
    longest = 2 * total_rows // lengths.shape[0]
    rates = (0.5 / model_width**0.5, 0.5 / (own_dn.shape[0] * dp_count) ** 0.5)
    small = device_count == 16 and dp_count == 1
    first_place = mine.reshape(1)
    fresh_place = first_place + 2 * ep_count

    where = jnp.stack([mine * dp_count + lax.axis_index("dp").astype(jnp.int32), role])
    block, base = prep_call(
        where, lengths, rows_in[0], cotangent, train_experts, train_gates, decode_experts,
        decode_gates, ep_count, longest,
    )
    if small:
        near, away = send_z(block, (0, 1))
        near, planes = tied(near, planes)
        cot_near, cot_away = send_z(tied(cotangent, near)[0], (0,))
        near, away = send_y(near, away, (0, 1))
        near, away, cot_near, cot_away = tied(near, away, cot_near, cot_away)
        every = send_core(near, away, (0, 1))
        cots = send_core(*send_y(cot_near, cot_away, (0,)), (0,))
        hidden_count = own_dn.shape[0]
        part_shape = jax.ShapeDtypeStruct(cots[0].shape, jnp.bfloat16)

        part = lax.cond(
            is_learner,
            lambda r, g, d: [unset(part_shape) for _ in r],
            lambda r, g, d: list(ffn_call(first_place, r, r, g, d, ep_count)),
            every,
            planes,
            own_dn,
        )
        near, away = sum_y(*sum_core(part, (1,)), (1,))
        current = (base + sum_z(near, away, (1,))).astype(jnp.bfloat16)
        current, cots[3] = tied(current, cots[3])
        learned = lax.cond(
            is_learner,
            lambda r, c, g, d: list(learn_call(first_place, r, r, c, g, d, ep_count, rates)),
            lambda r, c, g, d: [unset(one) for one in learn_shapes(total_rows, hidden_count, model_width)],
            every,
            cots,
            planes,
            own_dn,
        )
        dx_part = across(learned[0], 0, 1)
        hopped = across(current, 1, 0)
        near, away = send_y(*send_z(hopped, (0,)), (0,))
        arrived = send_core(near, away, (0,))
        fresh_part = lax.cond(
            is_learner,
            lambda r, t, g, d, *c: list(ffn_call(fresh_place, r, t, g, d, ep_count, c)),
            lambda r, t, g, d, *c: [unset(one) for one in r],
            arrived,
            every,
            planes,
            own_dn,
            *learned[1:],
        )
        fresh_part[3], dx_part = tied(fresh_part[3], dx_part)
        dx_sum = scatter_sum(dx_part, 16, (1,)).astype(jnp.bfloat16)
        dx_sum = across(dx_sum, 1, 0).astype(jnp.float32)
        near, away = sum_y(*sum_core(fresh_part, (0,)), (0,))
        moved = across(sum_z(near, away, (0,)).astype(jnp.bfloat16), 0, 1).astype(jnp.float32)
    else:
        every = [gather(block, device_count, (0, 1))]
        cots = gather(cotangent, device_count, (0,))

        def learn(every, cots, planes, own_dn):
            out = list(learn_plain(first_place, every, every, cots, planes, own_dn, ep_count, rates))
            return ([unset(out[0])], out[0], out[1], out[2])

        def decode(every, cots, planes, own_dn):
            out = list(ffn_plain(first_place, every, every, planes, own_dn, ep_count))
            return (out, unset(cots), unset(planes), unset(own_dn))

        part, dx_part, new_planes, new_dn = lax.cond(
            is_learner, learn, decode, every, cots, planes, own_dn
        )
        stale_sum = scatter_sum(part[0], device_count, (1,))
        current = (base + stale_sum).astype(jnp.bfloat16)
        dx_sum = scatter_sum(dx_part, device_count, (0,))
        arrived = [gather(across(current, 1, 0), device_count, (0,))]
        fresh_part = lax.cond(
            is_learner,
            lambda r, e, g, d: list(ffn_plain(fresh_place, r, e, g, d, ep_count)),
            lambda r, e, g, d: [unset(o) for o in r],
            arrived,
            every,
            new_planes,
            new_dn,
        )
        fresh_sum = scatter_sum(fresh_part[0], device_count, (0,))
        moved = across(fresh_sum.astype(jnp.bfloat16), 0, 1).astype(jnp.float32)
    final_rows = jnp.where(is_learner, base + dx_sum, current.astype(jnp.float32) + moved)
    return final_rows.astype(jnp.bfloat16)[None]


def solution(mesh):
    placed = (
        P("grp", ("ep", "dp"), None),
        P(("ep", "dp"), None),
        P(),
        P(("ep", "dp"), None),
        P(("ep", "dp"), None),
        P(None, ("ep", "dp"), None),
        P(None, ("ep", "dp"), None),
        P("grp", "ep", None, None, "dp"),
        P("grp", "ep", "dp", None),
    )
    return jax.shard_map(
        per_device,
        mesh=mesh,
        in_specs=placed,
        out_specs=P("grp", ("ep", "dp"), None),
        check_vma=False,
    )
```
